32 devices in a mesh: dp: 4 (over y, x), expert: 8 (over z, core).
Axes of the slice: x: 2, y: 2, z: 4, core: 2. Of those that a mesh axis runs over, the one named last changes fastest.
Arguments:
- hidden_in: bfloat16 [8192, 2048], P(('dp', 'expert')), may hold values from -6 to 6
- cotangent: bfloat16 [8192, 2048], P(('dp', 'expert')), may hold values from -6 to 6
- attention_gain: bfloat16 [2048], P(('dp', 'expert')), may hold values from 0.25 to 1.75
- query_gain: bfloat16 [2048], P(('dp', 'expert')), may hold values from 0.25 to 1.75
- key_gain: bfloat16 [2048], P(('dp', 'expert')), may hold values from 0.25 to 1.75
- mixture_gain: bfloat16 [2048], P(('dp', 'expert')), may hold values from 0.25 to 1.75
- query_weight: bfloat16 [2048, 2048], P(('dp', 'expert')), may hold values from -0.125 to 0.125
- key_weight: bfloat16 [2048, 2048], P(('dp', 'expert')), may hold values from -0.125 to 0.125
- value_weight: bfloat16 [2048, 2048], P(('dp', 'expert')), may hold values from -0.125 to 0.125
- output_weight: bfloat16 [2048, 2048], P(('dp', 'expert')), may hold values from -0.375 to 0.375
- router_weight: bfloat16 [2048, 16], P(('dp', 'expert')), may hold values from -0.0625 to 0.0625
- gate_weight: bfloat16 [16, 2048, 1024], P('expert', None, 'dp'), may hold values from -0.125 to 0.125
- up_weight: bfloat16 [16, 2048, 1024], P('expert', None, 'dp'), may hold values from -0.125 to 0.125
- down_weight: bfloat16 [16, 1024, 2048], P('expert', 'dp'), may hold values from -4 to 4
- routes: int32 [8192, 8], P(('dp', 'expert')), may hold values from 0 to 15, all different within a row; in each aligned block of 256 rows (0 to 255, 256 to 511, ...) at most 160 rows name the same one
- segments: int32 [32, 256], P(('dp', 'expert')), may hold values from 0 to 3, never falling along the last dimension, each value on 1 to 128 neighbouring positions
Outputs:
- layer_out: bfloat16 [8192, 2048], P(('dp', 'expert'))
- hidden_grad: float32 [8192, 2048], P(('dp', 'expert'))
- attention_gain_grad: float32 [2048], P(('dp', 'expert'))
- query_gain_grad: float32 [2048], P(('dp', 'expert'))
- key_gain_grad: float32 [2048], P(('dp', 'expert'))
- mixture_gain_grad: float32 [2048], P(('dp', 'expert'))
- query_weight_grad: float32 [2048, 2048], P(('dp', 'expert'))
- key_weight_grad: float32 [2048, 2048], P(('dp', 'expert'))
- value_weight_grad: float32 [2048, 2048], P(('dp', 'expert'))
- output_weight_grad: float32 [2048, 2048], P(('dp', 'expert'))
- router_weight_grad: float32 [2048, 16], P(('dp', 'expert'))
- gate_weight_grad: float32 [16, 2048, 1024], P('expert', None, 'dp')
- up_weight_grad: float32 [16, 2048, 1024], P('expert', None, 'dp')
- down_weight_grad: float32 [16, 1024, 2048], P('expert', 'dp')
The draws below stay inside these ranges and needn't reach their ends.
Inputs may be any that keep to these rules, and one draw needn't show every extreme that they name: `routes`: A token's 8 experts differ. Within the rows of one device no expert is named more than 160 times, and in every draw some expert is named exactly 160 times by the rows of some device. `segments`: along each sequence the segment numbers never fall.
All inputs are finite; a program needn't handle non-finite values.
Results may differ from the reference program's by a relative error of at most 0.019.
Values may be sent and summed in bfloat16 or wider, within the bound.
No kernel may reach another device: no remote copies, remote signals or barrier semaphores. Data moves between devices by JAX's collectives and lax.ppermute only.
A program may use at most 320 MiB of HBM per device.

```python
import math
import jax
import jax.numpy as jnp
import numpy as np
from jax import lax

D = 2048
H = 16
HD = 128
FF = 1024
TOP = 8
TOK_DEV = 256
SEQ = 256
EXPERTS = 16
CAP = 160
TOKENS = 8192
NSEQ = 32
N_DP = 4
N_EXPERT = 8


def block_scale(stream_key, extent, cuts, low, largest):
    factor_of = 1.0
    for dim, parts in cuts:
        draws = jax.random.uniform(jax.random.fold_in(jax.random.fold_in(stream_key, 6), dim), (parts,), jnp.float32, low / len(cuts), largest / len(cuts))
        factor_of = factor_of * jnp.repeat(jnp.exp(draws), extent[dim] // parts).reshape((-1,) + (1,) * (len(extent) - 1 - dim))
    return factor_of


def profile(number_of, total, limit, skew):
    weights = [(1 << 20) // math.isqrt(grade ** skew) + 1 for grade in range(2, number_of + 1)]
    surplus, counts = total - limit - (number_of - 1), [1] * (number_of - 1)
    while surplus > 0:
        movable = [i for i in range(number_of - 1) if counts[i] < limit]
        mass, left = sum([weights[i] for i in movable]), surplus
        for i in movable:
            more = min(limit - counts[i], max(1, left * weights[i] // mass), surplus)
            counts[i] = counts[i] + more
            surplus = surplus - more
    return np.array([limit] + counts)


def ragged_sizes(key, count, total, reach, skew):
    if count == 2:
        one = jax.random.randint(key, (), max(1, total - reach), min(reach, total - 1) + 1)
        return jnp.stack([one, total - one])
    lengths = jnp.asarray(profile(count, total, reach, skew), jnp.int32)
    twos = (count - 1) // 2
    giver, taker = lengths[1:1 + 2 * twos:2], lengths[2:2 + 2 * twos:2]
    slack = jnp.minimum(giver - 1, reach - taker)
    shifted = jax.random.randint(jax.random.fold_in(key, 1), (twos,), 0, 1 << 20) % (slack + 1)
    lengths = lengths.at[1:1 + 2 * twos:2].set(giver - shifted).at[2:2 + 2 * twos:2].set(taker + shifted)
    return lengths[jax.random.permutation(jax.random.fold_in(key, 2), count)]


def deal_out(own_key, own, number, rows, amount, top, limit, skew):
    sequence = jax.random.permutation(own_key, amount)
    crowded, common = shares(amount, rows * top, limit, skew, True), shares(amount, rows * top, limit, skew, False)
    places = jnp.arange(amount)

    def named(sizes, rotation):
        used = int((sizes > 0).sum())
        fixed = max(1, used // 4)
        shifted = fixed + (places - fixed + rotation * (used - fixed)) % max(1, amount - fixed)
        return jnp.zeros((amount,), jnp.int32).at[sequence[jnp.where(places < fixed, places, shifted)]].set(jnp.asarray(sizes, jnp.int32))

    sizes = jnp.where(number % 4 == 0, named(crowded, number // 4), named(common, number - number // 4 - 1))
    mixed = jax.random.permutation(jax.random.fold_in(own, 3), amount)
    donor, taker = mixed[0:amount // 2 * 2:2], mixed[1:amount // 2 * 2:2]
    room = jnp.minimum(sizes[donor] - 1, limit - sizes[taker]) // 2
    room = jnp.where((donor == sequence[0]) | (taker == sequence[0]) | (sizes[taker] == 0), 0, jnp.maximum(room, 0))
    shifted = jax.random.randint(jax.random.fold_in(own, 4), (amount // 2,), 0, 1 << 20) % (room + 1)
    sizes = sizes.at[donor].add(-shifted).at[taker].add(shifted)
    items = jnp.searchsorted(jnp.cumsum(sizes), jnp.arange(rows * top), side="right").astype(jnp.int32)
    listing = items.reshape(top, rows).T
    listing = listing[jax.random.permutation(jax.random.fold_in(own, 1), rows)]
    rotation = jax.random.randint(jax.random.fold_in(own, 2), (rows, 1), 0, top)
    return jnp.take_along_axis(listing, (jnp.arange(top)[None, :] + rotation) % top, axis=1)


def shares(count, total, bound, slope, full):
    portions = [(1 << 20) // math.isqrt(rank ** slope) + 1 for rank in range(1, count + 1)]
    largest = bound if full else min(bound, max(-(-total // count), total * portions[0] // sum(portions)))
    least = 1 if total - largest >= count - 1 else 0
    holding, surplus = [largest] + [least] * (count - 1), total - largest - least * (count - 1)
    while surplus > 0:
        free = [i for i in range(1, count) if holding[i] < largest] or [i for i in range(1, count) if holding[i] < bound]
        mass, remaining = sum([portions[i] for i in free]), surplus
        for i in free:
            extra = min(bound - holding[i], max(1, remaining * portions[i] // mass), surplus)
            holding[i] = holding[i] + extra
            surplus = surplus - extra
    return np.array(holding)


def gaussian(rng, shape, scale, most, cuts=(), kind=jnp.bfloat16):
    values = scale * jax.random.normal(rng, shape, jnp.float32)
    if cuts:
        values = values * block_scale(rng, shape, cuts, -0.22, 0.18)
    return jnp.clip(values, -most, most).astype(kind)


def setup_inputs(seed: int = 0) -> dict:
    key_of = jax.random.split(jax.random.key(seed), 17)
    hidden_in = gaussian(key_of[0], (TOKENS, D), 1.0, 6.0, ((0, 32),))
    cotangent = gaussian(key_of[1], (TOKENS, D), 1.0, 6.0, ((0, 32),))
    attention_gain = jnp.clip(1.0 + 0.15 * jax.random.normal(key_of[2], (D,), jnp.float32), 0.25, 1.75).astype(jnp.bfloat16)
    query_gain = jnp.clip(1.0 + 0.15 * jax.random.normal(key_of[3], (D,), jnp.float32), 0.25, 1.75).astype(jnp.bfloat16)
    key_gain = jnp.clip(1.0 + 0.15 * jax.random.normal(key_of[4], (D,), jnp.float32), 0.25, 1.75).astype(jnp.bfloat16)
    mixture_gain = jnp.clip(1.0 + 0.15 * jax.random.normal(key_of[5], (D,), jnp.float32), 0.25, 1.75).astype(jnp.bfloat16)
    query_weight = gaussian(key_of[6], (D, D), D ** -0.5, 0.125, ((0, 32),))
    key_weight = gaussian(key_of[7], (D, D), D ** -0.5, 0.125, ((0, 32),))
    value_weight = gaussian(key_of[8], (D, D), D ** -0.5, 0.125, ((0, 32),))
    output_weight = gaussian(key_of[9], (D, D), (D // 8) ** -0.5, 0.375, ((0, 32),))
    router_weight = gaussian(key_of[10], (D, EXPERTS), (4 * D) ** -0.5, 0.0625, ((0, 32),))
    gate_weight = gaussian(key_of[11], (EXPERTS, D, FF), D ** -0.5, 0.125, ((0, 8), (2, 4)))
    up_weight = gaussian(key_of[12], (EXPERTS, D, FF), D ** -0.5, 0.125, ((0, 8), (2, 4)))
    down_weight = gaussian(key_of[13], (EXPERTS, FF, D), (max(1, FF // 512)) ** -0.5, 4.0, ((0, 8), (1, 4)))
    routes_keys = jax.random.split(jax.random.fold_in(key_of[14], 1), TOKENS // TOK_DEV)
    routes_turns = jax.random.permutation(jax.random.fold_in(key_of[14], 3), TOKENS // TOK_DEV)
    routes = jax.vmap(lambda own, number: deal_out(jax.random.fold_in(key_of[14], 2), own, number, TOK_DEV, EXPERTS, TOP, CAP, 2))(routes_keys, routes_turns).reshape((TOKENS, TOP))
    segments = jax.vmap(lambda own: jnp.searchsorted(jnp.cumsum(ragged_sizes(own, max(3, SEQ // 64), SEQ, SEQ // 2, 1)), jnp.arange(SEQ), side="right"))(jax.random.split(key_of[15], NSEQ)).reshape((NSEQ, SEQ)).astype(jnp.int32)
    return dict(hidden_in=hidden_in, cotangent=cotangent, attention_gain=attention_gain, query_gain=query_gain, key_gain=key_gain, mixture_gain=mixture_gain, query_weight=query_weight, key_weight=key_weight, value_weight=value_weight, output_weight=output_weight, router_weight=router_weight, gate_weight=gate_weight, up_weight=up_weight, down_weight=down_weight, routes=routes, segments=segments)


epsilon = 1e-05
rope_base = 10000.0
masked_score = -1e+30
precise = lax.Precision.HIGHEST

@jax.custom_vjp
def low(v):
    return lax.optimization_barrier(v.astype(jnp.bfloat16)).astype(jnp.float32)

@jax.custom_vjp
def low_back(v):
    return v

def low_keep(v):
    return (low(v), None)

def low_pass(kept, grad):
    return (grad,)

def back_keep(v):
    return (v, None)

def back_low(kept, grad):
    return (low(grad),)
low.defvjp(low_keep, low_pass)
low_back.defvjp(back_keep, back_low)

def norm_scale(values):
    return lax.rsqrt(lax.optimization_barrier(jnp.mean(values * values, axis=-1, keepdims=True)) + epsilon)

def rotary_tables(segments, head_size):
    length = segments.shape[-1]
    order = jnp.arange(length, dtype=jnp.int32)
    starts = lax.optimization_barrier(jnp.sum((segments[..., None, :] < segments[..., :, None]).astype(jnp.int32), axis=-1))
    position = (order - starts).astype(jnp.float32)
    frequency = rope_base ** (-2.0 * jnp.arange(head_size // 2, dtype=jnp.float32) / head_size)
    angle = position[..., None] * frequency
    return (jnp.cos(angle), jnp.sin(angle))

def rotate(values, cosine, sine):
    half = values.shape[-1] // 2
    first = values[..., :half]
    second = values[..., half:]
    return jnp.concatenate([first * cosine - second * sine, second * cosine + first * sine], axis=-1)

def attend_group(block):
    queries, keys, values, segment_rows = block
    scores = low_back(jnp.einsum('gthd,gshd->ghts', queries, keys, precision=precise) * HD ** (-0.5))
    order = jnp.arange(SEQ, dtype=jnp.int32)
    allowed = (segment_rows[:, :, None] == segment_rows[:, None, :]) & (order[:, None] >= order[None, :])
    scores = jnp.where(allowed[:, None], scores, masked_score)
    weights = low(jax.nn.softmax(scores, axis=-1))
    return jnp.einsum('ghts,gshd->gthd', weights, values, precision=precise)

def expert_apply(block):
    rows, gate_matrix, up_matrix, down_matrix = block
    gate_pre = low_back(jnp.dot(rows, gate_matrix, precision=precise))
    up_pre = low_back(jnp.dot(rows, up_matrix, precision=precise))
    hidden = low(jax.nn.silu(gate_pre) * up_pre)
    return low(low_back(jnp.dot(hidden, down_matrix, precision=precise)))

def expert_slots(routes):
    devices = N_DP * N_EXPERT
    flat = routes.reshape(devices, TOK_DEV * TOP)
    hits = (flat[:, :, None] == jnp.arange(EXPERTS, dtype=jnp.int32)).astype(jnp.int32)
    ranks = lax.optimization_barrier(jnp.sum((jnp.cumsum(hits, axis=1) - 1) * hits, axis=-1))
    source = jnp.arange(devices, dtype=jnp.int32)[:, None]
    return ((flat * devices + source) * CAP + ranks).reshape(-1).astype(jnp.int32)

def forward(residual, attention_gain, query_gain, key_gain, mixture_gain, query_weight, key_weight, value_weight, output_weight, router_weight, gate_weight, up_weight, down_weight, routes, segments):
    unit_one = residual * norm_scale(residual)
    normed = low(unit_one * attention_gain)
    query_raw = low_back(jnp.dot(normed, query_weight, precision=precise))
    key_raw = low_back(jnp.dot(normed, key_weight, precision=precise))
    values = low(low_back(jnp.dot(normed, value_weight, precision=precise)))
    query_unit = query_raw * norm_scale(query_raw)
    key_unit = key_raw * norm_scale(key_raw)
    cosine, sine = rotary_tables(segments, HD)
    cosine = cosine[:, :, None, :]
    sine = sine[:, :, None, :]
    head_shape = (NSEQ, SEQ, H, HD)
    queries = low(rotate((query_unit * query_gain).reshape(head_shape), cosine, sine))
    keys = low(rotate((key_unit * key_gain).reshape(head_shape), cosine, sine))
    groups = NSEQ // N_EXPERT
    split = (groups, N_EXPERT, SEQ, H, HD)
    context = lax.map(jax.checkpoint(attend_group), (queries.reshape(split), keys.reshape(split), values.reshape(split), segments.reshape(groups, N_EXPERT, SEQ)))
    context = low(low_back(context.reshape(TOKENS, D)))
    middle = residual + low_back(jnp.dot(context, output_weight, precision=precise))
    unit_two = middle * norm_scale(middle)
    mixed_in = low(unit_two * mixture_gain)
    router_probs = jax.nn.softmax(low_back(jnp.dot(mixed_in, router_weight, precision=precise)), axis=-1)
    picks = (routes[:, :, None] == jnp.arange(EXPERTS, dtype=jnp.int32)).astype(jnp.float32)
    gates = lax.optimization_barrier(jnp.sum(picks * router_probs[:, None, :], axis=-1))
    dest = expert_slots(routes)
    slots = EXPERTS * N_DP * N_EXPERT * CAP
    owner = jnp.full((slots,), -1, jnp.int32).at[dest].set(jnp.arange(TOKENS * TOP, dtype=jnp.int32))
    filled = owner >= 0
    pick = jnp.where(filled, owner, 0)
    token_of = pick // TOP
    buffer = low_back(jnp.where(filled[:, None], mixed_in[token_of], 0.0))
    result = lax.map(jax.checkpoint(expert_apply), (buffer.reshape(EXPERTS, slots // EXPERTS, D), gate_weight, up_weight, down_weight))
    gate_of = jnp.where(filled, gates.reshape(-1)[pick], 0.0)
    mixture = jnp.zeros((TOKENS, D), jnp.float32).at[token_of].add(gate_of[:, None] * result.reshape(slots, D))
    return middle + mixture

def reference(hidden_in, cotangent, attention_gain, query_gain, key_gain, mixture_gain, query_weight, key_weight, value_weight, output_weight, router_weight, gate_weight, up_weight, down_weight, routes, segments):
    floats = tuple((item.astype(jnp.float32) for item in (hidden_in, attention_gain, query_gain, key_gain, mixture_gain, query_weight, key_weight, value_weight, output_weight, router_weight, gate_weight, up_weight, down_weight)))

    def closed(*params):
        return forward(*params, routes, segments)
    layer_out, pullback = jax.vjp(closed, *floats)
    grads = pullback(cotangent.astype(jnp.float32))
    return (layer_out.astype(jnp.bfloat16), grads[0], grads[1], grads[2], grads[3], grads[4], grads[5], grads[6], grads[7], grads[8], grads[9], grads[10], grads[11], grads[12])
```

```python
import functools
import math

import jax
import jax.numpy as jnp
from jax import lax
from jax.experimental import pallas as pl
from jax.experimental.pallas import tpu as pltpu
from jax.sharding import PartitionSpec as P

HD = 128


epsilon = 1e-05
rope_base = 10000.0
masked_score = -1e30


def norm_scale(values):
    return lax.rsqrt(jnp.mean(values * values, axis=-1, keepdims=True) + epsilon)


def norm_back(upstream, unit, scale):
    return scale * (upstream - unit * jnp.mean(upstream * unit, axis=-1, keepdims=True))


def rotary_tables(segments, head_size):
    length = segments.shape[-1]
    order = jnp.arange(length, dtype=jnp.int32)
    starts = jnp.sum((segments[..., None, :] < segments[..., :, None]).astype(jnp.int32), axis=-1)
    position = (order - starts).astype(jnp.float32)
    frequency = rope_base ** (-2.0 * jnp.arange(head_size // 2, dtype=jnp.float32) / head_size)
    angle = position[..., None] * frequency
    return (jnp.cos(angle), jnp.sin(angle))


def rotate(values, cosine, sine):
    half = values.shape[-1] // 2
    first = values[..., :half]
    second = values[..., half:]
    return jnp.concatenate(
        [first * cosine - second * sine, second * cosine + first * sine], axis=-1
    )


def rotate_back(upstream, cosine, sine):
    half = upstream.shape[-1] // 2
    first = upstream[..., :half]
    second = upstream[..., half:]
    return jnp.concatenate(
        [first * cosine + second * sine, second * cosine - first * sine], axis=-1
    )


VMEM_BYTES = 60 * 1024 * 1024


def dot_nt(a, b):
    return lax.dot_general(a, b, (((1,), (1,)), ((), ())), preferred_element_type=jnp.float32)


def dot_nn(a, b):
    return lax.dot_general(a, b, (((1,), (0,)), ((), ())), preferred_element_type=jnp.float32)


def dot_tn(a, b):
    return lax.dot_general(a, b, (((0,), (0,)), ((), ())), preferred_element_type=jnp.float32)


def block(start, size):
    return pl.ds(pl.multiple_of(start * size, size), size)


def swiglu(gate_pre, up_pre, back, gate):
    sig = 1.0 / (1.0 + jnp.exp(-gate_pre))
    act = gate_pre * sig
    hid = act * up_pre
    scaled = back * gate
    return (
        jnp.sum(hid * back, axis=1, keepdims=True),
        (scaled * up_pre * (sig + act * (1.0 - sig))).astype(jnp.bfloat16),
        (scaled * act).astype(jnp.bfloat16),
        (hid * gate).astype(jnp.bfloat16),
    )


def first_body(cap, ff, rb, nb, n_e, x_ref, g_ref, *rest):
    po, px, py = [rest[i * n_e : (i + 1) * n_e] for i in range(3)]
    (rr_ref, gt_ref, rg_ref, h_ref, gate_ref, dgr_ref, sx, kx, ky, sy,
     p, xs, gs, r, g, hb, dp, p_sem, in_sem, rg_sem, h_sem, d_sem) = rest[3 * n_e :]
    _, src, _, tok = rr_ref.shape
    rows, width = r.shape[1:]
    team = xs.shape[1]
    half = width // 2
    shards = (po, px, py)

    def load(f, e, slot):
        return pltpu.make_async_copy(shards[f][e], p.at[slot], p_sem.at[slot])

    load(0, 0, 0).start()

    def fetch(s, slot):
        return (
            pltpu.make_async_copy(x_ref.at[block(s, team), pl.ds(0, tok)], xs.at[slot], in_sem.at[0, slot]),
            pltpu.make_async_copy(g_ref.at[block(s, team), pl.ds(0, tok)], gs.at[slot], in_sem.at[1, slot]),
        )

    for c in fetch(0, 0):
        c.start()

    @pl.loop(0, src // team)
    def _(s):
        slot = lax.rem(s, 2)

        @pl.when(s + 1 < src // team)
        def _():
            for c in fetch(s + 1, 1 - slot):
                c.start()

        for c in fetch(s, slot):
            c.wait()
        got = [[[], [], []] for _ in range(n_e)]
        for j in range(team):
            hits = [lax.broadcasted_iota(jnp.int32, (cap, tok), 0) == rr_ref[e, s * team + j] for e in range(n_e)]
            one = jnp.concatenate([hit.astype(jnp.float32) for hit in hits], axis=0).astype(jnp.bfloat16)
            rx, rg = dot_nn(one, xs[slot, j]), dot_nn(one, gs[slot, j])
            for e in range(n_e):
                got[e][0].append(rx[e * cap : (e + 1) * cap])
                got[e][1].append(rg[e * cap : (e + 1) * cap])
                got[e][2].append(jnp.sum(jnp.where(hits[e], gt_ref[e, s * team + j], 0.0), axis=1, keepdims=True))
        at = block(s, team * cap)
        for e in range(n_e):
            a, b, c = [v[0] if team == 1 else jnp.concatenate(v, axis=0) for v in got[e]]
            r[e, at, :] = a.astype(jnp.bfloat16)
            g[e, at, :] = b.astype(jnp.bfloat16)
            gate_ref[e, at, :] = c

    keep = []
    for e in range(n_e):
        for i, v in enumerate((r, g)):
            c = pltpu.make_async_copy(v.at[e], rg_ref.at[e, i], rg_sem.at[e, i])
            c.start()
            keep.append(c)
    dgr_ref[...] = jnp.zeros_like(dgr_ref)

    def put_h(f, e, slot):
        return pltpu.make_async_copy(hb.at[slot], h_ref.at[e, :, :, pl.ds(f * ff, ff)], h_sem.at[slot])

    def put_d(f, e, slot):
        low, high = ((sx, kx), (ky, sy))[f - 1]
        return (
            pltpu.make_async_copy(dp.at[slot, :, pl.ds(0, half)], low.at[e], d_sem.at[0, slot]),
            pltpu.make_async_copy(dp.at[slot, :, pl.ds(half, half)], high.at[e], d_sem.at[1, slot]),
        )

    for f in range(3):
        for e in range(n_e):
            slot = e % 2
            if e + 1 < n_e:
                load(f, e + 1, 1 - slot).start()
            elif f < 2:
                load(f + 1, 0, 1 - slot).start()
            load(f, e, slot).wait()
            if f > 0:
                put_h(f - 1, e, slot).wait()

            @pl.loop(0, rows // rb)
            def _(m):
                at = block(m, rb)
                pre = dot_nt(r[e, at, :], p[slot, pl.ds(0, 2 * ff), :])
                back = dot_nt(g[e, at, :], p[slot, pl.ds(2 * ff, ff), :])
                total, a, b, c = swiglu(pre[:, :ff], pre[:, ff:], back, gate_ref[e, at, :])
                dgr_ref[e, at, :] += total
                hb[slot, 0, at, :] = a
                hb[slot, 1, at, :] = b
                hb[slot, 2, at, :] = c

            put_h(f, e, slot).start()
            if f > 0:
                if f > 1:
                    for c in put_d(f - 1, e, slot):
                        c.wait()
                both = jnp.concatenate([hb[slot, 0], hb[slot, 1]], axis=1)

                @pl.loop(0, width // nb)
                def _(n):
                    at = block(n, nb)
                    dp[slot, 0 : 2 * ff, at] = dot_tn(both, r[e, :, at]).astype(jnp.bfloat16)
                    dp[slot, 2 * ff : 3 * ff, at] = dot_tn(hb[slot, 2], g[e, :, at]).astype(jnp.bfloat16)

                for c in put_d(f, e, slot):
                    c.start()
    for e in range(n_e):
        put_h(2, e, e % 2).wait()
        for c in put_d(2, e, e % 2):
            c.wait()
    for c in keep:
        c.wait()


def experts_first(x, g, po, px, py, rr, gt, cap, rb=640, nb=1024):
    n_e, src, _, tok = rr.shape
    width = x.shape[2]
    ff = po[0].shape[0] // 3
    rows = src * cap
    team = 16 // math.gcd(cap, 16)
    bf, f32 = jnp.bfloat16, jnp.float32
    anys, vm = pl.BlockSpec(memory_space=pl.ANY), pl.BlockSpec(memory_space=pltpu.VMEM)
    part = jax.ShapeDtypeStruct((n_e, 3 * ff, width // 2), bf)
    return pl.pallas_call(
        functools.partial(first_body, cap, ff, rb, nb, n_e),
        out_shape=(
            jax.ShapeDtypeStruct((n_e, 2, rows, width), bf),
            jax.ShapeDtypeStruct((n_e, 3, rows, 3 * ff), bf),
            jax.ShapeDtypeStruct((n_e, rows, 1), f32),
            jax.ShapeDtypeStruct((n_e, rows, 1), f32),
            part, part, part, part,
        ),
        in_specs=[anys] * (2 + 3 * n_e) + [vm] * 2,
        out_specs=(anys, anys, vm, vm, anys, anys, anys, anys),
        scratch_shapes=[
            pltpu.VMEM((2, 3 * ff, width), bf),
            pltpu.VMEM((2, team, tok, width), bf),
            pltpu.VMEM((2, team, tok, width), bf),
            pltpu.VMEM((n_e, rows, width), bf),
            pltpu.VMEM((n_e, rows, width), bf),
            pltpu.VMEM((2, 3, rows, ff), bf),
            pltpu.VMEM((2, 3 * ff, width), bf),
            pltpu.SemaphoreType.DMA((2,)),
            pltpu.SemaphoreType.DMA((2, 2)),
            pltpu.SemaphoreType.DMA((n_e, 2)),
            pltpu.SemaphoreType.DMA((2,)),
            pltpu.SemaphoreType.DMA((2, 2)),
        ],
        compiler_params=pltpu.CompilerParams(vmem_limit_bytes=VMEM_BYTES),
    )(x, g, *po, *px, *py, rr, gt)


def spread_tiles(cap, nb, h, p, rc_ref, own_ref, sib_ref, acc, stage, st_sem):
    n_e = h.shape[0]
    nz, tok = stage.shape[2:4]
    tiles = p.shape[2] // nb

    def put(n, slot):
        return [
            pltpu.make_async_copy(stage.at[slot, w], ref.at[:, :, block(n, nb)], st_sem.at[slot, w])
            for w, ref in enumerate((own_ref, sib_ref))
        ]

    @pl.loop(0, tiles)
    def _(n):
        slot = lax.rem(n, 2)
        for e in range(n_e):
            acc[e] = dot_nn(h[e], p[e, :, block(n, nb)])

        @pl.when(n >= 2)
        def _():
            for c in put(n, slot):
                c.wait()

        def one(z, w):
            s = 2 * z + w
            hits = [
                (lax.broadcasted_iota(jnp.int32, (tok, cap), 1) == rc_ref[e, s]).astype(jnp.float32) for e in range(n_e)
            ]
            hit = jnp.concatenate(hits, axis=1).astype(jnp.bfloat16)
            part = jnp.concatenate([acc[e, block(s, cap)] for e in range(n_e)], axis=0).astype(jnp.bfloat16)
            stage[slot, w, z] = dot_nn(hit, part).astype(jnp.bfloat16)

        if nz <= 4:
            for z in range(nz):
                for w in range(2):
                    one(z, w)
        else:

            @pl.loop(0, nz)
            def _(z):
                for w in range(2):
                    one(z, w)

        for c in put(n, slot):
            c.start()

    for slot in range(2):
        for c in put(slot, slot):
            c.wait()


def last_body(cap, ff, rb, nb, n_e, rg_ref, ha_ref, gate_ref, dgr_in, *rest):
    po, px, py, da, db = [rest[i * n_e : (i + 1) * n_e] for i in range(5)]
    (rr_ref, rc_ref, hd_ref, dg_ref, own_ref, sib_ref,
     p, pd, h, r, g, hb, dgr, acc, stage, p_sem, h_sem, rg_sem, hb_sem, st_sem) = rest[5 * n_e :]
    _, src, _, tok = rr_ref.shape
    rows, width = ha_ref.shape[2], rg_ref.shape[3]
    half = width // 2
    hidden = 4 * ff
    early, late = [], []
    for e in range(n_e):
        for i in range(2):
            for j, ref in enumerate((da, db)):
                early.append(pltpu.make_async_copy(
                    ref[e].at[pl.ds(i * ff, ff)], p.at[e, pl.ds(i * hidden + 3 * ff, ff), pl.ds(j * half, half)], p_sem.at[e, 2 * i + j]))
            for j, ref in enumerate((po, px, py)):
                late.append(pltpu.make_async_copy(
                    ref[e].at[pl.ds(i * ff, ff)], p.at[e, pl.ds(i * hidden + j * ff, ff)], p_sem.at[e, 6 + 3 * i + j]))
            late.append(pltpu.make_async_copy(ha_ref.at[e, i], h.at[e, :, pl.ds(i * hidden, 3 * ff)], h_sem.at[e, i]))
        for j, ref in enumerate((da, db)):
            early.append(pltpu.make_async_copy(
                ref[e].at[pl.ds(2 * ff, ff)], pd.at[e, :, pl.ds(j * half, half)], p_sem.at[e, 4 + j]))
    per = rows // rb
    steps = [(e, m) for e in range(n_e) for m in range(per)]

    def fetch(k):
        e, m = steps[k]
        at = pl.ds(m * rb, rb)
        return [
            pltpu.make_async_copy(rg_ref.at[e, i, at], v.at[k % 2], rg_sem.at[i, k % 2]) for i, v in enumerate((r, g))
        ]

    for c in early + fetch(0):
        c.start()
    for c in late:
        c.start()
    for c in early:
        c.wait()
    dgr[...] = dgr_in[...]
    for k, (e, m) in enumerate(steps):
        if k + 1 < len(steps):
            for c in fetch(k + 1):
                c.start()
        for c in fetch(k):
            c.wait()
        at = pl.ds(m * rb, rb)
        rm, gm = r[k % 2], g[k % 2]
        gate_pre = dot_nt(rm, p[e, pl.ds(3 * ff, ff), :])
        up_pre = dot_nt(rm, p[e, pl.ds(hidden + 3 * ff, ff), :])
        back = dot_nt(gm, pd[e])
        total, a, b, c = swiglu(gate_pre, up_pre, back, gate_ref[e, at, :])
        dgr[e, at, :] += total
        h[e, at, pl.ds(3 * ff, ff)] = a
        h[e, at, pl.ds(hidden + 3 * ff, ff)] = b
        hb[e, 0, at, :] = a
        hb[e, 1, at, :] = b
        hb[e, 2, at, :] = c
    outs = [pltpu.make_async_copy(hb.at[e], hd_ref.at[e], hb_sem.at[e]) for e in range(n_e)]
    for c in outs:
        c.start()
    for e in range(n_e):

        @pl.loop(0, src)
        def _(s):
            hit = lax.broadcasted_iota(jnp.int32, (cap, tok), 0) == rr_ref[e, s]
            dg_ref[e, s] = jnp.sum(jnp.where(hit, dgr[e, block(s, cap), :], 0.0), axis=0, keepdims=True)

    for c in late:
        c.wait()
    spread_tiles(cap, nb, h, p, rc_ref, own_ref, sib_ref, acc, stage, st_sem)
    for c in outs:
        c.wait()


def tile_width(src):
    return 512 if src <= 8 else 128


def experts_last(rg, ha, gate, dgr, po, px, py, da, db, rr, rc, cap, rb=320):
    n_e, src, _, tok = rr.shape
    rows, width = rg.shape[2:]
    ff = po[0].shape[0] // 3
    nz = src // 2
    nb = tile_width(src)
    bf, f32 = jnp.bfloat16, jnp.float32
    anys, vm = pl.BlockSpec(memory_space=pl.ANY), pl.BlockSpec(memory_space=pltpu.VMEM)
    side = jax.ShapeDtypeStruct((nz, tok, width), bf)
    return pl.pallas_call(
        functools.partial(last_body, cap, ff, rb, nb, n_e),
        out_shape=(
            jax.ShapeDtypeStruct((n_e, 3, rows, ff), bf),
            jax.ShapeDtypeStruct((n_e, src, 1, tok), f32),
            side, side,
        ),
        in_specs=[anys] * 2 + [vm] * 2 + [anys] * (5 * n_e) + [vm] * 2,
        out_specs=(anys, vm, anys, anys),
        scratch_shapes=[
            pltpu.VMEM((n_e, 8 * ff, width), bf),
            pltpu.VMEM((n_e, ff, width), bf),
            pltpu.VMEM((n_e, rows, 8 * ff), bf),
            pltpu.VMEM((2, rb, width), bf),
            pltpu.VMEM((2, rb, width), bf),
            pltpu.VMEM((n_e, 3, rows, ff), bf),
            pltpu.VMEM((n_e, rows, 1), f32),
            pltpu.VMEM((n_e, rows, nb), f32),
            pltpu.VMEM((2, 2, nz, tok, nb), bf),
            pltpu.SemaphoreType.DMA((n_e, 12)),
            pltpu.SemaphoreType.DMA((n_e, 2)),
            pltpu.SemaphoreType.DMA((2, 2)),
            pltpu.SemaphoreType.DMA((n_e,)),
            pltpu.SemaphoreType.DMA((2, 2)),
        ],
        compiler_params=pltpu.CompilerParams(vmem_limit_bytes=VMEM_BYTES),
    )(rg, ha, gate, dgr, *po, *px, *py, *da, *db, rr, rc)


def mixture_body(cap, ff, nb, n_e, ha_ref, hd_ref, *rest):
    po, px, py, da, db = [rest[i * n_e : (i + 1) * n_e] for i in range(5)]
    rc_ref, own_ref, sib_ref, p, h, acc, stage, p_sem, st_sem = rest[5 * n_e :]
    half = p.shape[2] // 2
    copies = []
    for e in range(n_e):
        for j, ref in enumerate((po, px, py)):
            copies.append(pltpu.make_async_copy(ref[e].at[pl.ds(2 * ff, ff)], p.at[e, pl.ds(j * ff, ff)], p_sem.at[e, j]))
        for j, ref in enumerate((da, db)):
            copies.append(pltpu.make_async_copy(
                ref[e].at[pl.ds(2 * ff, ff)], p.at[e, pl.ds(3 * ff, ff), pl.ds(j * half, half)], p_sem.at[e, 3 + j]))
        copies.append(pltpu.make_async_copy(ha_ref.at[e, 2], h.at[e, :, pl.ds(0, 3 * ff)], p_sem.at[e, 5]))
        copies.append(pltpu.make_async_copy(hd_ref.at[e, 2], h.at[e, :, pl.ds(3 * ff, ff)], p_sem.at[e, 6]))
    for c in copies:
        c.start()
    for c in copies:
        c.wait()
    spread_tiles(cap, nb, h, p, rc_ref, own_ref, sib_ref, acc, stage, st_sem)


def experts_mixture(ha, hd, po, px, py, da, db, rc, cap):
    n_e, src, tok, _ = rc.shape
    rows, width = ha.shape[2], po[0].shape[1]
    ff = po[0].shape[0] // 3
    nz = src // 2
    nb = tile_width(src)
    bf, f32 = jnp.bfloat16, jnp.float32
    anys, vm = pl.BlockSpec(memory_space=pl.ANY), pl.BlockSpec(memory_space=pltpu.VMEM)
    side = jax.ShapeDtypeStruct((nz, tok, width), bf)
    return pl.pallas_call(
        functools.partial(mixture_body, cap, ff, nb, n_e),
        out_shape=(side, side),
        in_specs=[anys] * (2 + 5 * n_e) + [vm],
        out_specs=(anys, anys),
        scratch_shapes=[
            pltpu.VMEM((n_e, 4 * ff, width), bf),
            pltpu.VMEM((n_e, rows, 4 * ff), bf),
            pltpu.VMEM((n_e, rows, nb), f32),
            pltpu.VMEM((2, 2, nz, tok, nb), bf),
            pltpu.SemaphoreType.DMA((n_e, 7)),
            pltpu.SemaphoreType.DMA((2, 2)),
        ],
        compiler_params=pltpu.CompilerParams(vmem_limit_bytes=VMEM_BYTES),
    )(ha, hd, *po, *px, *py, *da, *db, rc)


def grads_body(ff, h_ref, rg_ref, low, high, ht):
    part = pl.program_id(1)

    @pl.when(part == 0)
    def _():
        for i in range(3):
            ht[pl.ds(i * ff, ff), :] = h_ref[0, i].T

    def out(ref):
        ref[0, 0 : 2 * ff, :] = dot_nn(ht[0 : 2 * ff, :], rg_ref[0, 0]).astype(jnp.bfloat16)
        ref[0, 2 * ff : 3 * ff, :] = dot_nn(ht[2 * ff : 3 * ff, :], rg_ref[0, 1]).astype(jnp.bfloat16)

    @pl.when(part == 0)
    def _():
        out(low)

    @pl.when(part == 1)
    def _():
        out(high)


def expert_grads(h, rg, quarter, ff):
    n_e, _, rows, _ = h.shape
    half = rg.shape[3] // 2
    side = jax.ShapeDtypeStruct((n_e, 3 * ff, half), jnp.bfloat16)
    return pl.pallas_call(
        functools.partial(grads_body, ff),
        out_shape=(side, side),
        grid=(n_e, 2),
        in_specs=[
            pl.BlockSpec((1, 3, rows, ff), lambda e, j: (e, 0, 0, quarter)),
            pl.BlockSpec((1, 2, rows, half), lambda e, j: (e, 0, 0, j)),
        ],
        out_specs=(pl.BlockSpec((1, 3 * ff, half), lambda e, j: (e, 0, 0)),) * 2,
        scratch_shapes=[pltpu.VMEM((3 * ff, rows), jnp.bfloat16)],
        compiler_params=pltpu.CompilerParams(vmem_limit_bytes=VMEM_BYTES),
    )(h, rg)


fence = lax.optimization_barrier


def all_heads(values):
    return values.reshape(values.shape[0], values.shape[1] // HD, HD)


def plus(a, b):
    return a.astype(jnp.float32) + b.astype(jnp.float32)


def on_device(
    hidden_in,
    cotangent,
    attention_gain,
    query_gain,
    key_gain,
    mixture_gain,
    query_weight,
    key_weight,
    value_weight,
    output_weight,
    router_weight,
    gate_weight,
    up_weight,
    down_weight,
    routes,
    segments,
):
    bf16, f32 = jnp.bfloat16, jnp.float32
    n_dp, owners = lax.axis_size("dp"), lax.axis_size("expert")
    nz = owners // 2
    n_dev = n_dp * owners
    tokens, width = hidden_in.shape
    half = width // 2
    unit = width // (n_dev // 2)
    top = routes.shape[1]
    exp_dev = gate_weight.shape[0]
    experts = exp_dev * owners
    cap = max(2, tokens * top * 5 // (experts * 4))
    ff = gate_weight.shape[2]
    rows_dev = attention_gain.shape[0]
    score_scale = HD ** (-0.5)
    dp, ex = lax.axis_index("dp"), lax.axis_index("expert")
    core, zc = ex % 2, ex // 2
    device = dp * owners + ex

    def swap(v, axis, bit):
        size = n_dp if axis == "dp" else owners
        return lax.ppermute(v, axis, [(i, i ^ bit) for i in range(size)])

    def swap_core(v):
        return swap(v, "expert", 1)

    def ring(v):
        return lax.ppermute(v, "expert", [(i, (i + 2) % owners) for i in range(owners)])

    def swap_x(v):
        return swap(v, "dp", 1)

    def swap_y(v):
        return swap(v, "dp", 2)

    def in_order(bit, mine, other, axis):
        return jnp.where(
            bit == 0,
            jnp.concatenate([mine, other], axis=axis),
            jnp.concatenate([other, mine], axis=axis),
        )

    def half_of(v, which, axis):
        return lax.dynamic_slice_in_dim(v, which * (v.shape[axis] // 2), v.shape[axis] // 2, axis)

    def other_first(v):
        return jnp.concatenate([v[tokens:], v[:tokens]], axis=0)

    def chip_row(plane, r):
        return ((dp ^ plane) * nz + (zc - r) % nz) * unit

    def turn(v):
        flipped = jnp.flip(v, 0)
        doubled = jnp.concatenate([flipped, flipped], axis=0)
        return lax.dynamic_slice_in_dim(doubled, nz - 1 - zc, nz, 0)

    def relative_sources(v):
        v = turn(v.reshape((nz, 2) + v.shape[1:]))
        v = jnp.where(core == 1, jnp.flip(v, 1), v)
        return v.reshape((owners,) + v.shape[2:])

    bits = []
    b = 1
    while b < owners:
        bits.append(("expert", b, (ex // b) % 2))
        b *= 2
    b = 1
    while b < n_dp:
        bits.append(("dp", b, (dp // b) % 2))
        b *= 2

    sources = (query_weight, key_weight, value_weight, output_weight)
    theirs = jnp.concatenate([half_of(w, 1 - core, 1) for w in sources], axis=1)
    mine = jnp.concatenate([half_of(w, core, 1) for w in sources], axis=1)
    small = jnp.concatenate(
        [attention_gain, query_gain, key_gain, mixture_gain, router_weight.T.reshape(-1)]
    )[None]
    theirs = swap_core(theirs)
    documents = jnp.concatenate([segments, swap_core(segments)], axis=0)
    for axis, bit, mark in bits:
        small = in_order(mark, small, swap(small, axis, bit), 0)
    piece = in_order(core, mine, theirs, 0)
    own_parts = tuple(
        jnp.concatenate([gate_weight[e].T, up_weight[e].T, down_weight[e]], axis=0)
        for e in range(exp_dev)
    )
    route_rows = routes.T.astype(bf16).reshape(-1, width)
    pad = -route_rows.shape[0] % 16
    cot_piece = jnp.concatenate(
        [cotangent, route_rows, jnp.zeros((pad, width), bf16)], axis=0
    )
    nought = jnp.zeros((1, 1), bf16)
    piece, small, documents, own_parts, cot_piece, nought = fence(
        (piece, small, documents, own_parts, cot_piece, nought)
    )

    weights = jnp.broadcast_to(nought, (width, 4 * half))
    cut = unit // 2
    before = None
    cot_steps = [cot_piece]
    for r in range(nz):
        by_x, by_y = swap_x(piece), swap_y(piece)
        following, low, high = (), (), ()
        if r + 1 < nz:
            following = ring(piece)
        if before is not None:
            low, high = swap_y(before[0][:cut]), swap_x(before[1][cut:])
        if r + 1 == nz:
            cot_steps.append(ring(cot_steps[-1]))
        weights = lax.dynamic_update_slice(weights, piece, (chip_row(0, r), 0))
        if before is not None:
            weights = lax.dynamic_update_slice(weights, before[0], (chip_row(1, r - 1), 0))
            weights = lax.dynamic_update_slice(weights, before[1], (chip_row(2, r - 1), 0))
        by_x, by_y, following, low, high, weights, cot_steps = fence(
            (by_x, by_y, following, low, high, weights, cot_steps)
        )
        if before is not None:
            weights = lax.dynamic_update_slice(weights, low, (chip_row(3, r - 1), 0))
            weights = lax.dynamic_update_slice(weights, high, (chip_row(3, r - 1) + cut, 0))
        before = (by_x, by_y)
        piece = following
    low, high = swap_y(before[0][:cut]), swap_x(before[1][cut:])
    weights = lax.dynamic_update_slice(weights, before[0], (chip_row(1, nz - 1), 0))
    weights = lax.dynamic_update_slice(weights, before[1], (chip_row(2, nz - 1), 0))

    gains_all = small[:, : 4 * rows_dev].reshape(n_dev, 4, rows_dev)
    gains_all = gains_all.swapaxes(0, 1).reshape(4, width).astype(f32)
    attention_gain_full, query_gain_full, key_gain_full, mixture_gain_full = (
        gains_all[0],
        gains_all[1],
        gains_all[2],
        gains_all[3],
    )
    router_t = (
        small[:, 4 * rows_dev :]
        .reshape(n_dev, experts, rows_dev)
        .swapaxes(0, 1)
        .reshape(experts, width)
    )
    query_gain_half = half_of(query_gain_full, core, 0)
    key_gain_half = half_of(key_gain_full, core, 0)
    residual = hidden_in.astype(f32)
    scale_one = norm_scale(residual)
    cosine, sine = rotary_tables(documents, HD)
    cosine = cosine.reshape(2 * tokens, 1, HD // 2)
    sine = sine.reshape(2 * tokens, 1, HD // 2)
    order = jnp.arange(tokens, dtype=jnp.int32)
    allowed = (documents[:, :, None] == documents[:, None, :]) & (
        order[:, None] >= order[None, :]
    )
    unit_one = residual * scale_one
    normed = (unit_one * attention_gain_full).astype(bf16)
    normed = jnp.concatenate([normed, swap_core(normed)], axis=0)
    (low, high, weights, normed, cosine, sine, router_t) = fence(
        (low, high, weights, normed, cosine, sine, router_t)
    )
    weights = lax.dynamic_update_slice(weights, low, (chip_row(3, nz - 1), 0))
    weights = lax.dynamic_update_slice(weights, high, (chip_row(3, nz - 1) + cut, 0))
    qkv_weight, out_weight = weights[:, : 3 * half], weights[:, 3 * half :]

    by_x = [swap_x(own_parts[0])]
    by_y = [swap_y(own_parts[0])]

    raw = jnp.dot(normed, qkv_weight, preferred_element_type=f32)
    query_raw, key_raw = raw[:, :half], raw[:, half : 2 * half]
    value_heads = raw[:, 2 * half :].astype(bf16)
    squares = jnp.stack(
        [jnp.sum(query_raw * query_raw, axis=-1), jnp.sum(key_raw * key_raw, axis=-1)]
    )
    squares = squares + jnp.roll(swap_core(squares), tokens, axis=1)
    scales = lax.rsqrt(squares / width + epsilon)
    query_scale, key_scale = scales[0][:, None], scales[1][:, None]
    query_unit, key_unit = query_raw * query_scale, key_raw * key_scale
    heads = half // HD

    def by_sequence(v):
        return v.reshape(2, tokens, heads, HD)

    query_heads = by_sequence(
        rotate(all_heads(query_unit * query_gain_half), cosine, sine).astype(bf16)
    )
    key_heads = by_sequence(rotate(all_heads(key_unit * key_gain_half), cosine, sine).astype(bf16))
    value_heads = by_sequence(value_heads)
    scores = (
        jnp.einsum("nthd,nshd->nhts", query_heads, key_heads, preferred_element_type=f32)
        * score_scale
    )
    scores = jnp.where(allowed[:, None], scores, masked_score)
    peak = jnp.max(scores, axis=-1, keepdims=True)
    grown = jnp.exp(scores - peak)
    chances = grown / jnp.sum(grown, axis=-1, keepdims=True)
    chances_low = chances.astype(bf16)
    context = jnp.einsum("nhts,nshd->nthd", chances_low, value_heads, preferred_element_type=f32)
    context = context.astype(bf16).reshape(2 * tokens, half)
    context_full = in_order(core, context, other_first(swap_core(context)), 1)
    while len(cot_steps) < nz:
        cot_steps.append(ring(cot_steps[-1]))
    out_half = jnp.dot(context_full, out_weight, preferred_element_type=f32)
    attended = in_order(core, out_half[:tokens], swap_core(out_half[tokens:]), 1)
    middle = residual + attended
    scale_two = norm_scale(middle)
    unit_two = middle * scale_two
    mixed_in = (unit_two * mixture_gain_full).astype(bf16)
    logits = jnp.einsum("et,dt->ed", router_t, mixed_in, preferred_element_type=f32)
    router_probs = jax.nn.softmax(logits, axis=0)
    prob_high = router_probs.astype(bf16)
    prob_low = (router_probs - prob_high.astype(f32)).astype(bf16)
    prob_rows = jnp.concatenate([prob_high, prob_low], axis=0).reshape(-1, width)
    n_prob = prob_rows.shape[0]
    pad = -n_prob % 16
    mixed_piece = jnp.concatenate([mixed_in, prob_rows, jnp.zeros((pad, width), bf16)], axis=0)
    mixed_piece, by_x[0], by_y[0], cot_steps = fence((mixed_piece, by_x[0], by_y[0], cot_steps))

    def place(buffer, piece, r, which):
        return lax.dynamic_update_slice(buffer, piece[None], (2 * r + which, 0, 0))

    for e in range(1, exp_dev):
        by_x.append(swap_x(own_parts[e]))
        by_y.append(swap_y(own_parts[e]))
    mixed_last = mixed_piece
    mixed_all = jnp.broadcast_to(nought, (owners,) + mixed_piece.shape)
    cot_all = jnp.broadcast_to(nought, (owners,) + cot_piece.shape)
    for r in range(nz):
        following = ring(mixed_last) if r + 1 < nz else ()
        other, cot_other = swap_core(mixed_last), swap_core(cot_steps[r])
        mixed_all = place(mixed_all, mixed_last, r, 0)
        cot_all = place(cot_all, cot_steps[r], r, 0)
        other, following, cot_other, mixed_all, cot_all = fence(
            (other, following, cot_other, mixed_all, cot_all)
        )
        mixed_all = place(mixed_all, other, r, 1)
        cot_all = place(cot_all, cot_other, r, 1)
        mixed_last = following
    probs = mixed_all[:, tokens : tokens + n_prob].reshape(owners, 2, experts, tokens)
    probs_all = probs[:, 0].astype(f32) + probs[:, 1].astype(f32)
    routes_all = cot_all[:, tokens : tokens + top * tokens // width]
    routes_all = routes_all.reshape(owners, top, tokens).astype(jnp.int32)

    lower = (order[:, None] <= order[None, :]).astype(bf16)

    number = ex * exp_dev + jnp.arange(exp_dev, dtype=jnp.int32)[:, None, None]
    hit = jnp.any(routes_all[None] == number[..., None], axis=2)
    rank = jnp.dot(
        hit.reshape(exp_dev * owners, tokens).astype(bf16), lower, preferred_element_type=f32
    )
    rank = jnp.where(hit, rank.reshape(hit.shape).astype(jnp.int32) - 1, -1)
    rank_row, rank_col = rank[:, :, None, :], rank[:, :, :, None]
    gate_row = lax.dynamic_slice_in_dim(probs_all, ex * exp_dev, exp_dev, 1).swapaxes(0, 1)[
        :, :, None, :
    ]
    mixed_all, cot_all, by_x, by_y, rank_row, rank_col, gate_row = fence(
        (mixed_all, cot_all, by_x, by_y, rank_row, rank_col, gate_row)
    )

    corner_low = tuple(swap_y(v[:, :half]) for v in by_x)
    corner_high = tuple(swap_x(v[:, half:]) for v in by_y)
    shards = (own_parts, tuple(by_x), tuple(by_y))
    rows, acts, gates, products, send_x, keep_x, keep_y, send_y = experts_first(
        mixed_all, cot_all, *shards, rank_row, gate_row, cap
    )
    got_x, got_y = swap_x(send_x), swap_y(send_y)
    shards = shards + (corner_low, corner_high)
    acts_last, gate_backs, copied, copied_other = experts_last(
        rows, acts, gates, products, *shards, rank_row, rank_col, cap
    )

    gate_block = jnp.zeros((owners, experts, tokens), f32)
    gate_block = lax.dynamic_update_slice(
        gate_block, gate_backs[:, :, 0].swapaxes(0, 1), (0, ex * exp_dev, 0)
    )
    gate_block = gate_block.reshape(nz, 2, experts, tokens)

    def blocks_of(v, got_v):
        return [plus(v[r], got_v[r]) for r in range(nz)]

    def sum_ring(blocks, kind):
        total = blocks[1]
        for r in range(2, nz):
            total = blocks[r] + ring(total.astype(kind)).astype(f32)
        return blocks[0] + ring(total.astype(kind)).astype(f32)

    got_gate, got_copy = swap_core(gate_block[:, 1]), swap_core(copied_other)
    got_gate, got_copy = fence((got_gate, got_copy))
    prob_upstream = sum_ring(blocks_of(gate_block[:, 0], got_gate), f32)
    copies_grad = sum_ring(blocks_of(copied, got_copy), bf16)
    send_last_x, send_last_y = expert_grads(acts_last, rows, 0, ff)
    got_last_x, got_last_y = swap_x(send_last_x), swap_y(send_last_y)
    own_low, own_high = expert_grads(acts, rows, 0, ff)
    mixture, mixture_other = experts_mixture(acts, acts_last, *shards, rank_col, cap)
    (prob_upstream, copies_grad, got_x, got_y, own_low, own_high, mixture, mixture_other) = fence(
        (prob_upstream, copies_grad, got_x, got_y, own_low, own_high, mixture, mixture_other)
    )

    own_low, own_high = plus(own_low, got_x), plus(own_high, got_y)
    upstream = cotangent.astype(f32)
    picked = jnp.any(
        routes.T[None] == jnp.arange(experts, dtype=jnp.int32)[:, None, None], axis=1
    )
    prob_upstream = jnp.where(picked, prob_upstream, 0.0)
    logit_upstream = (
        router_probs
        * (prob_upstream - jnp.sum(router_probs * prob_upstream, axis=0, keepdims=True))
    ).astype(bf16)
    mixed_upstream = copies_grad + jnp.einsum(
        "et,ed->td", logit_upstream, router_t, preferred_element_type=f32
    )
    router_grad = jnp.einsum("et,td->ed", logit_upstream, mixed_in, preferred_element_type=f32)
    mixture_gain_grad = jnp.sum(mixed_upstream * unit_two, axis=0)
    middle_grad = upstream + norm_back(mixed_upstream * mixture_gain_full, unit_two, scale_two)
    branch = middle_grad.astype(bf16)
    branch_half = jnp.concatenate(
        [half_of(branch, core, 1), swap_core(half_of(branch, 1 - core, 1))], axis=0
    )
    context_part = jnp.einsum(
        "td,cd->tc", branch_half, out_weight, preferred_element_type=f32
    ).astype(bf16)
    context_up = half_of(context_part, core, 1).astype(f32) + other_first(
        swap_core(half_of(context_part, 1 - core, 1))
    ).astype(f32)
    context_up = by_sequence(context_up.astype(bf16))
    output_grad = jnp.einsum("tc,td->cd", context_full, branch_half, preferred_element_type=f32)
    output_grad = output_grad.astype(bf16)
    context_up, got_last_x, got_last_y, output_grad = fence(
        (context_up, got_last_x, got_last_y, output_grad)
    )
    more_y = swap_y(plus(keep_y, got_last_x).astype(bf16))
    more_x = swap_x(plus(keep_x, got_last_y).astype(bf16))
    chance_up = jnp.einsum("nthd,nshd->nhts", context_up, value_heads, preferred_element_type=f32)
    value_term = jnp.einsum(
        "nhts,nthd->nshd", chances_low, context_up, preferred_element_type=f32
    )
    score_up = (
        chances * (chance_up - jnp.sum(chances * chance_up, axis=-1, keepdims=True))
    ).astype(bf16)
    query_term = (
        jnp.einsum("nhts,nshd->nthd", score_up, key_heads, preferred_element_type=f32)
        * score_scale
    )
    key_term = (
        jnp.einsum("nhts,nthd->nshd", score_up, query_heads, preferred_element_type=f32)
        * score_scale
    )
    value_up = value_term.astype(bf16).reshape(2 * tokens, half)
    value_grad = jnp.einsum("tc,td->cd", normed, value_up, preferred_element_type=f32).astype(bf16)

    def unturn(v):
        return rotate_back(v.reshape(2 * tokens, heads, HD), cosine, sine).reshape(
            2 * tokens, half
        )

    query_back, key_back = unturn(query_term), unturn(key_term)
    query_gain_grad = jnp.sum(query_back * query_unit, axis=0)
    key_gain_grad = jnp.sum(key_back * key_unit, axis=0)
    query_back, key_back = query_back * query_gain_half, key_back * key_gain_half
    means = jnp.stack(
        [jnp.sum(query_back * query_unit, axis=-1), jnp.sum(key_back * key_unit, axis=-1)]
    )
    means = (means + jnp.roll(swap_core(means), tokens, axis=1)) / width
    query_up = (query_scale * (query_back - query_unit * means[0][:, None])).astype(bf16)
    key_up = (key_scale * (key_back - key_unit * means[1][:, None])).astype(bf16)
    qk_up = jnp.concatenate([query_up, key_up], axis=1)
    first = jnp.einsum("tc,td->cd", normed, qk_up, preferred_element_type=f32).astype(bf16)
    second = jnp.concatenate([value_grad, output_grad], axis=1)
    first, second, more_y, more_x = fence((first, second, more_y, more_x))

    def chip_rows(v, plane, r):
        return lax.dynamic_slice_in_dim(v, chip_row(plane, r), unit, 0)

    def several(v, picks):
        return jnp.concatenate([chip_rows(v, plane, r) for plane, r in picks], axis=0)

    near = list(range(1, nz // 2 + 1))
    far = list(range(nz // 2 + 1, nz)) + [0]

    def step_one(rs):
        sent = several(first, [(1, r) for r in rs] + [(3, r) for r in rs])
        back = several(second, [(2, r) for r in rs] + [(3, r) for r in rs])
        return swap_x(sent), swap_y(back)

    def step_two(rs, by_x, by_y):
        n = len(rs) * unit
        more_y = plus(several(first, [(2, r) for r in rs]), by_x[n:]).astype(bf16)
        more_x = plus(several(second, [(1, r) for r in rs]), by_y[n:]).astype(bf16)
        return swap_y(more_y), swap_x(more_x)

    def step_three(rs, by_x, by_y, more_y, more_x):
        n = len(rs) * unit
        left = plus(several(first, [(0, r) for r in rs]), by_x[:n]) + more_y.astype(f32)
        right = plus(several(second, [(0, r) for r in rs]), by_y[:n]) + more_x.astype(f32)
        whole = jnp.concatenate([left, right], axis=1)
        return {r: whole[i * unit : (i + 1) * unit] for i, r in enumerate(rs)}

    near_x, near_y = step_one(near)
    own_low = own_low + more_y.astype(f32)
    own_high = own_high + more_x.astype(f32)
    got_mix = swap_core(mixture_other)
    qkv_up = jnp.concatenate([qk_up, value_up], axis=1)
    normed_part = jnp.einsum("td,cd->tc", qkv_up, qkv_weight, preferred_element_type=f32)
    normed_up = normed_part[:tokens] + swap_core(normed_part[tokens:].astype(bf16)).astype(f32)
    attention_gain_grad = jnp.sum(normed_up * unit_one, axis=0)
    hidden_grad = middle_grad + norm_back(normed_up * attention_gain_full, unit_one, scale_one)
    zeros = jnp.zeros_like(query_gain_grad)
    small_sum = jnp.concatenate(
        [
            attention_gain_grad.reshape(n_dev, rows_dev),
            in_order(core, query_gain_grad, zeros, 0).reshape(n_dev, rows_dev),
            in_order(core, key_gain_grad, zeros, 0).reshape(n_dev, rows_dev),
            mixture_gain_grad.reshape(n_dev, rows_dev),
            router_grad.reshape(experts, n_dev, rows_dev)
            .swapaxes(0, 1)
            .reshape(n_dev, experts * rows_dev),
        ],
        axis=1,
    )

    def fold(v, i):
        axis, bit, mark = bits[i]
        return half_of(v, mark, 0) + swap(half_of(v, 1 - mark, 0), axis, bit)

    near_x, near_y, got_mix, hidden_grad, small_sum = fence(
        (near_x, near_y, got_mix, hidden_grad, small_sum)
    )
    small_sum = fold(small_sum, len(bits) - 1)
    mix_blocks = blocks_of(mixture, got_mix)
    mixed = sum_ring(mix_blocks, bf16)
    near_more = step_two(near, near_x, near_y)
    far_x, far_y = step_one(far)
    near_more, far_x, far_y, small_sum, mixed = fence((near_more, far_x, far_y, small_sum, mixed))
    small_sum = fold(small_sum, len(bits) - 2)
    far_more = step_two(far, far_x, far_y)
    blocks = step_three(near, near_x, near_y, *near_more)
    total = blocks[near[0]]
    for r in near[1:]:
        total = blocks[r] + ring(total.astype(bf16)).astype(f32)
    got_total = ring(total.astype(bf16))
    layer_out = (middle + mixed).astype(bf16)
    far_more, got_total, small_sum = fence((far_more, got_total, small_sum))
    blocks = step_three(far, far_x, far_y, *far_more)
    for i, r in enumerate(far):
        total = blocks[r] + got_total.astype(f32)
        if i + 1 < len(far):
            got_total = ring(total.astype(bf16))
    for i in reversed(range(len(bits) - 2)):
        small_sum = fold(small_sum, i)
    small_sum = small_sum[0]
    gain_parts = small_sum[: 4 * rows_dev].reshape(4, rows_dev)
    router_part = small_sum[4 * rows_dev :].reshape(experts, rows_dev).T
    kept_rows = half_of(total, core, 0)
    got_rows = swap_core(half_of(total, 1 - core, 0))
    weight_grads = [
        in_order(
            core, kept_rows[:, i * half : (i + 1) * half], got_rows[:, i * half : (i + 1) * half], 1
        )
        for i in range(4)
    ]
    expert_grad = jnp.concatenate([own_low, own_high], axis=2)
    return (
        layer_out,
        hidden_grad,
        gain_parts[0],
        gain_parts[1],
        gain_parts[2],
        gain_parts[3],
        weight_grads[0],
        weight_grads[1],
        weight_grads[2],
        weight_grads[3],
        router_part,
        expert_grad[:, :ff].swapaxes(1, 2),
        expert_grad[:, ff : 2 * ff].swapaxes(1, 2),
        expert_grad[:, 2 * ff :],
    )


def solution(mesh):
    return jax.shard_map(
        on_device,
        mesh=mesh,
        in_specs=(
            P(("dp", "expert"), None),
            P(("dp", "expert"), None),
            P(("dp", "expert")),
            P(("dp", "expert")),
            P(("dp", "expert")),
            P(("dp", "expert")),
            P(("dp", "expert"), None),
            P(("dp", "expert"), None),
            P(("dp", "expert"), None),
            P(("dp", "expert"), None),
            P(("dp", "expert"), None),
            P("expert", None, "dp"),
            P("expert", None, "dp"),
            P("expert", "dp", None),
            P(("dp", "expert"), None),
            P(("dp", "expert"), None),
        ),
        out_specs=(
            P(("dp", "expert"), None),
            P(("dp", "expert"), None),
            P(("dp", "expert")),
            P(("dp", "expert")),
            P(("dp", "expert")),
            P(("dp", "expert")),
            P(("dp", "expert"), None),
            P(("dp", "expert"), None),
            P(("dp", "expert"), None),
            P(("dp", "expert"), None),
            P(("dp", "expert"), None),
            P("expert", None, "dp"),
            P("expert", None, "dp"),
            P("expert", "dp", None),
        ),
        check_vma=False,
    )
```

```python
import functools
import math

import jax
import jax.numpy as jnp
from jax import lax
from jax.experimental import pallas as pl
from jax.experimental.layout import Layout, with_layout_constraint
from jax.experimental.pallas import tpu as pltpu
from jax.sharding import PartitionSpec as P

HD = 128


epsilon = 1e-05
rope_base = 10000.0
masked_score = -1e30


def rotary_tables(segments, head_size):
    length = segments.shape[-1]
    order = jnp.arange(length, dtype=jnp.int32)
    starts = jnp.sum((segments[..., None, :] < segments[..., :, None]).astype(jnp.int32), axis=-1)
    position = (order - starts).astype(jnp.float32)
    frequency = rope_base ** (-2.0 * jnp.arange(head_size // 2, dtype=jnp.float32) / head_size)
    angle = position[..., None] * frequency
    return (jnp.cos(angle), jnp.sin(angle))


VMEM_BYTES = 60 * 1024 * 1024


def dot_nt(a, b):
    return lax.dot_general(a, b, (((1,), (1,)), ((), ())), preferred_element_type=jnp.float32)


def dot_nn(a, b):
    return lax.dot_general(a, b, (((1,), (0,)), ((), ())), preferred_element_type=jnp.float32)


def dot_tn(a, b):
    return lax.dot_general(a, b, (((0,), (0,)), ((), ())), preferred_element_type=jnp.float32)


def flat(shards):
    return [v for pair in shards for side in pair for v in side]


def counts(shards):
    return tuple(tuple(len(side) for side in pair) for pair in shards)


def unflat(refs, shape):
    out, at = [], 0
    for pair in shape:
        sides = []
        for n in pair:
            sides.append(refs[at : at + n])
            at += n
        out.append(sides)
    return out, refs[at:]


def third(side, i, e, ff):
    for ref in side:
        n = ref.shape[1] // ff
        if i < n:
            return ref.at[e, pl.ds(i * ff, ff)]
        i -= n


def block(start, size):
    return pl.ds(pl.multiple_of(start * size, size), size)


def swiglu(gate_pre, up_pre, back, gate):
    sig = 1.0 / (1.0 + jnp.exp(-gate_pre))
    act = gate_pre * sig
    hid = act * up_pre
    scaled = back * gate
    return (
        jnp.sum(hid * back, axis=1, keepdims=True),
        (scaled * up_pre * (sig + act * (1.0 - sig))).astype(jnp.bfloat16),
        (scaled * act).astype(jnp.bfloat16),
        (hid * gate).astype(jnp.bfloat16),
    )


def first_body(cap, ff, rb, nb, src, team, shape, pieces, *rest):
    xr, gr, rest = rest[:src], rest[src : 2 * src], rest[2 * src :]
    shards, rest = unflat(rest, shape)
    rr_ref, gt_ref, rg_ref, h_ref, gate_ref, dgr_ref = rest[:6]
    k = len(pieces)
    sx, kx, ky, sy, rest = rest[6 : 6 + k], rest[6 + k], rest[7 + k], rest[8 + k : 8 + 2 * k], rest[8 + 2 * k :]
    (p, xs, gs, r, g, hb, dp, p_sem, in_sem, rg_sem, h_sem, d_sem) = rest
    n_e, _, _, tok = rr_ref.shape
    rows, width = r.shape[1:]
    half = width // 2

    def load(f, e, slot):
        return [
            pltpu.make_async_copy(
                third(shards[f][j], i, e, ff), p.at[slot, pl.ds(i * ff, ff), pl.ds(j * half, half)], p_sem.at[slot, 3 * j + i]
            )
            for j in range(2)
            for i in range(3)
        ]

    for c in load(0, 0, 0):
        c.start()

    def fetch(k, j, slot):
        return (
            pltpu.make_async_copy(xr[k].at[pl.ds(0, tok)], xs.at[slot, j], in_sem.at[0, slot, j]),
            pltpu.make_async_copy(gr[k].at[pl.ds(0, tok)], gs.at[slot, j], in_sem.at[1, slot, j]),
        )

    def fetch_start(s, slot):
        for k in range(src):

            @pl.when(s == k // team)
            def _():
                for c in fetch(k, k % team, slot):
                    c.start()

    fetch_start(0, 0)

    @pl.loop(0, src // team)
    def _(s):
        slot = lax.rem(s, 2)

        @pl.when(s + 1 < src // team)
        def _():
            fetch_start(s + 1, 1 - slot)

        for j in range(team):
            for c in fetch(j, j, slot):
                c.wait()
        got = [[[], [], []] for _ in range(n_e)]
        for j in range(team):
            hits = [lax.broadcasted_iota(jnp.int32, (cap, tok), 0) == rr_ref[e, s * team + j] for e in range(n_e)]
            one = jnp.concatenate([hit.astype(jnp.float32) for hit in hits], axis=0).astype(jnp.bfloat16)
            rx, rg = dot_nn(one, xs[slot, j]), dot_nn(one, gs[slot, j])
            for e in range(n_e):
                got[e][0].append(rx[e * cap : (e + 1) * cap])
                got[e][1].append(rg[e * cap : (e + 1) * cap])
                got[e][2].append(jnp.sum(jnp.where(hits[e], gt_ref[e, s * team + j], 0.0), axis=1, keepdims=True))
        at = block(s, team * cap)
        for e in range(n_e):
            a, b, c = [v[0] if team == 1 else jnp.concatenate(v, axis=0) for v in got[e]]
            r[e, at, :] = a.astype(jnp.bfloat16)
            g[e, at, :] = b.astype(jnp.bfloat16)
            gate_ref[e, at, :] = c

    keep = []
    for e in range(n_e):
        for i, v in enumerate((r, g)):
            c = pltpu.make_async_copy(v.at[e], rg_ref.at[e, i], rg_sem.at[e, i])
            c.start()
            keep.append(c)
    dgr_ref[...] = jnp.zeros_like(dgr_ref)

    def put_h(f, e, slot):
        return pltpu.make_async_copy(hb.at[slot], h_ref.at[e, :, :, pl.ds(f * ff, ff)], h_sem.at[slot])

    def put_d(f, e, slot):
        kept, j, sent = ((kx, 1, sx), (ky, 0, sy))[f - 1]
        other = dp.at[slot, :, pl.ds(j * half, half)]
        return [pltpu.make_async_copy(other, kept.at[e], d_sem.at[len(pieces), slot])] + [
            pltpu.make_async_copy(
                dp.at[slot, pl.ds(at, n), pl.ds((1 - j) * half, half)], sent[i].at[e], d_sem.at[i, slot]
            )
            for i, (at, n) in enumerate(pieces)
        ]

    for f in range(3):
        for e in range(n_e):
            slot = e % 2
            following = load(f, e + 1, 1 - slot) if e + 1 < n_e else load(f + 1, 0, 1 - slot) if f < 2 else []
            for c in following:
                c.start()
            for c in load(f, e, slot):
                c.wait()
            if f > 0:
                put_h(f - 1, e, slot).wait()

            @pl.loop(0, rows // rb)
            def _(m):
                at = block(m, rb)
                pre = dot_nt(r[e, at, :], p[slot, pl.ds(0, 2 * ff), :])
                back = dot_nt(g[e, at, :], p[slot, pl.ds(2 * ff, ff), :])
                total, a, b, c = swiglu(pre[:, :ff], pre[:, ff:], back, gate_ref[e, at, :])
                dgr_ref[e, at, :] += total
                hb[slot, 0, at, :] = a
                hb[slot, 1, at, :] = b
                hb[slot, 2, at, :] = c

            put_h(f, e, slot).start()
            if f > 0:
                if f > 1:
                    for c in put_d(f - 1, e, slot):
                        c.wait()
                both = jnp.concatenate([hb[slot, 0], hb[slot, 1]], axis=1)

                @pl.loop(0, width // nb)
                def _(n):
                    at = block(n, nb)
                    dp[slot, 0 : 2 * ff, at] = dot_tn(both, r[e, :, at]).astype(jnp.bfloat16)
                    dp[slot, 2 * ff : 3 * ff, at] = dot_tn(hb[slot, 2], g[e, :, at]).astype(jnp.bfloat16)

                for c in put_d(f, e, slot):
                    c.start()
    for e in range(n_e):
        put_h(2, e, e % 2).wait()
        for c in put_d(2, e, e % 2):
            c.wait()
    for c in keep:
        c.wait()


def experts_first(xs, gs, shards, ff, rr, gt, cap, pieces, rb=640, nb=1024):
    n_e, src, _, tok = rr.shape
    width = xs[0].shape[1]
    shape = counts(shards)
    rows = src * cap
    team = 16 // math.gcd(cap, 16)
    bf, f32 = jnp.bfloat16, jnp.float32
    anys, vm = pl.BlockSpec(memory_space=pl.ANY), pl.BlockSpec(memory_space=pltpu.VMEM)
    part = jax.ShapeDtypeStruct((n_e, 3 * ff, width // 2), bf)
    ones = [jax.ShapeDtypeStruct((n_e, n, width // 2), bf) for _, n in pieces]
    outs = pl.pallas_call(
        functools.partial(first_body, cap, ff, rb, nb, src, team, shape, pieces),
        out_shape=(
            jax.ShapeDtypeStruct((n_e, 2, rows, width), bf),
            jax.ShapeDtypeStruct((n_e, 3, rows, 3 * ff), bf),
            jax.ShapeDtypeStruct((n_e, rows, 1), f32),
            jax.ShapeDtypeStruct((n_e, rows, 1), f32),
            *ones, part, part, *ones,
        ),
        in_specs=[anys] * (2 * src + len(flat(shards))) + [vm] * 2,
        out_specs=(anys, anys, vm, vm) + (anys,) * (2 + 2 * len(pieces)),
        scratch_shapes=[
            pltpu.VMEM((2, 3 * ff, width), bf),
            pltpu.VMEM((2, team, tok, width), bf),
            pltpu.VMEM((2, team, tok, width), bf),
            pltpu.VMEM((n_e, rows, width), bf),
            pltpu.VMEM((n_e, rows, width), bf),
            pltpu.VMEM((2, 3, rows, ff), bf),
            pltpu.VMEM((2, 3 * ff, width), bf),
            pltpu.SemaphoreType.DMA((2, 6)),
            pltpu.SemaphoreType.DMA((2, 2, team)),
            pltpu.SemaphoreType.DMA((n_e, 2)),
            pltpu.SemaphoreType.DMA((2,)),
            pltpu.SemaphoreType.DMA((len(pieces) + 1, 2)),
        ],
        compiler_params=pltpu.CompilerParams(vmem_limit_bytes=VMEM_BYTES),
    )(*xs, *gs, *flat(shards), rr, gt)
    k = len(pieces)
    return *outs[:4], outs[4 : 4 + k], outs[4 + k], outs[5 + k], outs[6 + k :]


def tile_width(src):
    return 512 if src <= 8 else 128


def plan_body(n_prob, top, number_ref, *rest):
    src = (len(rest) - 9) // 2
    xr, gr, rest = rest[:src], rest[src : 2 * src], rest[2 * src :]
    row_ref, col_ref, gate_ref, mx, gx, probs, sems, gate_sem, rank = rest
    n_e, _, _, tok = row_ref.shape
    width = mx.shape[2]
    copies = []
    for s in range(src):
        copies.append(pltpu.make_async_copy(xr[s].at[pl.ds(tok, mx.shape[1])], mx.at[s], sems.at[s]))
        copies.append(pltpu.make_async_copy(gr[s].at[pl.ds(tok, gx.shape[1])], gx.at[s], gate_sem.at[s]))
    for c in copies:
        c.start()
    for c in copies:
        c.wait()
    for s in range(src):
        line = gx[s].astype(jnp.float32)
        both = mx[s].astype(jnp.float32)
        probs[s] = both[0:n_prob] + both[n_prob : 2 * n_prob]
        for e in range(n_e):
            number = number_ref[0] + e
            hit = None
            for k in range(top):
                at = k * tok
                same = line[at // width : at // width + 1, at % width : at % width + tok] == number.astype(jnp.float32)
                hit = same if hit is None else hit | same
            rank[e * src + s : e * src + s + 1, :] = hit.astype(jnp.float32)
            at = number * tok
            gate_ref[e, s] = probs[s, pl.ds(at // width, 1), pl.ds(pl.multiple_of(lax.rem(at, width), tok), tok)]
    lower = lax.broadcasted_iota(jnp.int32, (tok, tok), 0) <= lax.broadcasted_iota(jnp.int32, (tok, tok), 1)
    hits = rank[...]
    places = dot_nn(hits.astype(jnp.bfloat16), lower.astype(jnp.float32).astype(jnp.bfloat16))
    places = jnp.where(hits > 0.0, places - 1.0, -1.0)
    col_ref[...] = places.T.astype(jnp.int32)
    for e in range(n_e):
        for s in range(src):
            i = e * src + s
            row_ref[e, s] = places[i : i + 1].astype(jnp.int32)


def plan(number, xs, gs, n_prob, top, n_e, tok):
    src, width = len(xs), xs[0].shape[1]
    anys, vm = pl.BlockSpec(memory_space=pl.ANY), pl.BlockSpec(memory_space=pltpu.VMEM)
    bf, f32 = jnp.bfloat16, jnp.float32
    return pl.pallas_call(
        functools.partial(plan_body, n_prob, top),
        out_shape=(
            jax.ShapeDtypeStruct((n_e, src, 1, tok), jnp.int32),
            jax.ShapeDtypeStruct((tok, n_e * src), jnp.int32),
            jax.ShapeDtypeStruct((n_e, src, 1, tok), f32),
        ),
        in_specs=[pl.BlockSpec(memory_space=pltpu.SMEM)] + [anys] * (2 * src),
        out_specs=(vm, vm, vm),
        scratch_shapes=[
            pltpu.VMEM((src, xs[0].shape[0] - tok, width), bf),
            pltpu.VMEM((src, gs[0].shape[0] - tok, width), bf),
            pltpu.VMEM((src, n_prob, width), f32),
            pltpu.SemaphoreType.DMA((src,)),
            pltpu.SemaphoreType.DMA((src,)),
            pltpu.VMEM((n_e * src, tok), f32),
        ],
        compiler_params=pltpu.CompilerParams(vmem_limit_bytes=VMEM_BYTES),
    )(number, *xs, *gs)


def last_body(ff, rb, nb, shape, pieces, rg_ref, gate_ref, dgr_in, *rest):
    (side,), rest = unflat(rest, shape)
    k = len(pieces)
    hd_ref, dgr_ref, low, high, rest = rest[0], rest[1], rest[2 : 2 + k], rest[2 + k : 2 + 2 * k], rest[2 + 2 * k :]
    p, r, g, hb, ht, dp, p_sem, rg_sem, h_sem, d_sem = rest
    n_e, rows, width = r.shape
    half = width // 2
    weights, loads = [], []
    for e in range(n_e):
        weights.append([
            pltpu.make_async_copy(
                third(side[j], i, e, ff), p.at[e, pl.ds(i * ff, ff), pl.ds(j * half, half)], p_sem.at[e, 3 * j + i])
            for j in range(2) for i in range(3)
        ])
        loads.append([[
            pltpu.make_async_copy(rg_ref.at[e, i, pl.ds(m * rb, rb)], v.at[e, pl.ds(m * rb, rb)], rg_sem.at[e, i, m])
            for i, v in enumerate((r, g))] for m in range(rows // rb)])
    def begin(e):
        for c in weights[e] + [c for m in loads[e] for c in m]:
            c.start()

    begin(0)
    outs = []
    for e in range(n_e):
        for c in weights[e]:
            c.wait()
        if e + 1 < n_e:
            begin(e + 1)
        for m in range(rows // rb):
            for c in loads[e][m]:
                c.wait()
            at = pl.ds(m * rb, rb)
            pre = dot_nt(r[e, at, :], p[e, pl.ds(0, 2 * ff), :])
            back = dot_nt(g[e, at, :], p[e, pl.ds(2 * ff, ff), :])
            total, a, b, c = swiglu(pre[:, :ff], pre[:, ff:], back, gate_ref[e, at, :])
            dgr_ref[e, at, :] = dgr_in[e, at, :] + total
            hb[e, 0, at, :] = a
            hb[e, 1, at, :] = b
            hb[e, 2, at, :] = c
        c = pltpu.make_async_copy(hb.at[e], hd_ref.at[e], h_sem.at[e])
        c.start()
        outs.append(c)
        for i in range(3):
            ht[pl.ds(i * ff, ff), :] = hb[e, i].T

        @pl.loop(0, width // nb)
        def _(n):
            at = block(n, nb)
            dp[e, 0 : 2 * ff, at] = dot_nn(ht[0 : 2 * ff, :], r[e, :, at]).astype(jnp.bfloat16)
            dp[e, 2 * ff : 3 * ff, at] = dot_nn(ht[2 * ff : 3 * ff, :], g[e, :, at]).astype(jnp.bfloat16)

        for j, refs in enumerate((low, high)):
            for i, (at, n) in enumerate(pieces):
                c = pltpu.make_async_copy(
                    dp.at[e, pl.ds(at, n), pl.ds(j * half, half)], refs[i].at[e], d_sem.at[e, len(pieces) * j + i]
                )
                c.start()
                outs.append(c)
    for c in outs:
        c.wait()


def experts_last(rg, gate, dgr, side, ff, pieces, rb=640, nb=1024):
    n_e, _, rows, width = rg.shape
    shape = counts((side,))
    bf, f32 = jnp.bfloat16, jnp.float32
    anys, vm = pl.BlockSpec(memory_space=pl.ANY), pl.BlockSpec(memory_space=pltpu.VMEM)
    parts = [jax.ShapeDtypeStruct((n_e, n, width // 2), bf) for _, n in pieces]
    outs = pl.pallas_call(
        functools.partial(last_body, ff, rb, nb, shape, pieces),
        out_shape=(
            jax.ShapeDtypeStruct((n_e, 3, rows, ff), bf),
            jax.ShapeDtypeStruct((n_e, rows, 1), f32),
            *parts, *parts,
        ),
        in_specs=[anys] + [vm] * 2 + [anys] * len(flat((side,))),
        out_specs=(anys, vm) + (anys,) * (2 * len(pieces)),
        scratch_shapes=[
            pltpu.VMEM((n_e, 3 * ff, width), bf),
            pltpu.VMEM((n_e, rows, width), bf),
            pltpu.VMEM((n_e, rows, width), bf),
            pltpu.VMEM((n_e, 3, rows, ff), bf),
            pltpu.VMEM((3 * ff, rows), bf),
            pltpu.VMEM((n_e, 3 * ff, width), bf),
            pltpu.SemaphoreType.DMA((n_e, 6)),
            pltpu.SemaphoreType.DMA((n_e, 2, rows // rb)),
            pltpu.SemaphoreType.DMA((n_e,)),
            pltpu.SemaphoreType.DMA((n_e, 2 * len(pieces))),
        ],
        compiler_params=pltpu.CompilerParams(vmem_limit_bytes=VMEM_BYTES),
    )(rg, gate, dgr, *flat((side,)))
    k = len(pieces)
    return outs[0], outs[1], outs[2 : 2 + k], outs[2 + k :]


def spread_body(cap, ff, nb, shape, kinds, zs, extra, number_ref, ha_ref, hd_ref, dgr, *rest):
    shards, rest = unflat(rest, shape)
    rr_ref, cols_ref, own_ref, sib_ref, p, h, dg, acc, stage, p_sem, h_sem, st_sem = rest
    n_e = ha_ref.shape[0]
    width = p.shape[2]
    half = width // 2
    hidden = 4 * ff
    src, tok, tall = rr_ref.shape[1], rr_ref.shape[3], stage.shape[3]
    tiles = width // nb
    loads = []
    for e in range(n_e):
        copies = []
        loads.append(copies)
        for i, kind in enumerate(kinds):
            for q in range(4):
                for j in range(2):
                    copies.append(pltpu.make_async_copy(
                        third(shards[q][j], kind, e, ff),
                        p.at[e, pl.ds(i * hidden + q * ff, ff), pl.ds(j * half, half)], p_sem.at[e, i, 2 * q + j]))
            for m, z in enumerate(zs):
                at, to = pl.ds(2 * z * cap, 2 * cap), pl.ds(2 * m * cap, 2 * cap)
                copies.append(pltpu.make_async_copy(
                    ha_ref.at[e, kind, at], h.at[e, to, pl.ds(i * hidden, 3 * ff)], h_sem.at[e, i, m, 0]))
                copies.append(pltpu.make_async_copy(
                    hd_ref.at[e, kind, at], h.at[e, to, pl.ds(i * hidden + 3 * ff, ff)], h_sem.at[e, i, m, 1]))
    for copies in loads:
        for c in copies:
            c.start()
    if extra:
        for e in range(n_e):
            for m, z in enumerate(zs):
                for w in range(2):
                    s = 2 * z + w
                    hit = lax.broadcasted_iota(jnp.int32, (cap, tok), 0) == rr_ref[e, s]
                    dg[e, 2 * m + w] = jnp.sum(
                        jnp.where(hit, dgr[e, pl.ds(s * cap, cap), :], 0.0), axis=0, keepdims=True)

    def extras(n, s):
        shape = (tall - tok, nb)
        line = lax.broadcasted_iota(jnp.int32, shape, 0)
        place = n * nb + lax.broadcasted_iota(jnp.int32, shape, 1)
        total = jnp.zeros(shape, jnp.float32)
        for e in range(n_e):
            v = dg[e, s]
            if nb >= tok:
                v = jnp.concatenate([v] * (nb // tok), axis=1)
            else:
                v = jnp.where(lax.rem(n, 2) == 0, v[:, :nb], v[:, nb:])
            at = (number_ref[0] + e) * tok
            inside = (place >= lax.rem(at, width)) & (place < lax.rem(at, width) + tok)
            low = v.astype(jnp.bfloat16).astype(jnp.float32)
            row = at // width
            total = jnp.where(inside & (line == row), low, total)
            total = jnp.where(inside & (line == row + extra), v - low, total)
        return total.astype(jnp.bfloat16)

    def put(n, slot):
        return [
            pltpu.make_async_copy(stage.at[slot, w], ref.at[:, :, block(n, nb)], st_sem.at[slot, w])
            for w, ref in enumerate((own_ref, sib_ref))
        ]

    def column(e, s):
        i = e * src + s
        if isinstance(s, int):
            return cols_ref[:, i : i + 1]
        lane = lax.broadcasted_iota(jnp.int32, cols_ref.shape, 1)
        return jnp.sum(jnp.where(lane == i, cols_ref[...], 0), axis=1, keepdims=True)

    @pl.loop(0, tiles)
    def _(n):
        slot = lax.rem(n, 2)
        for e in range(n_e):

            @pl.when(n == 0)
            def _():
                for c in loads[e]:
                    c.wait()

            acc[e] = dot_nn(h[e], p[e, :, block(n, nb)])

        @pl.when(n >= 2)
        def _():
            for c in put(n, slot):
                c.wait()

        def one(m, z, w):
            hits = [
                (lax.broadcasted_iota(jnp.int32, (tok, cap), 1) == column(e, 2 * z + w)).astype(jnp.float32)
                for e in range(n_e)
            ]
            hit = jnp.concatenate(hits, axis=1).astype(jnp.bfloat16)
            s = 2 * m + w
            part = jnp.concatenate([acc[e, block(s, cap)] for e in range(n_e)], axis=0).astype(jnp.bfloat16)
            stage[slot, w, m, 0:tok, :] = dot_nn(hit, part).astype(jnp.bfloat16)
            if extra:
                stage[slot, w, m, tok:tall, :] = extras(n, s)

        if len(zs) <= 4:
            for m, z in enumerate(zs):
                for w in range(2):
                    one(m, z, w)
        else:

            @pl.loop(0, len(zs))
            def _(m):
                z = lax.rem(m + zs[0], src // 2)
                for w in range(2):
                    one(m, z, w)

        for c in put(n, slot):
            c.start()

    for slot in range(2):
        for c in put(slot, slot):
            c.wait()


def experts_spread(number, ha, hd, dgr, shards, ff, width, rr, cols, cap, kinds, zs, gates):
    n_e, src, _, tok = rr.shape
    nb = tile_width(src)
    extra = n_e * src * tok // width if gates else 0
    tall = tok + 2 * extra + -2 * extra % 16
    shape = counts(shards)
    rows = 2 * len(zs) * cap
    bf, f32 = jnp.bfloat16, jnp.float32
    anys, vm = pl.BlockSpec(memory_space=pl.ANY), pl.BlockSpec(memory_space=pltpu.VMEM)
    side = jax.ShapeDtypeStruct((len(zs), tall, width), bf)
    return pl.pallas_call(
        functools.partial(spread_body, cap, ff, nb, shape, kinds, zs, extra),
        out_shape=(side, side),
        in_specs=[pl.BlockSpec(memory_space=pltpu.SMEM), anys, anys, vm] + [anys] * len(flat(shards)) + [vm, vm],
        out_specs=(anys, anys),
        scratch_shapes=[
            pltpu.VMEM((n_e, 4 * ff * len(kinds), width), bf),
            pltpu.VMEM((n_e, rows, 4 * ff * len(kinds)), bf),
            pltpu.VMEM((n_e, 2 * len(zs), 1, tok), f32),
            pltpu.VMEM((n_e, rows, nb), f32),
            pltpu.VMEM((2, 2, len(zs), tall, nb), bf),
            pltpu.SemaphoreType.DMA((n_e, len(kinds), 8)),
            pltpu.SemaphoreType.DMA((n_e, len(kinds), len(zs), 2)),
            pltpu.SemaphoreType.DMA((2, 2)),
        ],
        compiler_params=pltpu.CompilerParams(vmem_limit_bytes=VMEM_BYTES),
    )(number, ha, hd, dgr, *flat(shards), rr, cols)


def grads_body(ff, h_ref, rg_ref, low, high, ht):
    part = pl.program_id(1)

    @pl.when(part == 0)
    def _():
        for i in range(3):
            ht[pl.ds(i * ff, ff), :] = h_ref[0, i].T

    def out(ref):
        ref[0, 0 : 2 * ff, :] = dot_nn(ht[0 : 2 * ff, :], rg_ref[0, 0]).astype(jnp.bfloat16)
        ref[0, 2 * ff : 3 * ff, :] = dot_nn(ht[2 * ff : 3 * ff, :], rg_ref[0, 1]).astype(jnp.bfloat16)

    @pl.when(part == 0)
    def _():
        out(low)

    @pl.when(part == 1)
    def _():
        out(high)


def expert_grads(h, rg, ff):
    n_e, _, rows, _ = h.shape
    half = rg.shape[3] // 2
    side = jax.ShapeDtypeStruct((n_e, 3 * ff, half), jnp.bfloat16)
    return pl.pallas_call(
        functools.partial(grads_body, ff),
        out_shape=(side, side),
        grid=(n_e, 2),
        in_specs=[
            pl.BlockSpec((1, 3, rows, ff), lambda e, j: (e, 0, 0, 0)),
            pl.BlockSpec((1, 2, rows, half), lambda e, j: (e, 0, 0, j)),
        ],
        out_specs=(pl.BlockSpec((1, 3 * ff, half), lambda e, j: (e, 0, 0)),) * 2,
        scratch_shapes=[pltpu.VMEM((3 * ff, rows), jnp.bfloat16)],
        compiler_params=pltpu.CompilerParams(vmem_limit_bytes=VMEM_BYTES),
    )(h, rg)


def blank(*shape):
    return pl.pallas_call(
        lambda ref: None,
        out_shape=jax.ShapeDtypeStruct(shape, jnp.bfloat16),
        out_specs=pl.BlockSpec(memory_space=pl.ANY),
    )()


def kernel_params():
    return pltpu.CompilerParams(vmem_limit_bytes=VMEM_BYTES)


def row_scale(squares, width):
    return lax.rsqrt(squares / width + epsilon)


def project_body(first, *refs):
    if first:
        x_ref, gain_ref, w_ref, normed_ref, raw_ref, qs_ref, ks_ref = refs
    else:
        normed_ref, w_ref, qs_in, ks_in, _, raw_ref, qs_ref, ks_ref = refs
    n = pl.program_id(0)

    @pl.when(n == 0)
    def _():
        if first:
            x = x_ref[...].astype(jnp.float32)
            scale = row_scale(jnp.sum(x * x, axis=1, keepdims=True), x.shape[1])
            normed_ref[...] = (x * scale * gain_ref[...]).astype(jnp.bfloat16)
            qs_ref[...] = jnp.zeros_like(qs_ref)
            ks_ref[...] = jnp.zeros_like(ks_ref)
        else:
            qs_ref[...] = qs_in[...]
            ks_ref[...] = ks_in[...]

    raw = dot_nn(normed_ref[...], w_ref[...])
    raw_ref[...] = raw
    squares = jnp.sum(raw * raw, axis=1, keepdims=True)
    qs_ref[...] += jnp.where(n == 0, squares, 0.0)
    ks_ref[...] += jnp.where(n == 1, squares, 0.0)


def project(x, gain, weights):
    tokens, width = x.shape
    half = width // 2
    f32 = jnp.float32
    sums = jax.ShapeDtypeStruct((tokens, 1), f32)

    def whole(*shape):
        return pl.BlockSpec(shape, lambda n: (0, 0))

    return pl.pallas_call(
        functools.partial(project_body, True),
        out_shape=(
            jax.ShapeDtypeStruct((tokens, width), jnp.bfloat16),
            jax.ShapeDtypeStruct((tokens, 6 * half), f32),
            sums,
            sums,
        ),
        grid=(3,),
        in_specs=[whole(tokens, width), whole(1, width), pl.BlockSpec((width, half), lambda n: (0, n))],
        out_specs=(whole(tokens, width), pl.BlockSpec((tokens, half), lambda n: (0, n)), whole(tokens, 1), whole(tokens, 1)),
        compiler_params=kernel_params(),
    )(x, gain[None], weights)


def project_other(normed, weights, qs, ks, raw):
    tokens, width = normed.shape
    half = width // 2
    f32 = jnp.float32
    sums = jax.ShapeDtypeStruct((tokens, 1), f32)

    def whole(*shape):
        return pl.BlockSpec(shape, lambda n: (0, 0))

    return pl.pallas_call(
        functools.partial(project_body, False),
        out_shape=(jax.ShapeDtypeStruct((tokens, 6 * half), f32), sums, sums),
        grid=(3,),
        in_specs=[whole(tokens, width), pl.BlockSpec((width, half), lambda n: (0, n)), whole(tokens, 1), whole(tokens, 1),
                  pl.BlockSpec(memory_space=pl.ANY)],
        out_specs=(pl.BlockSpec((tokens, half), lambda n: (0, 3 + n)), whole(tokens, 1), whole(tokens, 1)),
        input_output_aliases={4: 0},
        compiler_params=kernel_params(),
    )(normed, weights, qs, ks, raw)


def turned(v, cosine, sine):
    return v * cosine + pltpu.roll(v, v.shape[1] // 2, 1) * sine


def masked_chances(q, k, allowed, scale):
    scores = jnp.where(allowed, dot_nt(q, k) * scale, masked_score)
    grown = jnp.exp(scores - jnp.max(scores, axis=1, keepdims=True))
    return grown / jnp.sum(grown, axis=1, keepdims=True)


def allowed_pairs(row_ref, col_ref):
    n = row_ref.shape[1]
    rows = lax.broadcasted_iota(jnp.int32, (n, n), 0)
    cols = lax.broadcasted_iota(jnp.int32, (n, n), 1)
    return (row_ref[...] == col_ref[...]) & (rows >= cols)


def attend_body(width, q_ref, k_ref, v_ref, qs, ks, qg, kg, cos, sin, doc_row, doc_col, q_out, k_out, v_out, c_out):
    allowed = allowed_pairs(doc_row, doc_col)
    q_scale, k_scale = row_scale(qs[...], width), row_scale(ks[...], width)
    for i in range(q_ref.shape[1] // HD):
        at = slice(i * HD, (i + 1) * HD)
        q = turned(q_ref[:, at] * q_scale * qg[:, at], cos[...], sin[...]).astype(jnp.bfloat16)
        k = turned(k_ref[:, at] * k_scale * kg[:, at], cos[...], sin[...]).astype(jnp.bfloat16)
        v = v_ref[:, at].astype(jnp.bfloat16)
        q_out[:, at] = q
        k_out[:, at] = k
        v_out[:, at] = v
        chances = masked_chances(q, k, allowed, HD ** (-0.5)).astype(jnp.bfloat16)
        c_out[:, at] = dot_nn(chances, v).astype(jnp.bfloat16)


def attend(raw, qs, ks, qg, kg, cos, sin, document):
    tokens, width = raw.shape[0], raw.shape[1] // 3
    nb = width // 4

    def part(i):
        return pl.BlockSpec((tokens, nb), lambda h: (0, 6 * (h // 2) + 2 * i + h % 2))

    head = pl.BlockSpec((tokens, nb), lambda h: (0, h))
    gain = pl.BlockSpec((1, nb), lambda h: (0, h))

    def whole(*shape):
        return pl.BlockSpec(shape, lambda h: (0, 0))

    out = jax.ShapeDtypeStruct((tokens, width), jnp.bfloat16)
    return pl.pallas_call(
        functools.partial(attend_body, width),
        out_shape=(out,) * 4,
        grid=(4,),
        in_specs=[part(0), part(1), part(2), whole(tokens, 1), whole(tokens, 1), gain, gain]
        + [whole(tokens, HD), whole(tokens, HD), whole(1, tokens), whole(tokens, 1)],
        out_specs=(head,) * 4,
        compiler_params=kernel_params(),
    )(raw, raw, raw, qs, ks, qg[None], kg[None], cos, sin, document[None], document[:, None])


def lines(v, width):
    n, k = v.shape
    per = width // k
    return jnp.concatenate(
        [jnp.concatenate([v[i + j : i + j + 1] for j in range(per)], axis=1) for i in range(0, n, per)], axis=0
    )


def unlines(v, k):
    return jnp.concatenate([v[i : i + 1, j : j + k] for i in range(v.shape[0]) for j in range(0, v.shape[1], k)], axis=0)


def middle_body(core_ref, ctx_ref, wm_ref, wo_ref, x_ref, gain_ref, router_ref, middle_ref, piece_ref, probs_ref):
    w, j = pl.program_id(0), pl.program_id(1)
    tokens, width = x_ref.shape
    half = width // 2

    def out(ref, side):
        at = pl.ds(pl.multiple_of(side * half, half), half)
        part = dot_nn(ctx_ref[...], ref[...])

        @pl.when(j == 0)
        def _():
            middle_ref[:, at] = x_ref[:, at].astype(jnp.float32) + part

        @pl.when(j == 1)
        def _():
            middle_ref[:, at] += part

    @pl.when(w == 0)
    def _():
        out(wm_ref, core_ref[0])

    @pl.when(w == 1)
    def _():
        out(wo_ref, 1 - core_ref[0])

    @pl.when((w == 1) & (j == 1))
    def _():
        middle = middle_ref[...]
        scale = row_scale(jnp.sum(middle * middle, axis=1, keepdims=True), width)
        mixed = (middle * scale * gain_ref[...]).astype(jnp.bfloat16)
        piece_ref[0:tokens, :] = mixed
        logits = dot_nt(router_ref[...], mixed)
        grown = jnp.exp(logits - jnp.max(logits, axis=0, keepdims=True))
        probs = grown / jnp.sum(grown, axis=0, keepdims=True)
        probs_ref[...] = probs
        high = probs.astype(jnp.bfloat16).astype(jnp.float32)
        rows = [lines(high, width), lines(probs - high, width)]
        n = piece_ref.shape[0] - tokens - 2 * rows[0].shape[0]
        if n:
            rows.append(jnp.zeros((n, width), jnp.float32))
        piece_ref[tokens : piece_ref.shape[0], :] = jnp.concatenate(rows, axis=0).astype(jnp.bfloat16)


def half_specs(half):
    return [
        pl.BlockSpec((half, half), lambda w, j, core: (jnp.where(w == 0, core[0] ^ j, 1 - core[0]), 3)),
        pl.BlockSpec((half, half), lambda w, j, core: (jnp.where(w == 0, core[0], core[0] ^ j), 3)),
    ]


def middle_of(core, context, weights, weights_other, x, gain, router_t):
    tokens, width = x.shape
    half = width // 2
    experts = router_t.shape[0]
    extra = 2 * experts * tokens // width
    tall = tokens + extra + -extra % 16

    def whole(*shape):
        return pl.BlockSpec(shape, lambda w, j, core: (0, 0))

    return pl.pallas_call(
        middle_body,
        out_shape=(
            jax.ShapeDtypeStruct((tokens, width), jnp.float32),
            jax.ShapeDtypeStruct((tall, width), jnp.bfloat16),
            jax.ShapeDtypeStruct((experts, tokens), jnp.float32),
        ),
        grid_spec=pltpu.PrefetchScalarGridSpec(
            num_scalar_prefetch=1,
            grid=(2, 2),
            in_specs=[pl.BlockSpec((tokens, half), lambda w, j, core: (0, j))]
            + half_specs(half)
            + [whole(tokens, width), whole(1, width), whole(experts, width)],
            out_specs=(whole(tokens, width), whole(tall, width), whole(experts, tokens)),
        ),
        compiler_params=kernel_params(),
    )(core, context, weights, weights_other, x, gain[None], router_t)


def middle_back_body(core_ref, sum_ref, middle_ref, cot_ref, gain_ref, probs_ref, router_ref, wm_ref, wo_ref,
                     grad_ref, mine_ref, other_ref, up_ref, gain_out, router_out, logit_ref, branch, acc):
    j, w = pl.program_id(0), pl.program_id(1)
    tokens, width = middle_ref.shape
    half = width // 2

    @pl.when((j == 0) & (w == 0))
    def _():
        middle = middle_ref[...]
        scale = row_scale(jnp.sum(middle * middle, axis=1, keepdims=True), width)
        unit = middle * scale
        probs = probs_ref[...]
        n = probs.shape[0] * tokens // width
        total = sum_ref[tokens : tokens + n, :] + sum_ref[tokens + n : tokens + 2 * n, :]
        raised = unlines(total, tokens)
        logit = (probs * (raised - jnp.sum(probs * raised, axis=0, keepdims=True))).astype(jnp.bfloat16)
        logit_ref[...] = logit
        mixed_up = sum_ref[0:tokens, :] + dot_tn(logit, router_ref[...])
        gain_out[...] = jnp.sum(mixed_up * unit, axis=0, keepdims=True)
        router_out[...] = dot_nn(logit, (unit * gain_ref[...]).astype(jnp.bfloat16))
        raised = mixed_up * gain_ref[...]
        mean = jnp.sum(raised * unit, axis=1, keepdims=True) / width
        grad = cot_ref[...].astype(jnp.float32) + scale * (raised - unit * mean)
        grad_ref[...] = grad
        branch[...] = grad.astype(jnp.bfloat16)
        mine_ref[...] = branch[:, pl.ds(pl.multiple_of(core_ref[0] * half, half), half)]
        other_ref[...] = branch[:, pl.ds(pl.multiple_of((1 - core_ref[0]) * half, half), half)]

    @pl.when(w == 0)
    def _():
        acc[...] = dot_nt(mine_ref[...], wm_ref[...])

    @pl.when(w == 1)
    def _():
        up_ref[...] = (acc[...] + dot_nt(other_ref[...], wo_ref[...])).astype(jnp.bfloat16)


def middle_back(core, total, middle, cotangent, gain, probs, router_t, weights, weights_other):
    tokens, width = middle.shape
    half = width // 2
    experts = probs.shape[0]
    bf, f32 = jnp.bfloat16, jnp.float32

    def whole(*shape):
        return pl.BlockSpec(shape, lambda j, w, core: (0, 0))

    specs = [
        pl.BlockSpec((half, half), lambda j, w, core: (core[0] ^ j, 3)),
        pl.BlockSpec((half, half), lambda j, w, core: (core[0] ^ j, 3)),
    ]
    return pl.pallas_call(
        middle_back_body,
        out_shape=(
            jax.ShapeDtypeStruct((tokens, width), f32),
            jax.ShapeDtypeStruct((tokens, half), bf),
            jax.ShapeDtypeStruct((tokens, half), bf),
            jax.ShapeDtypeStruct((tokens, width), bf),
            jax.ShapeDtypeStruct((1, width), f32),
            jax.ShapeDtypeStruct((experts, width), f32),
            jax.ShapeDtypeStruct((experts, tokens), bf),
        ),
        grid_spec=pltpu.PrefetchScalarGridSpec(
            num_scalar_prefetch=1,
            grid=(2, 2),
            in_specs=[whole(*total.shape), whole(tokens, width), whole(tokens, width), whole(1, width),
                      whole(experts, tokens), whole(experts, width)] + specs,
            out_specs=(
                whole(tokens, width), whole(tokens, half), whole(tokens, half),
                pl.BlockSpec((tokens, half), lambda j, w, core: (0, j)),
                whole(1, width), whole(experts, width), whole(experts, tokens),
            ),
            scratch_shapes=[pltpu.VMEM((tokens, width), bf), pltpu.VMEM((tokens, half), f32)],
        ),
        compiler_params=kernel_params(),
    )(core, total, middle, cotangent, gain[None], probs, router_t, weights, weights_other)


def attend_back_body(width, q_ref, k_ref, v_ref, u_ref, q_raw, k_raw, qs, ks, qg, kg, cos, sin, doc_row, doc_col,
                     ups, qg_out, kg_out, q_back, k_back, v_back, q_mean, k_mean):
    phase, h = pl.program_id(0), pl.program_id(1)
    nb = q_ref.shape[1]
    q_scale, k_scale = row_scale(qs[...], width), row_scale(ks[...], width)
    cols = pl.ds(pl.multiple_of(h * nb, nb), nb)

    @pl.when((phase == 0) & (h == 0))
    def _():
        q_mean[...] = jnp.zeros_like(q_mean)
        k_mean[...] = jnp.zeros_like(k_mean)

    @pl.when(phase == 0)
    def _():
        allowed = allowed_pairs(doc_row, doc_col)
        dq, dk, dv = [], [], []
        for i in range(nb // HD):
            at = slice(i * HD, (i + 1) * HD)
            q, k, u = q_ref[:, at], k_ref[:, at], u_ref[:, at]
            chances = masked_chances(q, k, allowed, HD ** (-0.5))
            raised = dot_nt(u, v_ref[:, at])
            dv.append(dot_tn(chances.astype(jnp.bfloat16), u).astype(jnp.bfloat16))
            back = chances * (raised - jnp.sum(chances * raised, axis=1, keepdims=True))
            back = back.astype(jnp.bfloat16)
            dq.append(turned(dot_nn(back, k) * HD ** (-0.5), cos[...], -sin[...]))
            dk.append(turned(dot_tn(back, q) * HD ** (-0.5), cos[...], -sin[...]))
        for parts, raw, scale, gain, mean, kept, out in (
            (dq, q_raw, q_scale, qg, q_mean, q_back, qg_out),
            (dk, k_raw, k_scale, kg, k_mean, k_back, kg_out),
        ):
            back = jnp.concatenate(parts, axis=1)
            kept[h] = back
            grown = back * (raw[...] * scale)
            out[0:1, cols] = jnp.sum(grown, axis=0, keepdims=True)
            mean[...] += jnp.sum(grown * gain[...], axis=1, keepdims=True)
        v_back[h] = jnp.concatenate(dv, axis=1)

    @pl.when(phase == 1)
    def _():
        for i, (raw, scale, gain, mean, kept) in enumerate(
            ((q_raw, q_scale, qg, q_mean, q_back), (k_raw, k_scale, kg, k_mean, k_back))
        ):
            up = scale * (kept[h] * gain[...] - raw[...] * scale * (mean[...] / width))
            ups[0, i] = up.astype(jnp.bfloat16)
        ups[0, 2] = v_back[h]


def attend_back(q, k, v, up, raw, qs, ks, qg, kg, cos, sin, document):
    tokens, width = v.shape
    nb = width // 4
    f32 = jnp.float32

    def part(i):
        return pl.BlockSpec((tokens, nb), lambda p, h: (0, 6 * (h // 2) + 2 * i + h % 2))

    head = pl.BlockSpec((tokens, nb), lambda p, h: (0, jnp.where(p == 0, h, 3)))
    gain = pl.BlockSpec((1, nb), lambda p, h: (0, h))

    def whole(*shape):
        return pl.BlockSpec(shape, lambda p, h: (0, 0))

    def out_place(p, h):
        at = jnp.where(p == 0, 0, h)
        return (at // 2, 0, 0, at % 2)

    return pl.pallas_call(
        functools.partial(attend_back_body, width),
        out_shape=(
            jax.ShapeDtypeStruct((2, 3, tokens, width // 2), jnp.bfloat16),
            jax.ShapeDtypeStruct((1, width), f32),
            jax.ShapeDtypeStruct((1, width), f32),
        ),
        grid=(2, 4),
        in_specs=[head, head, head, head, part(0), part(1), whole(tokens, 1), whole(tokens, 1), gain, gain]
        + [whole(tokens, HD), whole(tokens, HD), whole(1, tokens), whole(tokens, 1)],
        out_specs=(pl.BlockSpec((1, 3, tokens, nb), out_place), whole(1, width), whole(1, width)),
        scratch_shapes=[
            pltpu.VMEM((4, tokens, nb), f32),
            pltpu.VMEM((4, tokens, nb), f32),
            pltpu.VMEM((4, tokens, nb), jnp.bfloat16),
            pltpu.VMEM((tokens, 1), f32),
            pltpu.VMEM((tokens, 1), f32),
        ],
        compiler_params=kernel_params(),
    )(q, k, v, up, raw, raw, qs, ks, qg[None], kg[None], cos, sin, document[None], document[:, None])


def qkv_grad_body(n_ref, no_ref, u_ref, uo_ref, first, second, pair):
    i = pl.program_id(0)
    tokens = n_ref.shape[0]

    @pl.when(i == 0)
    def _():
        pair[:, 0:tokens] = n_ref[...].T
        pair[:, tokens : 2 * tokens] = no_ref[...].T

    ups = jnp.concatenate([u_ref[0, 0], uo_ref[0]], axis=0)
    got = dot_nn(pair[...], ups).astype(jnp.bfloat16)

    @pl.when(i < 3)
    def _():
        first[...] = got

    @pl.when(i >= 3)
    def _():
        second[...] = got


def qkv_grad(normed, normed_other, ups, got):
    tokens, width = normed.shape
    nb = width // 4
    out = jax.ShapeDtypeStruct((width, 3 * nb), jnp.bfloat16)

    def whole(*shape):
        return pl.BlockSpec(shape, lambda i: (0, 0))

    return pl.pallas_call(
        qkv_grad_body,
        out_shape=(out, out),
        grid=(6,),
        in_specs=[
            whole(tokens, width),
            whole(tokens, width),
            pl.BlockSpec((1, 1, tokens, nb), lambda i: (0, i // 2, 0, i % 2)),
            pl.BlockSpec((1, tokens, nb), lambda i: (i // 2, 0, i % 2)),
        ],
        out_specs=(
            pl.BlockSpec((width, nb), lambda i: (0, jnp.minimum(i, 2))),
            pl.BlockSpec((width, nb), lambda i: (0, jnp.maximum(i - 3, 0))),
        ),
        scratch_shapes=[pltpu.VMEM((width, 2 * tokens), jnp.bfloat16)],
        compiler_params=kernel_params(),
    )(normed, normed_other, ups, got)


def input_grad_body(ups_ref, wm_ref, wo_ref, x_ref, grad_ref, gain_ref, out_ref, gain_out, total, turned_ups):
    n = pl.program_id(0)
    tokens, width = x_ref.shape
    half = width // 2
    nb = wm_ref.shape[0]

    @pl.when(n == 0)
    def _():
        for w in range(2):
            for i in range(3):
                turned_ups[w, i * half : (i + 1) * half, :] = ups_ref[w, i].T

    acc = dot_nn(wm_ref[...], turned_ups[0]) + dot_nn(wo_ref[...], turned_ups[1])
    total[n] = acc.T

    @pl.when(n == pl.num_programs(0) - 1)
    def _():
        x = x_ref[...].astype(jnp.float32)
        scale = row_scale(jnp.sum(x * x, axis=1, keepdims=True), width)
        unit = x * scale
        up = jnp.concatenate([total[i] for i in range(width // nb)], axis=1)
        gain_out[...] = jnp.sum(up * unit, axis=0, keepdims=True)
        raised = up * gain_ref[...]
        mean = jnp.sum(raised * unit, axis=1, keepdims=True) / width
        out_ref[...] = grad_ref[...] + scale * (raised - unit * mean)


def input_grad(ups, weights, weights_other, x, grad, gain):
    tokens, width = x.shape
    nb = 512
    f32 = jnp.float32

    def whole(*shape):
        return pl.BlockSpec(shape, lambda n: (0,) * len(shape))

    return pl.pallas_call(
        input_grad_body,
        out_shape=(jax.ShapeDtypeStruct((tokens, width), f32), jax.ShapeDtypeStruct((1, width), f32)),
        grid=(width // nb,),
        in_specs=[
            whole(*ups.shape),
            pl.BlockSpec((nb, 3 * width // 2), lambda n: (n, 0)),
            pl.BlockSpec((nb, 3 * width // 2), lambda n: (n, 0)),
            whole(tokens, width),
            whole(tokens, width),
            whole(1, width),
        ],
        out_specs=(whole(tokens, width), whole(1, width)),
        scratch_shapes=[
            pltpu.VMEM((width // nb, tokens, nb), f32),
            pltpu.VMEM((2, 3 * width // 2, tokens), jnp.bfloat16),
        ],
        compiler_params=kernel_params(),
    )(ups, weights, weights_other, x, grad, gain[None])


def cut_body(x_ref, y_ref, low, high):
    low[...] = x_ref[...]
    high[...] = y_ref[...]


def cut_pair(x, y):
    n, width = x.shape[0] // 2, x.shape[1]
    out = jax.ShapeDtypeStruct((n, width), x.dtype)
    place = pl.BlockSpec((n, width), lambda i: (0, 0))
    return pl.pallas_call(
        cut_body,
        out_shape=(out, out),
        grid=(1,),
        in_specs=[place, pl.BlockSpec((n, width), lambda i: (1, 0))],
        out_specs=(place, place),
    )(x, y)


def finish_body(k, low, high, *rest):
    got_x, got_y, more_y, more_x = rest[:k], rest[k : 2 * k], rest[2 * k : 2 * k + 3], rest[2 * k + 3 : 2 * k + 6]
    gate, up, down = rest[2 * k + 6 :]
    j = pl.program_id(1)
    ff = more_y[0].shape[1]

    def out(part, got, more):
        f32 = jnp.float32
        total = part[0].astype(f32) + jnp.concatenate([v[0].astype(f32) for v in got], axis=0)
        total = total + jnp.concatenate([v[0].astype(f32) for v in more], axis=0)
        gate[0] = total[:ff].T
        up[0] = total[ff : 2 * ff].T
        down[0] = total[2 * ff :]

    @pl.when(j == 0)
    def _():
        out(low, got_x, more_y)

    @pl.when(j == 1)
    def _():
        out(high, got_y, more_x)


def finish(low, high, got_x, got_y, more):
    n_e, rows, half = low.shape
    ff = rows // 3
    k = len(got_x)

    def place(v):
        return pl.BlockSpec((1,) + v.shape[1:], lambda e, j: (e, 0, 0))

    ins = [low, high, *got_x, *got_y, *[m[0] for m in more], *[m[1] for m in more]]
    f32 = jnp.float32
    turned_out = jax.ShapeDtypeStruct((n_e, 2 * half, ff), f32)
    return pl.pallas_call(
        functools.partial(finish_body, k),
        out_shape=(turned_out, turned_out, jax.ShapeDtypeStruct((n_e, ff, 2 * half), f32)),
        grid=(n_e, 2),
        in_specs=[place(v) for v in ins],
        out_specs=(
            pl.BlockSpec((1, half, ff), lambda e, j: (e, j, 0)),
            pl.BlockSpec((1, half, ff), lambda e, j: (e, j, 0)),
            pl.BlockSpec((1, ff, half), lambda e, j: (e, 0, j)),
        ),
        compiler_params=kernel_params(),
    )(*ins)


fence = lax.optimization_barrier


def plus(a, b):
    return a.astype(jnp.float32) + b.astype(jnp.float32)


def on_device(
    hidden_in,
    cotangent,
    attention_gain,
    query_gain,
    key_gain,
    mixture_gain,
    query_weight,
    key_weight,
    value_weight,
    output_weight,
    router_weight,
    gate_weight,
    up_weight,
    down_weight,
    routes,
    segments,
):
    bf16, f32 = jnp.bfloat16, jnp.float32
    n_dp, owners = lax.axis_size("dp"), lax.axis_size("expert")
    nz = owners // 2
    n_dev = n_dp * owners
    tokens, width = hidden_in.shape
    half = width // 2
    unit = width // (n_dev // 2)
    cut = unit // 2
    top = routes.shape[1]
    exp_dev = gate_weight.shape[0]
    experts = exp_dev * owners
    cap = max(2, tokens * top * 5 // (experts * 4))
    ff = gate_weight.shape[2]
    rows_dev = attention_gain.shape[0]
    score_scale = HD ** (-0.5)
    dp, ex = lax.axis_index("dp"), lax.axis_index("expert")
    core, zc = ex % 2, ex // 2

    def swap(v, axis, bit):
        size = n_dp if axis == "dp" else owners
        return lax.ppermute(v, axis, [(i, i ^ bit) for i in range(size)])

    def swap_core(v):
        return swap(v, "expert", 1)

    def swap_x(v):
        return swap(v, "dp", 1)

    def swap_y(v):
        return swap(v, "dp", 2)

    def ring(v):
        return lax.ppermute(v, "expert", [(i, (i + 2) % owners) for i in range(owners)])

    def in_order(bit, mine, other, axis):
        return jnp.where(
            bit == 0,
            jnp.concatenate([mine, other], axis=axis),
            jnp.concatenate([other, mine], axis=axis),
        )

    def half_of(v, which, axis):
        return lax.dynamic_slice_in_dim(v, which * (v.shape[axis] // 2), v.shape[axis] // 2, axis)

    def halves(v, axis):
        return half_of(v, core, axis), half_of(v, 1 - core, axis)

    def by_rows(v):
        return with_layout_constraint(v, Layout((0, 1)))

    def thirds(v):
        return [v[:, t * ff : (t + 1) * ff] for t in range(3)]

    def chip_row(plane, r):
        return ((dp ^ plane) * nz + (zc - r) % nz) * unit

    bits = []
    b = 1
    while b < owners:
        bits.append(("expert", b, (ex // b) % 2))
        b *= 2
    b = 1
    while b < n_dp:
        bits.append(("dp", b, (dp // b) % 2))
        b *= 2

    sources = (query_weight, key_weight, value_weight, output_weight)
    gains = (attention_gain, query_gain, key_gain, mixture_gain)
    small = jnp.concatenate([v[:, None] for v in gains] + [router_weight], axis=1)
    small = jnp.pad(small, ((0, 0), (0, -small.shape[1] % 128)))
    theirs = jnp.concatenate([half_of(w, 1 - core, 1) for w in sources] + [small], axis=1)
    mine = jnp.concatenate([half_of(w, core, 1) for w in sources] + [small], axis=1)
    piece = by_rows(in_order(core, mine, swap_core(theirs), 0))
    piece, gate_weight, up_weight, down_weight, cotangent, segments, hidden_in = fence(
        (piece, gate_weight, up_weight, down_weight, cotangent, segments, hidden_in)
    )

    main = 4 * half
    weights, small_all = blank(width, main), blank(width, small.shape[1])
    route_rows = routes.T.astype(bf16).reshape(-1, width)
    pad = -route_rows.shape[0] % 16
    cot_piece = jnp.concatenate([cotangent, route_rows, jnp.zeros((pad, width), bf16)], axis=0)
    cot_steps = [cot_piece]

    def put(buffers, v, row):
        kept, kept_small = buffers
        kept = lax.dynamic_update_slice(kept, v[:, :main], (row, 0))
        kept_small = by_rows(lax.dynamic_update_slice(kept_small, v[:, main:], (row, 0)))
        return kept, kept_small

    buffers = (weights, small_all)
    before, arrived = None, []
    for r in range(nz):
        by_x, by_y = by_rows(swap_x(piece)), by_rows(swap_y(piece))
        following, sent = (), ()
        if before is not None:
            sent = cut_pair(*before)
            sent = (by_rows(swap_y(sent[0])), by_rows(swap_x(sent[1])))
        if r + 1 < nz:
            following = by_rows(ring(piece))
        else:
            cot_steps.append(ring(cot_steps[-1]))
        for v, row in arrived + [(piece, chip_row(0, r))]:
            buffers = put(buffers, v, row)
        by_x, by_y, following, sent, buffers, cot_steps = fence(
            (by_x, by_y, following, sent, buffers, cot_steps)
        )
        arrived = [(by_x, chip_row(1, r)), (by_y, chip_row(2, r))]
        if before is not None:
            arrived += [(sent[0], chip_row(3, r - 1)), (sent[1], chip_row(3, r - 1) + cut)]
        before, piece = (by_x, by_y), following
    sent = cut_pair(*before)
    sent = (by_rows(swap_y(sent[0])), by_rows(swap_x(sent[1])))
    own_first, own_rest = [], []
    for j in range(2):
        part = slice(j * half, (j + 1) * half)
        own_first.append(gate_weight[:, part].swapaxes(1, 2))
        own_rest.append(
            jnp.concatenate([up_weight[:, part].swapaxes(1, 2), down_weight[:, :, part]], axis=1)
        )
    cosine, sine = rotary_tables(segments, HD)
    cosine = jnp.concatenate([cosine[0], cosine[0]], axis=1)
    sine = jnp.concatenate([-sine[0], sine[0]], axis=1)
    document = segments[0]
    for v, row in arrived:
        buffers = put(buffers, v, row)
    buffers, own_first, own_rest, cosine, sine, document, sent, cot_steps = fence(
        (buffers, own_first, own_rest, cosine, sine, document, sent, cot_steps)
    )
    buffers = put(buffers, sent[0], chip_row(3, nz - 1))
    buffers = put(buffers, sent[1], chip_row(3, nz - 1) + cut)
    weights, small_all = fence(buffers)

    weights_other = swap_core(weights)
    x_low, y_high = [swap_x(own_first[0])], [swap_y(own_first[1])]
    if len(cot_steps) < nz:
        cot_steps.append(ring(cot_steps[-1]))
    gains_all = small_all[:, :4].astype(f32).T
    router_t = small_all[:, 4 : 4 + experts].T
    attention_gain_full, mixture_gain_full = gains_all[0], gains_all[3]
    query_gain_rel = jnp.concatenate(halves(gains_all[1], 0))
    key_gain_rel = jnp.concatenate(halves(gains_all[2], 0))
    core_ref = core[None]
    normed, raw, query_squares, key_squares = project(hidden_in, attention_gain_full, weights)
    (
        weights,
        weights_other,
        mixture_gain_full,
        router_t,
        normed,
        raw,
        x_low,
        y_high,
        cot_steps,
        own_first,
        own_rest,
    ) = fence(
        (
            weights,
            weights_other,
            mixture_gain_full,
            router_t,
            normed,
            raw,
            x_low,
            y_high,
            cot_steps,
            own_first,
            own_rest,
        )
    )

    x_low.append(swap_x(own_rest[0]))
    y_high.append(swap_y(own_rest[1]))
    while len(cot_steps) < nz:
        cot_steps.append(ring(cot_steps[-1]))
    raw, query_squares, key_squares = project_other(
        normed, weights_other, query_squares, key_squares, raw
    )
    query_heads, key_heads, value_heads, context = attend(
        raw, query_squares, key_squares, query_gain_rel, key_gain_rel, cosine, sine, document
    )
    middle, mixed_piece, router_probs = middle_of(
        core_ref, context, weights, weights_other, hidden_in, mixture_gain_full, router_t
    )
    mixed_piece, x_low, y_high, cot_steps, context, middle, normed = fence(
        (mixed_piece, x_low, y_high, cot_steps, context, middle, normed)
    )
    n_prob = 2 * experts * tokens // width

    mixed_all, cot_all, mixed_last = [], [], mixed_piece
    x_high, y_low = [], []
    for r in range(nz):
        following = ring(mixed_last) if r + 1 < nz else ()
        got = ()
        if r < 3:
            sent = [(v[:, :ff], w[:, :ff], w[:, ff:])[r] for v, w in zip(own_first, own_rest)]
            got = (swap_x(sent[1]), swap_y(sent[0]))
        mixed_all += [mixed_last, swap_core(mixed_last)]
        cot_all += [cot_steps[r], swap_core(cot_steps[r])]
        following, mixed_all, cot_all, got = fence((following, mixed_all, cot_all, got))
        if r < 3:
            x_high.append(got[0])
            y_low.append(got[1])
        mixed_last = following
    number = (ex * exp_dev)[None]
    rank_row, rank_col, gate_row = plan(
        number, mixed_all, cot_all, n_prob // 2, top, exp_dev, tokens
    )

    send_pieces = ((0, 5 * ff // 4), (5 * ff // 4, 17 * ff // 16), (37 * ff // 16, 11 * ff // 16))
    last_pieces = ((0, 3 * ff // 4), (3 * ff // 4, 5 * ff // 4), (2 * ff, ff))
    corner_low, corner_high = [swap_y(v) for v in x_low], [swap_x(v) for v in y_high]
    shards = (tuple(zip(own_first, own_rest)), (x_low, x_high), (y_low, y_high))
    rows, acts, gates, products, send_x, keep_x, keep_y, send_y = experts_first(
        mixed_all, cot_all, shards, ff, rank_row, gate_row, cap, send_pieces
    )
    corner_low, corner_high, rows, acts, gates, products, send_x, send_y = fence(
        (corner_low, corner_high, rows, acts, gates, products, send_x, send_y)
    )

    got_x, got_y = [swap_x(send_x[0])], [swap_y(send_y[0])]
    parts = ()
    if nz > 4:
        parts = fence(expert_grads(acts, rows, ff))
    shards = shards + ((corner_low, corner_high),)
    acts_last, products, last_low, last_high = experts_last(
        rows, gates, products, shards[3], ff, last_pieces
    )
    acts_last, products, last_low, last_high, got_x, got_y, send_x, send_y = fence(
        (acts_last, products, last_low, last_high, got_x, got_y, send_x, send_y)
    )

    def spread(kinds, zs, gates):
        return experts_spread(
            number,
            acts,
            acts_last,
            products,
            shards,
            ff,
            width,
            rank_row,
            rank_col,
            cap,
            kinds,
            zs,
            gates,
        )

    near = tuple(range(1, nz // 2 + 1))
    far = tuple(range(nz // 2 + 1, nz)) + (0,)
    got_x.append(swap_x(send_x[1]))
    got_y.append(swap_y(send_y[1]))
    copied_near, other_near = spread((0, 1), near, True)
    copied_near, other_near, got_x, got_y, send_x, send_y = fence(
        (copied_near, other_near, got_x, got_y, send_x, send_y)
    )
    got_near = swap_core(other_near)
    got_near = fence(got_near)

    class Total:
        def __init__(self, blocks):
            self.blocks, self.value, self.at = blocks, blocks[1], 2

        def move(self):
            self.value = ring(self.value.astype(bf16))

        def add(self):
            self.value = plus(self.value, self.blocks[self.at % nz])
            self.at += 1

        def rest(self):
            while self.at <= nz:
                self.move()
                self.add()
            return self.value

    copies_sum = Total({r: plus(copied_near[i], got_near[i]) for i, r in enumerate(near)})
    copies_sum.move()
    got_x.append(swap_x(send_x[2]))
    got_y.append(swap_y(send_y[2]))
    got_last_x, got_last_y = [swap_x(last_low[0])], [swap_y(last_high[0])]
    copied_far, other_far = spread((0, 1), far, True)
    copies_sum.value, copied_far, other_far, got_x, got_y, got_last_x, got_last_y = fence(
        (copies_sum.value, copied_far, other_far, got_x, got_y, got_last_x, got_last_y)
    )
    got_far = swap_core(other_far)
    copies_sum.add()
    copies_sum.move()
    got_last_x.append(swap_x(last_low[1]))
    got_last_y.append(swap_y(last_high[1]))
    mixture, mixture_other = spread((2,), tuple(range(nz)), False)
    copies_sum.value, got_far, mixture, mixture_other, got_last_x, got_last_y = fence(
        (copies_sum.value, got_far, mixture, mixture_other, got_last_x, got_last_y)
    )
    copies_sum.blocks.update({r: plus(copied_far[i], got_far[i]) for i, r in enumerate(far)})
    copies_sum.add()
    copies_sum.move()
    got_last_x.append(swap_x(last_low[2]))
    got_last_y.append(swap_y(last_high[2]))
    got_mix = swap_core(mixture_other)
    context = in_order(core, context[:, :half], context[:, half:], 1)
    first_x = jnp.concatenate(got_last_x[:2], axis=1)
    first_y = jnp.concatenate(got_last_y[:2], axis=1)
    more_y = [plus(a, b).astype(bf16) for a, b in zip(thirds(keep_y)[:2], thirds(first_x)[:2])]
    more_x = [plus(a, b).astype(bf16) for a, b in zip(thirds(keep_x)[:2], thirds(first_y)[:2])]
    copies_sum.value, got_last_x, got_last_y, context, got_mix, more_x, more_y = fence(
        (copies_sum.value, got_last_x, got_last_y, context, got_mix, more_x, more_y)
    )
    for sums, kept, got in ((more_y, keep_y, got_last_x), (more_x, keep_x, got_last_y)):
        sums.append(plus(thirds(kept)[2], got[2]).astype(bf16))
    copies_sum.add()
    copies_sum = copies_sum.rest()

    def send_more(t):
        return swap_y(more_y[t]), swap_x(more_x[t])

    more = [send_more(0)]
    mixed = Total({r: plus(mixture[r], got_mix[r]) for r in range(nz)})
    mixed.move()
    normed_other, context_other = swap_core(normed), swap_core(context)
    (middle_grad, branch, branch_other, context_up, mixture_gain_grad, router_grad, _) = middle_back(
        core_ref,
        copies_sum,
        middle,
        cotangent,
        mixture_gain_full,
        router_probs,
        router_t,
        weights,
        weights_other,
    )
    (context_up, branch, branch_other, mixed.value, normed_other, context_other, more, more_x, more_y) = fence(
        (context_up, branch, branch_other, mixed.value, normed_other, context_other, more, more_x, more_y)
    )
    mixed.add()
    mixed.move()
    more.append(send_more(1))
    got_branch = swap_core(branch_other)
    ups, query_gain_grad, key_gain_grad = attend_back(
        query_heads,
        key_heads,
        value_heads,
        context_up,
        raw,
        query_squares,
        key_squares,
        query_gain_rel,
        key_gain_rel,
        cosine,
        sine,
        document,
    )
    ups, mixed.value, got_branch, more = fence((ups, mixed.value, got_branch, more))
    got_ups = swap_core(ups[1])
    more.append(send_more(2))
    first, second = qkv_grad(normed, normed_other, ups, got_ups)
    mixed.add()
    mixed.move()
    def several(v, picks):
        return jnp.concatenate(
            [lax.dynamic_slice_in_dim(v, chip_row(plane, r), unit, 0) for plane, r in picks],
            axis=0,
        )

    def pack(v, n):
        k = n * unit // v.shape[0]
        step = v.shape[1] // k
        return jnp.concatenate([v[:, i * step : (i + 1) * step] for i in range(k)], axis=0)

    def unpack(v, rows):
        return jnp.concatenate([v[i : i + rows] for i in range(0, v.shape[0], rows)], axis=1)

    side = 3 * half // 2

    def step_one(rs):
        sent = several(first, [(1, r) for r in rs] + [(3, r) for r in rs])
        back = several(second, [(2, r) for r in rs] + [(3, r) for r in rs])
        return sent, back

    def step_two(rs, by_x, by_y):
        n = len(rs) * unit
        more_y = plus(several(first, [(2, r) for r in rs]), by_x[n:]).astype(bf16)
        more_x = plus(several(second, [(1, r) for r in rs]), by_y[n:]).astype(bf16)
        return more_y, more_x

    def step_three(rs, by_x, by_y, more_y, more_x):
        n = len(rs) * unit
        left = plus(several(first, [(0, r) for r in rs]), by_x[:n]) + more_y.astype(f32)
        right = plus(several(second, [(0, r) for r in rs]), by_y[:n]) + more_x.astype(f32)
        whole = jnp.concatenate([left, right], axis=1)
        return {r: whole[i * unit : (i + 1) * unit] for i, r in enumerate(rs)}

    near_sent = step_one(near)
    near_sent, more, ups, first, second, branch, got_branch = fence(
        (near_sent, more, ups, first, second, branch, got_branch)
    )
    output_grad = jnp.einsum(
        "tc,td->cd",
        jnp.concatenate([context, context_other], axis=0),
        jnp.concatenate([branch, got_branch], axis=0),
        preferred_element_type=f32,
    ).astype(bf16)
    near_got = (swap_x(near_sent[0]), swap_y(near_sent[1]))
    output_sum = Total(
        [several(output_grad, [(plane, r) for plane in range(n_dp)]) for r in range(nz)]
    )
    output_sum.move()
    far_sent = step_one(far)
    hidden_grad, attention_gain_grad = input_grad(
        ups, weights, weights_other, hidden_in, middle_grad, attention_gain_full
    )

    def canonical(v):
        return in_order(core, v[:half], v[half:], 0)

    gain_grads = (
        attention_gain_grad[0],
        canonical(query_gain_grad[0]),
        canonical(key_gain_grad[0]),
        mixture_gain_grad[0],
    )
    small_sum = jnp.concatenate(
        [v.reshape(n_dev, rows_dev) for v in gain_grads]
        + [
            router_grad.reshape(experts, n_dev, rows_dev)
            .swapaxes(0, 1)
            .reshape(n_dev, experts * rows_dev)
        ],
        axis=1,
    )
    folded = []

    def fold(v):
        axis, bit, mark = bits[len(folded)]
        folded.append(bit)
        v = v.reshape(v.shape[0] // 2, 2, v.shape[1])
        keep = lax.dynamic_index_in_dim(v, mark, 1, False)
        return keep + swap(lax.dynamic_index_in_dim(v, 1 - mark, 1, False), axis, bit)

    near_got, output_sum.value, small_sum, hidden_grad, far_sent, mixed.value = fence(
        (near_got, output_sum.value, small_sum, hidden_grad, far_sent, mixed.value)
    )
    mixed.add()
    mixed = mixed.rest()
    layer_out = (middle + mixed).astype(bf16)
    near_more = step_two(near, *near_got)
    near_more = fence(near_more)
    near_more = (swap_y(near_more[0]), swap_x(near_more[1]))
    far_got = (swap_x(far_sent[0]), swap_y(far_sent[1]))
    output_sum.add()
    output_sum.move()
    near_more, output_sum.value = fence((near_more, output_sum.value))
    output_sum.add()
    output_sum.move()
    blocks = step_three(near, *near_got, *near_more)
    small_sum = fold(small_sum)
    far_got, output_sum.value, blocks, small_sum = fence(
        (far_got, output_sum.value, blocks, small_sum)
    )
    output_sum.add()
    output_sum = output_sum.rest()
    out_low = output_sum[:, : half // 2].astype(bf16)
    out_high = output_sum[:, half // 2 :].astype(bf16)
    far_more = step_two(far, *far_got)
    to_y = jnp.concatenate([far_more[0], pack(out_high[2 * unit :], len(far))], axis=1)
    to_x = jnp.concatenate(
        [
            far_more[1],
            pack(jnp.concatenate([out_low[unit : 2 * unit], out_low[3 * unit :]], axis=0), len(far)),
        ],
        axis=1,
    )
    by_y, by_x = swap_y(to_y), swap_x(to_x)
    weight_sum = Total(blocks)
    for _ in near[:-1]:
        weight_sum.move()
        if weight_sum.at < near[-1]:
            weight_sum.add()
    small_sum = fold(small_sum)
    if not parts:
        acts, rows, _ = fence((acts, rows, to_y))
        parts = expert_grads(acts, rows, ff)
    by_y, by_x, weight_sum.value, small_sum, parts, got_x, got_y, more = fence(
        (by_y, by_x, weight_sum.value, small_sum, parts, got_x, got_y, more)
    )
    expert_grad = finish(*parts, got_x, got_y, more)
    far_more = (by_y[:, :side], by_x[:, :side])
    got_out_x = unpack(by_x[:, side:], 2 * unit)
    got_out_y = unpack(by_y[:, side:], 2 * unit)
    out_more_y = plus(out_low[2 * unit : 3 * unit], got_out_x[unit:]).astype(bf16)
    out_more_x = plus(out_high[unit : 2 * unit], got_out_y[unit:]).astype(bf16)
    if len(near) > 1:
        weight_sum.add()
    weight_sum.move()
    out_more_y, out_more_x = swap_y(out_more_y), swap_x(out_more_x)
    small_sum = fold(small_sum)
    weight_sum.blocks.update(step_three(far, *far_got, *far_more))
    weight_sum.value, out_more_y, out_more_x, small_sum, expert_grad = fence(
        (weight_sum.value, out_more_y, out_more_x, small_sum, expert_grad)
    )
    weight_sum.add()
    while weight_sum.at <= nz:
        weight_sum.move()
        if len(folded) < len(bits):
            small_sum = fold(small_sum)
        weight_sum.value, small_sum = fence((weight_sum.value, small_sum))
        weight_sum.add()
    total = weight_sum.value
    while len(folded) < len(bits):
        small_sum = fold(small_sum)
    small_sum = small_sum[0]
    gain_parts = small_sum[: 4 * rows_dev].reshape(4, rows_dev)
    router_part = small_sum[4 * rows_dev :].reshape(experts, rows_dev).T
    out_total = jnp.concatenate(
        [
            plus(out_low[:unit], got_out_x[:unit]) + out_more_y.astype(f32),
            plus(out_high[:unit], got_out_y[:unit]) + out_more_x.astype(f32),
        ],
        axis=1,
    )
    total = jnp.concatenate([total, out_total], axis=1)
    kept_rows = half_of(total, core, 0)
    got_rows = swap_core(half_of(total, 1 - core, 0))
    weight_grads = [
        in_order(
            core, kept_rows[:, i * half : (i + 1) * half], got_rows[:, i * half : (i + 1) * half], 1
        )
        for i in range(4)
    ]
    return (
        layer_out,
        hidden_grad,
        gain_parts[0],
        gain_parts[1],
        gain_parts[2],
        gain_parts[3],
        weight_grads[0],
        weight_grads[1],
        weight_grads[2],
        weight_grads[3],
        router_part,
        *expert_grad,
    )


def solution(mesh):
    return jax.shard_map(
        on_device,
        mesh=mesh,
        in_specs=(
            P(("dp", "expert"), None),
            P(("dp", "expert"), None),
            P(("dp", "expert")),
            P(("dp", "expert")),
            P(("dp", "expert")),
            P(("dp", "expert")),
            P(("dp", "expert"), None),
            P(("dp", "expert"), None),
            P(("dp", "expert"), None),
            P(("dp", "expert"), None),
            P(("dp", "expert"), None),
            P("expert", None, "dp"),
            P("expert", None, "dp"),
            P("expert", "dp", None),
            P(("dp", "expert"), None),
            P(("dp", "expert"), None),
        ),
        out_specs=(
            P(("dp", "expert"), None),
            P(("dp", "expert"), None),
            P(("dp", "expert")),
            P(("dp", "expert")),
            P(("dp", "expert")),
            P(("dp", "expert")),
            P(("dp", "expert"), None),
            P(("dp", "expert"), None),
            P(("dp", "expert"), None),
            P(("dp", "expert"), None),
            P(("dp", "expert"), None),
            P("expert", None, "dp"),
            P("expert", None, "dp"),
            P("expert", "dp", None),
        ),
        check_vma=False,
    )
```

```python
import functools
import math

import jax
import jax.numpy as jnp
from jax import lax
from jax.experimental import pallas as pl
from jax.experimental.layout import Layout, with_layout_constraint
from jax.experimental.pallas import tpu as pltpu
from jax.sharding import PartitionSpec as P

HD = 128


epsilon = 1e-05
rope_base = 10000.0
masked_score = -1e30


def rotary_tables(segments, head_size):
    length = segments.shape[-1]
    order = jnp.arange(length, dtype=jnp.int32)
    starts = jnp.sum((segments[..., None, :] < segments[..., :, None]).astype(jnp.int32), axis=-1)
    position = (order - starts).astype(jnp.float32)
    frequency = rope_base ** (-2.0 * jnp.arange(head_size // 2, dtype=jnp.float32) / head_size)
    angle = position[..., None] * frequency
    return (jnp.cos(angle), jnp.sin(angle))


VMEM_BYTES = 60 * 1024 * 1024


def dot_nt(a, b):
    return lax.dot_general(a, b, (((1,), (1,)), ((), ())), preferred_element_type=jnp.float32)


def dot_nn(a, b):
    return lax.dot_general(a, b, (((1,), (0,)), ((), ())), preferred_element_type=jnp.float32)


def dot_tn(a, b):
    return lax.dot_general(a, b, (((0,), (0,)), ((), ())), preferred_element_type=jnp.float32)


def flat(shards):
    return [v for pair in shards for side in pair for v in side]


def counts(shards):
    return tuple(tuple(len(side) for side in pair) for pair in shards)


def unflat(refs, shape):
    out, at = [], 0
    for pair in shape:
        sides = []
        for n in pair:
            sides.append(refs[at : at + n])
            at += n
        out.append(sides)
    return out, refs[at:]


def third(side, i, e, ff):
    for ref in side:
        n = ref.shape[1] // ff
        if i < n:
            return ref.at[e, pl.ds(i * ff, ff)]
        i -= n


def block(start, size):
    return pl.ds(pl.multiple_of(start * size, size), size)


def swiglu(gate_pre, up_pre, back, gate):
    sig = 1.0 / (1.0 + jnp.exp(-gate_pre))
    act = gate_pre * sig
    hid = act * up_pre
    scaled = back * gate
    return (
        jnp.sum(hid * back, axis=1, keepdims=True),
        (scaled * up_pre * (sig + act * (1.0 - sig))).astype(jnp.bfloat16),
        (scaled * act).astype(jnp.bfloat16),
        (hid * gate).astype(jnp.bfloat16),
    )


def first_body(cap, ff, rb, nb, src, team, shape, pieces, *rest):
    xr, gr, rest = rest[:src], rest[src : 2 * src], rest[2 * src :]
    shards, rest = unflat(rest, shape)
    rr_ref, gt_ref, rg_ref, h_ref, gate_ref, dgr_ref = rest[:6]
    k = len(pieces)
    sx, kx, ky, sy, rest = rest[6 : 6 + k], rest[6 + k], rest[7 + k], rest[8 + k : 8 + 2 * k], rest[8 + 2 * k :]
    (p, xs, gs, r, g, hb, dp, p_sem, in_sem, rg_sem, h_sem, d_sem) = rest
    n_e, _, _, tok = rr_ref.shape
    rows, width = r.shape[1:]
    half = width // 2

    def load(f, e, slot):
        return [
            pltpu.make_async_copy(
                third(shards[f][j], i, e, ff), p.at[slot, pl.ds(i * ff, ff), pl.ds(j * half, half)], p_sem.at[slot, 3 * j + i]
            )
            for j in range(2)
            for i in range(3)
        ]

    for c in load(0, 0, 0):
        c.start()

    def fetch(k, j, slot):
        return (
            pltpu.make_async_copy(xr[k].at[pl.ds(0, tok)], xs.at[slot, j], in_sem.at[0, slot, j]),
            pltpu.make_async_copy(gr[k].at[pl.ds(0, tok)], gs.at[slot, j], in_sem.at[1, slot, j]),
        )

    def fetch_start(s, slot):
        for k in range(src):

            @pl.when(s == k // team)
            def _():
                for c in fetch(k, k % team, slot):
                    c.start()

    fetch_start(0, 0)

    @pl.loop(0, src // team)
    def _(s):
        slot = lax.rem(s, 2)

        @pl.when(s + 1 < src // team)
        def _():
            fetch_start(s + 1, 1 - slot)

        for j in range(team):
            for c in fetch(j, j, slot):
                c.wait()
        got = [[[], [], []] for _ in range(n_e)]
        for j in range(team):
            hits = [lax.broadcasted_iota(jnp.int32, (cap, tok), 0) == rr_ref[e, s * team + j] for e in range(n_e)]
            one = jnp.concatenate([hit.astype(jnp.float32) for hit in hits], axis=0).astype(jnp.bfloat16)
            rx, rg = dot_nn(one, xs[slot, j]), dot_nn(one, gs[slot, j])
            for e in range(n_e):
                got[e][0].append(rx[e * cap : (e + 1) * cap])
                got[e][1].append(rg[e * cap : (e + 1) * cap])
                got[e][2].append(jnp.sum(jnp.where(hits[e], gt_ref[e, s * team + j], 0.0), axis=1, keepdims=True))
        at = block(s, team * cap)
        for e in range(n_e):
            a, b, c = [v[0] if team == 1 else jnp.concatenate(v, axis=0) for v in got[e]]
            r[e, at, :] = a.astype(jnp.bfloat16)
            g[e, at, :] = b.astype(jnp.bfloat16)
            gate_ref[e, at, :] = c

    keep = []
    for e in range(n_e):
        for i, v in enumerate((r, g)):
            c = pltpu.make_async_copy(v.at[e], rg_ref.at[e, i], rg_sem.at[e, i])
            c.start()
            keep.append(c)
    dgr_ref[...] = jnp.zeros_like(dgr_ref)

    def put_h(f, e, slot):
        return pltpu.make_async_copy(hb.at[slot], h_ref.at[e, :, :, pl.ds(f * ff, ff)], h_sem.at[slot])

    def put_d(f, e, slot):
        kept, j, sent = ((kx, 1, sx), (ky, 0, sy))[f - 1]
        other = dp.at[slot, :, pl.ds(j * half, half)]
        return [pltpu.make_async_copy(other, kept.at[e], d_sem.at[len(pieces), slot])] + [
            pltpu.make_async_copy(
                dp.at[slot, pl.ds(at, n), pl.ds((1 - j) * half, half)], sent[i].at[e], d_sem.at[i, slot]
            )
            for i, (at, n) in enumerate(pieces)
        ]

    for f in range(3):
        for e in range(n_e):
            slot = e % 2
            following = load(f, e + 1, 1 - slot) if e + 1 < n_e else load(f + 1, 0, 1 - slot) if f < 2 else []
            for c in following:
                c.start()
            for c in load(f, e, slot):
                c.wait()
            if f > 0:
                put_h(f - 1, e, slot).wait()

            @pl.loop(0, rows // rb)
            def _(m):
                at = block(m, rb)
                pre = dot_nt(r[e, at, :], p[slot, pl.ds(0, 2 * ff), :])
                back = dot_nt(g[e, at, :], p[slot, pl.ds(2 * ff, ff), :])
                total, a, b, c = swiglu(pre[:, :ff], pre[:, ff:], back, gate_ref[e, at, :])
                dgr_ref[e, at, :] += total
                hb[slot, 0, at, :] = a
                hb[slot, 1, at, :] = b
                hb[slot, 2, at, :] = c

            put_h(f, e, slot).start()
            if f > 0:
                if f > 1:
                    for c in put_d(f - 1, e, slot):
                        c.wait()
                both = jnp.concatenate([hb[slot, 0], hb[slot, 1]], axis=1)

                @pl.loop(0, width // nb)
                def _(n):
                    at = block(n, nb)
                    dp[slot, 0 : 2 * ff, at] = dot_tn(both, r[e, :, at]).astype(jnp.bfloat16)
                    dp[slot, 2 * ff : 3 * ff, at] = dot_tn(hb[slot, 2], g[e, :, at]).astype(jnp.bfloat16)

                for c in put_d(f, e, slot):
                    c.start()
    for e in range(n_e):
        put_h(2, e, e % 2).wait()
        for c in put_d(2, e, e % 2):
            c.wait()
    for c in keep:
        c.wait()


def experts_first(xs, gs, shards, ff, rr, gt, cap, pieces, rb=640, nb=1024):
    n_e, src, _, tok = rr.shape
    width = xs[0].shape[1]
    shape = counts(shards)
    rows = src * cap
    team = 16 // math.gcd(cap, 16)
    bf, f32 = jnp.bfloat16, jnp.float32
    anys, vm = pl.BlockSpec(memory_space=pl.ANY), pl.BlockSpec(memory_space=pltpu.VMEM)
    part = jax.ShapeDtypeStruct((n_e, 3 * ff, width // 2), bf)
    ones = [jax.ShapeDtypeStruct((n_e, n, width // 2), bf) for _, n in pieces]
    outs = pl.pallas_call(
        functools.partial(first_body, cap, ff, rb, nb, src, team, shape, pieces),
        out_shape=(
            jax.ShapeDtypeStruct((n_e, 2, rows, width), bf),
            jax.ShapeDtypeStruct((n_e, 3, rows, 3 * ff), bf),
            jax.ShapeDtypeStruct((n_e, rows, 1), f32),
            jax.ShapeDtypeStruct((n_e, rows, 1), f32),
            *ones, part, part, *ones,
        ),
        in_specs=[anys] * (2 * src + len(flat(shards))) + [vm] * 2,
        out_specs=(anys, anys, vm, vm) + (anys,) * (2 + 2 * len(pieces)),
        scratch_shapes=[
            pltpu.VMEM((2, 3 * ff, width), bf),
            pltpu.VMEM((2, team, tok, width), bf),
            pltpu.VMEM((2, team, tok, width), bf),
            pltpu.VMEM((n_e, rows, width), bf),
            pltpu.VMEM((n_e, rows, width), bf),
            pltpu.VMEM((2, 3, rows, ff), bf),
            pltpu.VMEM((2, 3 * ff, width), bf),
            pltpu.SemaphoreType.DMA((2, 6)),
            pltpu.SemaphoreType.DMA((2, 2, team)),
            pltpu.SemaphoreType.DMA((n_e, 2)),
            pltpu.SemaphoreType.DMA((2,)),
            pltpu.SemaphoreType.DMA((len(pieces) + 1, 2)),
        ],
        compiler_params=pltpu.CompilerParams(vmem_limit_bytes=VMEM_BYTES),
    )(*xs, *gs, *flat(shards), rr, gt)
    k = len(pieces)
    return *outs[:4], outs[4 : 4 + k], outs[4 + k], outs[5 + k], outs[6 + k :]


def tile_width(src):
    return 512 if src <= 8 else 128


def plan_body(n_prob, top, number_ref, *rest):
    src = (len(rest) - 9) // 2
    xr, gr, rest = rest[:src], rest[src : 2 * src], rest[2 * src :]
    row_ref, col_ref, gate_ref, mx, gx, probs, sems, gate_sem, rank = rest
    n_e, _, _, tok = row_ref.shape
    width = mx.shape[2]
    copies = []
    for s in range(src):
        copies.append(pltpu.make_async_copy(xr[s].at[pl.ds(tok, mx.shape[1])], mx.at[s], sems.at[s]))
        copies.append(pltpu.make_async_copy(gr[s].at[pl.ds(tok, gx.shape[1])], gx.at[s], gate_sem.at[s]))
    for c in copies:
        c.start()
    for c in copies:
        c.wait()
    for s in range(src):
        line = gx[s].astype(jnp.float32)
        both = mx[s].astype(jnp.float32)
        probs[s] = both[0:n_prob] + both[n_prob : 2 * n_prob]
        for e in range(n_e):
            number = number_ref[0] + e
            hit = None
            for k in range(top):
                at = k * tok
                same = line[at // width : at // width + 1, at % width : at % width + tok] == number.astype(jnp.float32)
                hit = same if hit is None else hit | same
            rank[e * src + s : e * src + s + 1, :] = hit.astype(jnp.float32)
            at = number * tok
            gate_ref[e, s] = probs[s, pl.ds(at // width, 1), pl.ds(pl.multiple_of(lax.rem(at, width), tok), tok)]
    lower = lax.broadcasted_iota(jnp.int32, (tok, tok), 0) <= lax.broadcasted_iota(jnp.int32, (tok, tok), 1)
    hits = rank[...]
    places = dot_nn(hits.astype(jnp.bfloat16), lower.astype(jnp.float32).astype(jnp.bfloat16))
    places = jnp.where(hits > 0.0, places - 1.0, -1.0)
    col_ref[...] = places.T.astype(jnp.int32)
    for e in range(n_e):
        for s in range(src):
            i = e * src + s
            row_ref[e, s] = places[i : i + 1].astype(jnp.int32)


def plan(number, xs, gs, n_prob, top, n_e, tok):
    src, width = len(xs), xs[0].shape[1]
    anys, vm = pl.BlockSpec(memory_space=pl.ANY), pl.BlockSpec(memory_space=pltpu.VMEM)
    bf, f32 = jnp.bfloat16, jnp.float32
    return pl.pallas_call(
        functools.partial(plan_body, n_prob, top),
        out_shape=(
            jax.ShapeDtypeStruct((n_e, src, 1, tok), jnp.int32),
            jax.ShapeDtypeStruct((tok, n_e * src), jnp.int32),
            jax.ShapeDtypeStruct((n_e, src, 1, tok), f32),
        ),
        in_specs=[pl.BlockSpec(memory_space=pltpu.SMEM)] + [anys] * (2 * src),
        out_specs=(vm, vm, vm),
        scratch_shapes=[
            pltpu.VMEM((src, xs[0].shape[0] - tok, width), bf),
            pltpu.VMEM((src, gs[0].shape[0] - tok, width), bf),
            pltpu.VMEM((src, n_prob, width), f32),
            pltpu.SemaphoreType.DMA((src,)),
            pltpu.SemaphoreType.DMA((src,)),
            pltpu.VMEM((n_e * src, tok), f32),
        ],
        compiler_params=pltpu.CompilerParams(vmem_limit_bytes=VMEM_BYTES),
    )(number, *xs, *gs)


def last_body(ff, rb, nb, shape, pieces, rg_ref, gate_ref, dgr_in, *rest):
    (side,), rest = unflat(rest, shape)
    k = len(pieces)
    hd_ref, dgr_ref, low, high, rest = rest[0], rest[1], rest[2 : 2 + k], rest[2 + k : 2 + 2 * k], rest[2 + 2 * k :]
    p, r, g, hb, ht, dp, p_sem, rg_sem, h_sem, d_sem = rest
    n_e, rows, width = r.shape
    half = width // 2
    weights, loads = [], []
    for e in range(n_e):
        weights.append([
            pltpu.make_async_copy(
                third(side[j], i, e, ff), p.at[e, pl.ds(i * ff, ff), pl.ds(j * half, half)], p_sem.at[e, 3 * j + i])
            for j in range(2) for i in range(3)
        ])
        loads.append([[
            pltpu.make_async_copy(rg_ref.at[e, i, pl.ds(m * rb, rb)], v.at[e, pl.ds(m * rb, rb)], rg_sem.at[e, i, m])
            for i, v in enumerate((r, g))] for m in range(rows // rb)])
    def begin(e):
        for c in weights[e] + [c for m in loads[e] for c in m]:
            c.start()

    begin(0)
    outs = []
    for e in range(n_e):
        for c in weights[e]:
            c.wait()
        if e + 1 < n_e:
            begin(e + 1)
        for m in range(rows // rb):
            for c in loads[e][m]:
                c.wait()
            at = pl.ds(m * rb, rb)
            pre = dot_nt(r[e, at, :], p[e, pl.ds(0, 2 * ff), :])
            back = dot_nt(g[e, at, :], p[e, pl.ds(2 * ff, ff), :])
            total, a, b, c = swiglu(pre[:, :ff], pre[:, ff:], back, gate_ref[e, at, :])
            dgr_ref[e, at, :] = dgr_in[e, at, :] + total
            hb[e, 0, at, :] = a
            hb[e, 1, at, :] = b
            hb[e, 2, at, :] = c
        c = pltpu.make_async_copy(hb.at[e], hd_ref.at[e], h_sem.at[e])
        c.start()
        outs.append(c)
        for i in range(3):
            ht[pl.ds(i * ff, ff), :] = hb[e, i].T

        @pl.loop(0, width // nb)
        def _(n):
            at = block(n, nb)
            dp[e, 0 : 2 * ff, at] = dot_nn(ht[0 : 2 * ff, :], r[e, :, at]).astype(jnp.bfloat16)
            dp[e, 2 * ff : 3 * ff, at] = dot_nn(ht[2 * ff : 3 * ff, :], g[e, :, at]).astype(jnp.bfloat16)

        for j, refs in enumerate((low, high)):
            for i, (at, n) in enumerate(pieces):
                c = pltpu.make_async_copy(
                    dp.at[e, pl.ds(at, n), pl.ds(j * half, half)], refs[i].at[e], d_sem.at[e, len(pieces) * j + i]
                )
                c.start()
                outs.append(c)
    for c in outs:
        c.wait()


def experts_last(rg, gate, dgr, side, ff, pieces, rb=640, nb=1024):
    n_e, _, rows, width = rg.shape
    shape = counts((side,))
    bf, f32 = jnp.bfloat16, jnp.float32
    anys, vm = pl.BlockSpec(memory_space=pl.ANY), pl.BlockSpec(memory_space=pltpu.VMEM)
    parts = [jax.ShapeDtypeStruct((n_e, n, width // 2), bf) for _, n in pieces]
    outs = pl.pallas_call(
        functools.partial(last_body, ff, rb, nb, shape, pieces),
        out_shape=(
            jax.ShapeDtypeStruct((n_e, 3, rows, ff), bf),
            jax.ShapeDtypeStruct((n_e, rows, 1), f32),
            *parts, *parts,
        ),
        in_specs=[anys] + [vm] * 2 + [anys] * len(flat((side,))),
        out_specs=(anys, vm) + (anys,) * (2 * len(pieces)),
        scratch_shapes=[
            pltpu.VMEM((n_e, 3 * ff, width), bf),
            pltpu.VMEM((n_e, rows, width), bf),
            pltpu.VMEM((n_e, rows, width), bf),
            pltpu.VMEM((n_e, 3, rows, ff), bf),
            pltpu.VMEM((3 * ff, rows), bf),
            pltpu.VMEM((n_e, 3 * ff, width), bf),
            pltpu.SemaphoreType.DMA((n_e, 6)),
            pltpu.SemaphoreType.DMA((n_e, 2, rows // rb)),
            pltpu.SemaphoreType.DMA((n_e,)),
            pltpu.SemaphoreType.DMA((n_e, 2 * len(pieces))),
        ],
        compiler_params=pltpu.CompilerParams(vmem_limit_bytes=VMEM_BYTES),
    )(rg, gate, dgr, *flat((side,)))
    k = len(pieces)
    return outs[0], outs[1], outs[2 : 2 + k], outs[2 + k :]


def spread_body(cap, ff, nb, shape, kinds, zs, extra, number_ref, ha_ref, hd_ref, dgr, *rest):
    shards, rest = unflat(rest, shape)
    rr_ref, cols_ref, own_ref, sib_ref, p, h, dg, acc, stage, p_sem, h_sem, st_sem = rest
    n_e = ha_ref.shape[0]
    width = p.shape[2]
    half = width // 2
    hidden = 4 * ff
    src, tok, tall = rr_ref.shape[1], rr_ref.shape[3], stage.shape[3]
    tiles = width // nb
    loads = []
    for e in range(n_e):
        copies = []
        loads.append(copies)
        for i, kind in enumerate(kinds):
            for q in range(4):
                for j in range(2):
                    copies.append(pltpu.make_async_copy(
                        third(shards[q][j], kind, e, ff),
                        p.at[e, pl.ds(i * hidden + q * ff, ff), pl.ds(j * half, half)], p_sem.at[e, i, 2 * q + j]))
            for m, z in enumerate(zs):
                at, to = pl.ds(2 * z * cap, 2 * cap), pl.ds(2 * m * cap, 2 * cap)
                copies.append(pltpu.make_async_copy(
                    ha_ref.at[e, kind, at], h.at[e, to, pl.ds(i * hidden, 3 * ff)], h_sem.at[e, i, m, 0]))
                copies.append(pltpu.make_async_copy(
                    hd_ref.at[e, kind, at], h.at[e, to, pl.ds(i * hidden + 3 * ff, ff)], h_sem.at[e, i, m, 1]))
    for copies in loads:
        for c in copies:
            c.start()
    if extra:
        for e in range(n_e):
            for m, z in enumerate(zs):
                for w in range(2):
                    s = 2 * z + w
                    hit = lax.broadcasted_iota(jnp.int32, (cap, tok), 0) == rr_ref[e, s]
                    dg[e, 2 * m + w] = jnp.sum(
                        jnp.where(hit, dgr[e, pl.ds(s * cap, cap), :], 0.0), axis=0, keepdims=True)

    def extras(n, s):
        shape = (tall - tok, nb)
        line = lax.broadcasted_iota(jnp.int32, shape, 0)
        place = n * nb + lax.broadcasted_iota(jnp.int32, shape, 1)
        total = jnp.zeros(shape, jnp.float32)
        for e in range(n_e):
            v = dg[e, s]
            if nb >= tok:
                v = jnp.concatenate([v] * (nb // tok), axis=1)
            else:
                v = jnp.where(lax.rem(n, 2) == 0, v[:, :nb], v[:, nb:])
            at = (number_ref[0] + e) * tok
            inside = (place >= lax.rem(at, width)) & (place < lax.rem(at, width) + tok)
            low = v.astype(jnp.bfloat16).astype(jnp.float32)
            row = at // width
            total = jnp.where(inside & (line == row), low, total)
            total = jnp.where(inside & (line == row + extra), v - low, total)
        return total.astype(jnp.bfloat16)

    def put(n, slot):
        return [
            pltpu.make_async_copy(stage.at[slot, w], ref.at[:, :, block(n, nb)], st_sem.at[slot, w])
            for w, ref in enumerate((own_ref, sib_ref))
        ]

    def column(e, s):
        i = e * src + s
        if isinstance(s, int):
            return cols_ref[:, i : i + 1]
        lane = lax.broadcasted_iota(jnp.int32, cols_ref.shape, 1)
        return jnp.sum(jnp.where(lane == i, cols_ref[...], 0), axis=1, keepdims=True)

    @pl.loop(0, tiles)
    def _(n):
        slot = lax.rem(n, 2)
        for e in range(n_e):

            @pl.when(n == 0)
            def _():
                for c in loads[e]:
                    c.wait()

            acc[e] = dot_nn(h[e], p[e, :, block(n, nb)])

        @pl.when(n >= 2)
        def _():
            for c in put(n, slot):
                c.wait()

        def one(m, z, w):
            hits = [
                (lax.broadcasted_iota(jnp.int32, (tok, cap), 1) == column(e, 2 * z + w)).astype(jnp.float32)
                for e in range(n_e)
            ]
            hit = jnp.concatenate(hits, axis=1).astype(jnp.bfloat16)
            s = 2 * m + w
            part = jnp.concatenate([acc[e, block(s, cap)] for e in range(n_e)], axis=0).astype(jnp.bfloat16)
            stage[slot, w, m, 0:tok, :] = dot_nn(hit, part).astype(jnp.bfloat16)
            if extra:
                stage[slot, w, m, tok:tall, :] = extras(n, s)

        if len(zs) <= 4:
            for m, z in enumerate(zs):
                for w in range(2):
                    one(m, z, w)
        else:

            @pl.loop(0, len(zs))
            def _(m):
                z = lax.rem(m + zs[0], src // 2)
                for w in range(2):
                    one(m, z, w)

        for c in put(n, slot):
            c.start()

    for slot in range(2):
        for c in put(slot, slot):
            c.wait()


def experts_spread(number, ha, hd, dgr, shards, ff, width, rr, cols, cap, kinds, zs, gates):
    n_e, src, _, tok = rr.shape
    nb = tile_width(src)
    extra = n_e * src * tok // width if gates else 0
    tall = tok + 2 * extra + -2 * extra % 16
    shape = counts(shards)
    rows = 2 * len(zs) * cap
    bf, f32 = jnp.bfloat16, jnp.float32
    anys, vm = pl.BlockSpec(memory_space=pl.ANY), pl.BlockSpec(memory_space=pltpu.VMEM)
    side = jax.ShapeDtypeStruct((len(zs), tall, width), bf)
    return pl.pallas_call(
        functools.partial(spread_body, cap, ff, nb, shape, kinds, zs, extra),
        out_shape=(side, side),
        in_specs=[pl.BlockSpec(memory_space=pltpu.SMEM), anys, anys, vm] + [anys] * len(flat(shards)) + [vm, vm],
        out_specs=(anys, anys),
        scratch_shapes=[
            pltpu.VMEM((n_e, 4 * ff * len(kinds), width), bf),
            pltpu.VMEM((n_e, rows, 4 * ff * len(kinds)), bf),
            pltpu.VMEM((n_e, 2 * len(zs), 1, tok), f32),
            pltpu.VMEM((n_e, rows, nb), f32),
            pltpu.VMEM((2, 2, len(zs), tall, nb), bf),
            pltpu.SemaphoreType.DMA((n_e, len(kinds), 8)),
            pltpu.SemaphoreType.DMA((n_e, len(kinds), len(zs), 2)),
            pltpu.SemaphoreType.DMA((2, 2)),
        ],
        compiler_params=pltpu.CompilerParams(vmem_limit_bytes=VMEM_BYTES),
    )(number, ha, hd, dgr, *flat(shards), rr, cols)


def grads_body(ff, h_ref, rg_ref, low, high, ht):
    part = pl.program_id(1)

    @pl.when(part == 0)
    def _():
        for i in range(3):
            ht[pl.ds(i * ff, ff), :] = h_ref[0, i].T

    def out(ref):
        ref[0, 0 : 2 * ff, :] = dot_nn(ht[0 : 2 * ff, :], rg_ref[0, 0]).astype(jnp.bfloat16)
        ref[0, 2 * ff : 3 * ff, :] = dot_nn(ht[2 * ff : 3 * ff, :], rg_ref[0, 1]).astype(jnp.bfloat16)

    @pl.when(part == 0)
    def _():
        out(low)

    @pl.when(part == 1)
    def _():
        out(high)


def expert_grads(h, rg, ff):
    n_e, _, rows, _ = h.shape
    half = rg.shape[3] // 2
    side = jax.ShapeDtypeStruct((n_e, 3 * ff, half), jnp.bfloat16)
    return pl.pallas_call(
        functools.partial(grads_body, ff),
        out_shape=(side, side),
        grid=(n_e, 2),
        in_specs=[
            pl.BlockSpec((1, 3, rows, ff), lambda e, j: (e, 0, 0, 0)),
            pl.BlockSpec((1, 2, rows, half), lambda e, j: (e, 0, 0, j)),
        ],
        out_specs=(pl.BlockSpec((1, 3 * ff, half), lambda e, j: (e, 0, 0)),) * 2,
        scratch_shapes=[pltpu.VMEM((3 * ff, rows), jnp.bfloat16)],
        compiler_params=pltpu.CompilerParams(vmem_limit_bytes=VMEM_BYTES),
    )(h, rg)


def blank(*shape):
    return pl.pallas_call(
        lambda ref: None,
        out_shape=jax.ShapeDtypeStruct(shape, jnp.bfloat16),
        out_specs=pl.BlockSpec(memory_space=pl.ANY),
    )()


def kernel_params():
    return pltpu.CompilerParams(vmem_limit_bytes=VMEM_BYTES)


def row_scale(squares, width):
    return lax.rsqrt(squares / width + epsilon)


def project_body(first, *refs):
    if first:
        x_ref, gain_ref, w_ref, normed_ref, raw_ref, qs_ref, ks_ref = refs
    else:
        normed_ref, w_ref, qs_in, ks_in, _, raw_ref, qs_ref, ks_ref = refs
    n = pl.program_id(0)

    @pl.when(n == 0)
    def _():
        if first:
            x = x_ref[...].astype(jnp.float32)
            scale = row_scale(jnp.sum(x * x, axis=1, keepdims=True), x.shape[1])
            normed_ref[...] = (x * scale * gain_ref[...]).astype(jnp.bfloat16)
            qs_ref[...] = jnp.zeros_like(qs_ref)
            ks_ref[...] = jnp.zeros_like(ks_ref)
        else:
            qs_ref[...] = qs_in[...]
            ks_ref[...] = ks_in[...]

    raw = dot_nn(normed_ref[...], w_ref[...])
    raw_ref[...] = raw
    squares = jnp.sum(raw * raw, axis=1, keepdims=True)
    qs_ref[...] += jnp.where(n == 0, squares, 0.0)
    ks_ref[...] += jnp.where(n == 1, squares, 0.0)


def project(x, gain, weights):
    tokens, width = x.shape
    half = width // 2
    f32 = jnp.float32
    sums = jax.ShapeDtypeStruct((tokens, 1), f32)

    def whole(*shape):
        return pl.BlockSpec(shape, lambda n: (0, 0))

    return pl.pallas_call(
        functools.partial(project_body, True),
        out_shape=(
            jax.ShapeDtypeStruct((tokens, width), jnp.bfloat16),
            jax.ShapeDtypeStruct((tokens, 6 * half), f32),
            sums,
            sums,
        ),
        grid=(3,),
        in_specs=[whole(tokens, width), whole(1, width), pl.BlockSpec((width, half), lambda n: (0, n))],
        out_specs=(whole(tokens, width), pl.BlockSpec((tokens, half), lambda n: (0, n)), whole(tokens, 1), whole(tokens, 1)),
        compiler_params=kernel_params(),
    )(x, gain[None], weights)


def project_other(normed, weights, qs, ks, raw):
    tokens, width = normed.shape
    half = width // 2
    f32 = jnp.float32
    sums = jax.ShapeDtypeStruct((tokens, 1), f32)

    def whole(*shape):
        return pl.BlockSpec(shape, lambda n: (0, 0))

    return pl.pallas_call(
        functools.partial(project_body, False),
        out_shape=(jax.ShapeDtypeStruct((tokens, 6 * half), f32), sums, sums),
        grid=(3,),
        in_specs=[whole(tokens, width), pl.BlockSpec((width, half), lambda n: (0, n)), whole(tokens, 1), whole(tokens, 1),
                  pl.BlockSpec(memory_space=pl.ANY)],
        out_specs=(pl.BlockSpec((tokens, half), lambda n: (0, 3 + n)), whole(tokens, 1), whole(tokens, 1)),
        input_output_aliases={4: 0},
        compiler_params=kernel_params(),
    )(normed, weights, qs, ks, raw)


def turned(v, cosine, sine):
    return v * cosine + pltpu.roll(v, v.shape[1] // 2, 1) * sine


def masked_chances(q, k, allowed, scale):
    scores = jnp.where(allowed, dot_nt(q, k) * scale, masked_score)
    grown = jnp.exp(scores - jnp.max(scores, axis=1, keepdims=True))
    return grown / jnp.sum(grown, axis=1, keepdims=True)


def allowed_pairs(row_ref, col_ref):
    n = row_ref.shape[1]
    rows = lax.broadcasted_iota(jnp.int32, (n, n), 0)
    cols = lax.broadcasted_iota(jnp.int32, (n, n), 1)
    return (row_ref[...] == col_ref[...]) & (rows >= cols)


def attend_body(width, q_ref, k_ref, v_ref, qs, ks, qg, kg, cos, sin, doc_row, doc_col, q_out, k_out, v_out, c_out):
    allowed = allowed_pairs(doc_row, doc_col)
    q_scale, k_scale = row_scale(qs[...], width), row_scale(ks[...], width)
    for i in range(q_ref.shape[1] // HD):
        at = slice(i * HD, (i + 1) * HD)
        q = turned(q_ref[:, at] * q_scale * qg[:, at], cos[...], sin[...]).astype(jnp.bfloat16)
        k = turned(k_ref[:, at] * k_scale * kg[:, at], cos[...], sin[...]).astype(jnp.bfloat16)
        v = v_ref[:, at].astype(jnp.bfloat16)
        q_out[:, at] = q
        k_out[:, at] = k
        v_out[:, at] = v
        chances = masked_chances(q, k, allowed, HD ** (-0.5)).astype(jnp.bfloat16)
        c_out[:, at] = dot_nn(chances, v).astype(jnp.bfloat16)


def attend(raw, qs, ks, qg, kg, cos, sin, document):
    tokens, width = raw.shape[0], raw.shape[1] // 3
    nb = width // 4

    def part(i):
        return pl.BlockSpec((tokens, nb), lambda h: (0, 6 * (h // 2) + 2 * i + h % 2))

    head = pl.BlockSpec((tokens, nb), lambda h: (0, h))
    gain = pl.BlockSpec((1, nb), lambda h: (0, h))

    def whole(*shape):
        return pl.BlockSpec(shape, lambda h: (0, 0))

    out = jax.ShapeDtypeStruct((tokens, width), jnp.bfloat16)
    return pl.pallas_call(
        functools.partial(attend_body, width),
        out_shape=(out,) * 4,
        grid=(4,),
        in_specs=[part(0), part(1), part(2), whole(tokens, 1), whole(tokens, 1), gain, gain]
        + [whole(tokens, HD), whole(tokens, HD), whole(1, tokens), whole(tokens, 1)],
        out_specs=(head,) * 4,
        compiler_params=kernel_params(),
    )(raw, raw, raw, qs, ks, qg[None], kg[None], cos, sin, document[None], document[:, None])


def lines(v, width):
    n, k = v.shape
    per = width // k
    return jnp.concatenate(
        [jnp.concatenate([v[i + j : i + j + 1] for j in range(per)], axis=1) for i in range(0, n, per)], axis=0
    )


def unlines(v, k):
    return jnp.concatenate([v[i : i + 1, j : j + k] for i in range(v.shape[0]) for j in range(0, v.shape[1], k)], axis=0)


def middle_body(core_ref, ctx_ref, wm_ref, wo_ref, x_ref, gain_ref, router_ref, middle_ref, piece_ref, probs_ref):
    w, j = pl.program_id(0), pl.program_id(1)
    tokens, width = x_ref.shape
    half = width // 2

    def out(ref, side):
        at = pl.ds(pl.multiple_of(side * half, half), half)
        part = dot_nn(ctx_ref[...], ref[...])

        @pl.when(j == 0)
        def _():
            middle_ref[:, at] = x_ref[:, at].astype(jnp.float32) + part

        @pl.when(j == 1)
        def _():
            middle_ref[:, at] += part

    @pl.when(w == 0)
    def _():
        out(wm_ref, core_ref[0])

    @pl.when(w == 1)
    def _():
        out(wo_ref, 1 - core_ref[0])

    @pl.when((w == 1) & (j == 1))
    def _():
        middle = middle_ref[...]
        scale = row_scale(jnp.sum(middle * middle, axis=1, keepdims=True), width)
        mixed = (middle * scale * gain_ref[...]).astype(jnp.bfloat16)
        piece_ref[0:tokens, :] = mixed
        logits = dot_nt(router_ref[...], mixed)
        grown = jnp.exp(logits - jnp.max(logits, axis=0, keepdims=True))
        probs = grown / jnp.sum(grown, axis=0, keepdims=True)
        probs_ref[...] = probs
        high = probs.astype(jnp.bfloat16).astype(jnp.float32)
        rows = [lines(high, width), lines(probs - high, width)]
        n = piece_ref.shape[0] - tokens - 2 * rows[0].shape[0]
        if n:
            rows.append(jnp.zeros((n, width), jnp.float32))
        piece_ref[tokens : piece_ref.shape[0], :] = jnp.concatenate(rows, axis=0).astype(jnp.bfloat16)


def half_specs(half):
    return [
        pl.BlockSpec((half, half), lambda w, j, core: (jnp.where(w == 0, core[0] ^ j, 1 - core[0]), 3)),
        pl.BlockSpec((half, half), lambda w, j, core: (jnp.where(w == 0, core[0], core[0] ^ j), 3)),
    ]


def middle_of(core, context, weights, weights_other, x, gain, router_t):
    tokens, width = x.shape
    half = width // 2
    experts = router_t.shape[0]
    extra = 2 * experts * tokens // width
    tall = tokens + extra + -extra % 16

    def whole(*shape):
        return pl.BlockSpec(shape, lambda w, j, core: (0, 0))

    return pl.pallas_call(
        middle_body,
        out_shape=(
            jax.ShapeDtypeStruct((tokens, width), jnp.float32),
            jax.ShapeDtypeStruct((tall, width), jnp.bfloat16),
            jax.ShapeDtypeStruct((experts, tokens), jnp.float32),
        ),
        grid_spec=pltpu.PrefetchScalarGridSpec(
            num_scalar_prefetch=1,
            grid=(2, 2),
            in_specs=[pl.BlockSpec((tokens, half), lambda w, j, core: (0, j))]
            + half_specs(half)
            + [whole(tokens, width), whole(1, width), whole(experts, width)],
            out_specs=(whole(tokens, width), whole(tall, width), whole(experts, tokens)),
        ),
        compiler_params=kernel_params(),
    )(core, context, weights, weights_other, x, gain[None], router_t)


def middle_back_body(core_ref, sum_ref, middle_ref, cot_ref, gain_ref, probs_ref, router_ref, wm_ref, wo_ref,
                     grad_ref, mine_ref, other_ref, up_ref, gain_out, router_out, logit_ref, branch, acc):
    j, w = pl.program_id(0), pl.program_id(1)
    tokens, width = middle_ref.shape
    half = width // 2

    @pl.when((j == 0) & (w == 0))
    def _():
        middle = middle_ref[...]
        scale = row_scale(jnp.sum(middle * middle, axis=1, keepdims=True), width)
        unit = middle * scale
        probs = probs_ref[...]
        n = probs.shape[0] * tokens // width
        total = sum_ref[tokens : tokens + n, :] + sum_ref[tokens + n : tokens + 2 * n, :]
        raised = unlines(total, tokens)
        logit = (probs * (raised - jnp.sum(probs * raised, axis=0, keepdims=True))).astype(jnp.bfloat16)
        logit_ref[...] = logit
        mixed_up = sum_ref[0:tokens, :] + dot_tn(logit, router_ref[...])
        gain_out[...] = jnp.sum(mixed_up * unit, axis=0, keepdims=True)
        router_out[...] = dot_nn(logit, (unit * gain_ref[...]).astype(jnp.bfloat16))
        raised = mixed_up * gain_ref[...]
        mean = jnp.sum(raised * unit, axis=1, keepdims=True) / width
        grad = cot_ref[...].astype(jnp.float32) + scale * (raised - unit * mean)
        grad_ref[...] = grad
        branch[...] = grad.astype(jnp.bfloat16)
        mine_ref[...] = branch[:, pl.ds(pl.multiple_of(core_ref[0] * half, half), half)]
        other_ref[...] = branch[:, pl.ds(pl.multiple_of((1 - core_ref[0]) * half, half), half)]

    @pl.when(w == 0)
    def _():
        acc[...] = dot_nt(mine_ref[...], wm_ref[...])

    @pl.when(w == 1)
    def _():
        up_ref[...] = (acc[...] + dot_nt(other_ref[...], wo_ref[...])).astype(jnp.bfloat16)


def middle_back(core, total, middle, cotangent, gain, probs, router_t, weights, weights_other):
    tokens, width = middle.shape
    half = width // 2
    experts = probs.shape[0]
    bf, f32 = jnp.bfloat16, jnp.float32

    def whole(*shape):
        return pl.BlockSpec(shape, lambda j, w, core: (0, 0))

    specs = [
        pl.BlockSpec((half, half), lambda j, w, core: (core[0] ^ j, 3)),
        pl.BlockSpec((half, half), lambda j, w, core: (core[0] ^ j, 3)),
    ]
    return pl.pallas_call(
        middle_back_body,
        out_shape=(
            jax.ShapeDtypeStruct((tokens, width), f32),
            jax.ShapeDtypeStruct((tokens, half), bf),
            jax.ShapeDtypeStruct((tokens, half), bf),
            jax.ShapeDtypeStruct((tokens, width), bf),
            jax.ShapeDtypeStruct((1, width), f32),
            jax.ShapeDtypeStruct((experts, width), f32),
            jax.ShapeDtypeStruct((experts, tokens), bf),
        ),
        grid_spec=pltpu.PrefetchScalarGridSpec(
            num_scalar_prefetch=1,
            grid=(2, 2),
            in_specs=[whole(*total.shape), whole(tokens, width), whole(tokens, width), whole(1, width),
                      whole(experts, tokens), whole(experts, width)] + specs,
            out_specs=(
                whole(tokens, width), whole(tokens, half), whole(tokens, half),
                pl.BlockSpec((tokens, half), lambda j, w, core: (0, j)),
                whole(1, width), whole(experts, width), whole(experts, tokens),
            ),
            scratch_shapes=[pltpu.VMEM((tokens, width), bf), pltpu.VMEM((tokens, half), f32)],
        ),
        compiler_params=kernel_params(),
    )(core, total, middle, cotangent, gain[None], probs, router_t, weights, weights_other)


def attend_back_body(width, q_ref, k_ref, v_ref, u_ref, q_raw, k_raw, qs, ks, qg, kg, cos, sin, doc_row, doc_col,
                     ups_mine, ups_other, qg_out, kg_out, q_back, k_back, v_back, q_mean, k_mean):
    phase, h = pl.program_id(0), pl.program_id(1)
    nb = q_ref.shape[1]
    q_scale, k_scale = row_scale(qs[...], width), row_scale(ks[...], width)
    cols = pl.ds(pl.multiple_of(h * nb, nb), nb)

    @pl.when((phase == 0) & (h == 0))
    def _():
        q_mean[...] = jnp.zeros_like(q_mean)
        k_mean[...] = jnp.zeros_like(k_mean)

    @pl.when(phase == 0)
    def _():
        allowed = allowed_pairs(doc_row, doc_col)
        dq, dk, dv = [], [], []
        for i in range(nb // HD):
            at = slice(i * HD, (i + 1) * HD)
            q, k, u = q_ref[:, at], k_ref[:, at], u_ref[:, at]
            chances = masked_chances(q, k, allowed, HD ** (-0.5))
            raised = dot_nt(u, v_ref[:, at])
            dv.append(dot_tn(chances.astype(jnp.bfloat16), u).astype(jnp.bfloat16))
            back = chances * (raised - jnp.sum(chances * raised, axis=1, keepdims=True))
            back = back.astype(jnp.bfloat16)
            dq.append(turned(dot_nn(back, k) * HD ** (-0.5), cos[...], -sin[...]))
            dk.append(turned(dot_tn(back, q) * HD ** (-0.5), cos[...], -sin[...]))
        for parts, raw, scale, gain, mean, kept, out in (
            (dq, q_raw, q_scale, qg, q_mean, q_back, qg_out),
            (dk, k_raw, k_scale, kg, k_mean, k_back, kg_out),
        ):
            back = jnp.concatenate(parts, axis=1)
            kept[h] = back
            grown = back * (raw[...] * scale)
            out[0:1, cols] = jnp.sum(grown, axis=0, keepdims=True)
            mean[...] += jnp.sum(grown * gain[...], axis=1, keepdims=True)
        v_back[h] = jnp.concatenate(dv, axis=1)

    @pl.when(phase == 1)
    def _():
        ups = []
        for raw, scale, gain, mean, kept in (
            (q_raw, q_scale, qg, q_mean, q_back),
            (k_raw, k_scale, kg, k_mean, k_back),
        ):
            up = scale * (kept[h] * gain[...] - raw[...] * scale * (mean[...] / width))
            ups.append(up.astype(jnp.bfloat16))
        ups.append(v_back[h])

        @pl.when(h < 2)
        def _():
            for i in range(3):
                ups_mine[i] = ups[i]

        @pl.when(h >= 2)
        def _():
            for i in range(3):
                ups_other[i] = ups[i]


def attend_back(q, k, v, up, raw, qs, ks, qg, kg, cos, sin, document):
    tokens, width = v.shape
    nb = width // 4
    f32 = jnp.float32

    def part(i):
        return pl.BlockSpec((tokens, nb), lambda p, h: (0, 6 * (h // 2) + 2 * i + h % 2))

    head = pl.BlockSpec((tokens, nb), lambda p, h: (0, jnp.where(p == 0, h, 3)))
    gain = pl.BlockSpec((1, nb), lambda p, h: (0, h))

    def whole(*shape):
        return pl.BlockSpec(shape, lambda p, h: (0, 0))

    def mine_place(p, h):
        return (0, 0, jnp.where(p == 0, 0, jnp.minimum(h, 1)))

    def other_place(p, h):
        return (0, 0, jnp.where(p == 0, 0, jnp.maximum(h - 2, 0)))

    side = jax.ShapeDtypeStruct((3, tokens, width // 2), jnp.bfloat16)
    return pl.pallas_call(
        functools.partial(attend_back_body, width),
        out_shape=(
            side,
            side,
            jax.ShapeDtypeStruct((1, width), f32),
            jax.ShapeDtypeStruct((1, width), f32),
        ),
        grid=(2, 4),
        in_specs=[head, head, head, head, part(0), part(1), whole(tokens, 1), whole(tokens, 1), gain, gain]
        + [whole(tokens, HD), whole(tokens, HD), whole(1, tokens), whole(tokens, 1)],
        out_specs=(
            pl.BlockSpec((3, tokens, nb), mine_place),
            pl.BlockSpec((3, tokens, nb), other_place),
            whole(1, width),
            whole(1, width),
        ),
        scratch_shapes=[
            pltpu.VMEM((4, tokens, nb), f32),
            pltpu.VMEM((4, tokens, nb), f32),
            pltpu.VMEM((4, tokens, nb), jnp.bfloat16),
            pltpu.VMEM((tokens, 1), f32),
            pltpu.VMEM((tokens, 1), f32),
        ],
        compiler_params=kernel_params(),
    )(q, k, v, up, raw, raw, qs, ks, qg[None], kg[None], cos, sin, document[None], document[:, None])


def qkv_grad_body(n_ref, no_ref, u_ref, uo_ref, first, second, pair):
    i = pl.program_id(0)
    tokens = n_ref.shape[0]

    @pl.when(i == 0)
    def _():
        pair[:, 0:tokens] = n_ref[...].T
        pair[:, tokens : 2 * tokens] = no_ref[...].T

    ups = jnp.concatenate([u_ref[0], uo_ref[0]], axis=0)
    got = dot_nn(pair[...], ups).astype(jnp.bfloat16)

    @pl.when(i < 3)
    def _():
        first[...] = got

    @pl.when(i >= 3)
    def _():
        second[...] = got


def qkv_grad(normed, normed_other, ups, got):
    tokens, width = normed.shape
    nb = width // 4
    out = jax.ShapeDtypeStruct((width, 3 * nb), jnp.bfloat16)

    def whole(*shape):
        return pl.BlockSpec(shape, lambda i: (0, 0))

    return pl.pallas_call(
        qkv_grad_body,
        out_shape=(out, out),
        grid=(6,),
        in_specs=[
            whole(tokens, width),
            whole(tokens, width),
            pl.BlockSpec((1, tokens, nb), lambda i: (i // 2, 0, i % 2)),
            pl.BlockSpec((1, tokens, nb), lambda i: (i // 2, 0, i % 2)),
        ],
        out_specs=(
            pl.BlockSpec((width, nb), lambda i: (0, jnp.minimum(i, 2))),
            pl.BlockSpec((width, nb), lambda i: (0, jnp.maximum(i - 3, 0))),
        ),
        scratch_shapes=[pltpu.VMEM((width, 2 * tokens), jnp.bfloat16)],
        compiler_params=kernel_params(),
    )(normed, normed_other, ups, got)


def input_grad_body(um_ref, uo_ref, wm_ref, wo_ref, x_ref, grad_ref, gain_ref, out_ref, gain_out, total, turned_ups):
    n = pl.program_id(0)
    tokens, width = x_ref.shape
    half = width // 2
    nb = wm_ref.shape[0]

    @pl.when(n == 0)
    def _():
        for w, ref in enumerate((um_ref, uo_ref)):
            for i in range(3):
                turned_ups[w, i * half : (i + 1) * half, :] = ref[i].T

    acc = dot_nn(wm_ref[...], turned_ups[0]) + dot_nn(wo_ref[...], turned_ups[1])
    total[n] = acc.T

    @pl.when(n == pl.num_programs(0) - 1)
    def _():
        x = x_ref[...].astype(jnp.float32)
        scale = row_scale(jnp.sum(x * x, axis=1, keepdims=True), width)
        unit = x * scale
        up = jnp.concatenate([total[i] for i in range(width // nb)], axis=1)
        gain_out[...] = jnp.sum(up * unit, axis=0, keepdims=True)
        raised = up * gain_ref[...]
        mean = jnp.sum(raised * unit, axis=1, keepdims=True) / width
        out_ref[...] = grad_ref[...] + scale * (raised - unit * mean)


def input_grad(ups, weights, weights_other, x, grad, gain):
    tokens, width = x.shape
    nb = 512
    f32 = jnp.float32

    def whole(*shape):
        return pl.BlockSpec(shape, lambda n: (0,) * len(shape))

    return pl.pallas_call(
        input_grad_body,
        out_shape=(jax.ShapeDtypeStruct((tokens, width), f32), jax.ShapeDtypeStruct((1, width), f32)),
        grid=(width // nb,),
        in_specs=[
            whole(*ups[0].shape),
            whole(*ups[1].shape),
            pl.BlockSpec((nb, 3 * width // 2), lambda n: (n, 0)),
            pl.BlockSpec((nb, 3 * width // 2), lambda n: (n, 0)),
            whole(tokens, width),
            whole(tokens, width),
            whole(1, width),
        ],
        out_specs=(whole(tokens, width), whole(1, width)),
        scratch_shapes=[
            pltpu.VMEM((width // nb, tokens, nb), f32),
            pltpu.VMEM((2, 3 * width // 2, tokens), jnp.bfloat16),
        ],
        compiler_params=kernel_params(),
    )(*ups, weights, weights_other, x, grad, gain[None])


def cut_body(x_ref, y_ref, low, high):
    low[...] = x_ref[...]
    high[...] = y_ref[...]


def cut_pair(x, y):
    n, width = x.shape[0] // 2, x.shape[1]
    out = jax.ShapeDtypeStruct((n, width), x.dtype)
    place = pl.BlockSpec((n, width), lambda i: (0, 0))
    return pl.pallas_call(
        cut_body,
        out_shape=(out, out),
        grid=(1,),
        in_specs=[place, pl.BlockSpec((n, width), lambda i: (1, 0))],
        out_specs=(place, place),
    )(x, y)


def finish_body(k, low, high, *rest):
    got_x, got_y, more_y, more_x = rest[:k], rest[k : 2 * k], rest[2 * k : 2 * k + 3], rest[2 * k + 3 : 2 * k + 6]
    gate, up, down = rest[2 * k + 6 :]
    j = pl.program_id(1)
    ff = more_y[0].shape[1]

    def out(part, got, more):
        f32 = jnp.float32
        total = part[0].astype(f32) + jnp.concatenate([v[0].astype(f32) for v in got], axis=0)
        total = total + jnp.concatenate([v[0].astype(f32) for v in more], axis=0)
        gate[0] = total[:ff].T
        up[0] = total[ff : 2 * ff].T
        down[0] = total[2 * ff :]

    @pl.when(j == 0)
    def _():
        out(low, got_x, more_y)

    @pl.when(j == 1)
    def _():
        out(high, got_y, more_x)


def finish(low, high, got_x, got_y, more):
    n_e, rows, half = low.shape
    ff = rows // 3
    k = len(got_x)

    def place(v):
        return pl.BlockSpec((1,) + v.shape[1:], lambda e, j: (e, 0, 0))

    ins = [low, high, *got_x, *got_y, *[m[0] for m in more], *[m[1] for m in more]]
    f32 = jnp.float32
    turned_out = jax.ShapeDtypeStruct((n_e, 2 * half, ff), f32)
    return pl.pallas_call(
        functools.partial(finish_body, k),
        out_shape=(turned_out, turned_out, jax.ShapeDtypeStruct((n_e, ff, 2 * half), f32)),
        grid=(n_e, 2),
        in_specs=[place(v) for v in ins],
        out_specs=(
            pl.BlockSpec((1, half, ff), lambda e, j: (e, j, 0)),
            pl.BlockSpec((1, half, ff), lambda e, j: (e, j, 0)),
            pl.BlockSpec((1, ff, half), lambda e, j: (e, 0, j)),
        ),
        compiler_params=kernel_params(),
    )(*ins)


fence = lax.optimization_barrier


def plus(a, b):
    return a.astype(jnp.float32) + b.astype(jnp.float32)


def on_device(
    hidden_in,
    cotangent,
    attention_gain,
    query_gain,
    key_gain,
    mixture_gain,
    query_weight,
    key_weight,
    value_weight,
    output_weight,
    router_weight,
    gate_weight,
    up_weight,
    down_weight,
    routes,
    segments,
):
    bf16, f32 = jnp.bfloat16, jnp.float32
    n_dp, owners = lax.axis_size("dp"), lax.axis_size("expert")
    nz = owners // 2
    n_dev = n_dp * owners
    tokens, width = hidden_in.shape
    half = width // 2
    unit = width // (n_dev // 2)
    cut = unit // 2
    top = routes.shape[1]
    exp_dev = gate_weight.shape[0]
    experts = exp_dev * owners
    cap = max(2, tokens * top * 5 // (experts * 4))
    ff = gate_weight.shape[2]
    rows_dev = attention_gain.shape[0]
    score_scale = HD ** (-0.5)
    dp, ex = lax.axis_index("dp"), lax.axis_index("expert")
    core, zc = ex % 2, ex // 2

    def swap(v, axis, bit):
        size = n_dp if axis == "dp" else owners
        return lax.ppermute(v, axis, [(i, i ^ bit) for i in range(size)])

    def swap_core(v):
        return swap(v, "expert", 1)

    def swap_x(v):
        return swap(v, "dp", 1)

    def swap_y(v):
        return swap(v, "dp", 2)

    def ring(v):
        return lax.ppermute(v, "expert", [(i, (i + 2) % owners) for i in range(owners)])

    def in_order(bit, mine, other, axis):
        return jnp.where(
            bit == 0,
            jnp.concatenate([mine, other], axis=axis),
            jnp.concatenate([other, mine], axis=axis),
        )

    def half_of(v, which, axis):
        return lax.dynamic_slice_in_dim(v, which * (v.shape[axis] // 2), v.shape[axis] // 2, axis)

    def halves(v, axis):
        return half_of(v, core, axis), half_of(v, 1 - core, axis)

    def by_rows(v):
        return with_layout_constraint(v, Layout((0, 1)))

    def thirds(v):
        return [v[:, t * ff : (t + 1) * ff] for t in range(3)]

    def chip_row(plane, r):
        return ((dp ^ plane) * nz + (zc - r) % nz) * unit

    bits = []
    b = 1
    while b < owners:
        bits.append(("expert", b, (ex // b) % 2))
        b *= 2
    b = 1
    while b < n_dp:
        bits.append(("dp", b, (dp // b) % 2))
        b *= 2

    sources = (query_weight, key_weight, value_weight, output_weight)
    gains = (attention_gain, query_gain, key_gain, mixture_gain)
    small = jnp.concatenate([v[:, None] for v in gains] + [router_weight], axis=1)
    small = jnp.pad(small, ((0, 0), (0, -small.shape[1] % 128)))
    theirs = jnp.concatenate([half_of(w, 1 - core, 1) for w in sources] + [small], axis=1)
    mine = jnp.concatenate([half_of(w, core, 1) for w in sources] + [small], axis=1)
    piece = by_rows(in_order(core, mine, swap_core(theirs), 0))
    piece, gate_weight, up_weight, down_weight, cotangent, segments, hidden_in = fence(
        (piece, gate_weight, up_weight, down_weight, cotangent, segments, hidden_in)
    )

    main = 4 * half
    weights, small_all = blank(width, main), blank(width, small.shape[1])
    route_rows = routes.T.astype(bf16).reshape(-1, width)
    pad = -route_rows.shape[0] % 16
    cot_piece = jnp.concatenate([cotangent, route_rows, jnp.zeros((pad, width), bf16)], axis=0)
    cot_steps = [cot_piece]

    def put(buffers, v, row):
        kept, kept_small = buffers
        kept = lax.dynamic_update_slice(kept, v[:, :main], (row, 0))
        kept_small = by_rows(lax.dynamic_update_slice(kept_small, v[:, main:], (row, 0)))
        return kept, kept_small

    buffers = (weights, small_all)
    before, arrived = None, []
    for r in range(nz):
        by_x, by_y = by_rows(swap_x(piece)), by_rows(swap_y(piece))
        following, sent = (), ()
        if before is not None:
            sent = cut_pair(*before)
            sent = (by_rows(swap_y(sent[0])), by_rows(swap_x(sent[1])))
        if r + 1 < nz:
            following = by_rows(ring(piece))
        else:
            cot_steps.append(ring(cot_steps[-1]))
        for v, row in arrived + [(piece, chip_row(0, r))]:
            buffers = put(buffers, v, row)
        by_x, by_y, following, sent, buffers, cot_steps = fence(
            (by_x, by_y, following, sent, buffers, cot_steps)
        )
        arrived = [(by_x, chip_row(1, r)), (by_y, chip_row(2, r))]
        if before is not None:
            arrived += [(sent[0], chip_row(3, r - 1)), (sent[1], chip_row(3, r - 1) + cut)]
        before, piece = (by_x, by_y), following
    sent = cut_pair(*before)
    sent = (by_rows(swap_y(sent[0])), by_rows(swap_x(sent[1])))
    own_first, own_rest = [], []
    for j in range(2):
        part = slice(j * half, (j + 1) * half)
        own_first.append(gate_weight[:, part].swapaxes(1, 2))
        own_rest.append(
            jnp.concatenate([up_weight[:, part].swapaxes(1, 2), down_weight[:, :, part]], axis=1)
        )
    cosine, sine = rotary_tables(segments, HD)
    cosine = jnp.concatenate([cosine[0], cosine[0]], axis=1)
    sine = jnp.concatenate([-sine[0], sine[0]], axis=1)
    document = segments[0]
    for v, row in arrived:
        buffers = put(buffers, v, row)
    buffers, own_first, own_rest, cosine, sine, document, sent, cot_steps = fence(
        (buffers, own_first, own_rest, cosine, sine, document, sent, cot_steps)
    )
    buffers = put(buffers, sent[0], chip_row(3, nz - 1))
    buffers = put(buffers, sent[1], chip_row(3, nz - 1) + cut)
    weights, small_all = fence(buffers)

    weights_other = swap_core(weights)
    x_low, y_high = [swap_x(own_first[0])], [swap_y(own_first[1])]
    if len(cot_steps) < nz:
        cot_steps.append(ring(cot_steps[-1]))
    gains_all = small_all[:, :4].astype(f32).T
    router_t = small_all[:, 4 : 4 + experts].T
    attention_gain_full, mixture_gain_full = gains_all[0], gains_all[3]
    query_gain_rel = jnp.concatenate(halves(gains_all[1], 0))
    key_gain_rel = jnp.concatenate(halves(gains_all[2], 0))
    core_ref = core[None]
    normed, raw, query_squares, key_squares = project(hidden_in, attention_gain_full, weights)
    (
        weights,
        weights_other,
        mixture_gain_full,
        router_t,
        normed,
        raw,
        x_low,
        y_high,
        cot_steps,
        own_first,
        own_rest,
    ) = fence(
        (
            weights,
            weights_other,
            mixture_gain_full,
            router_t,
            normed,
            raw,
            x_low,
            y_high,
            cot_steps,
            own_first,
            own_rest,
        )
    )

    x_low.append(swap_x(own_rest[0]))
    y_high.append(swap_y(own_rest[1]))
    while len(cot_steps) < nz:
        cot_steps.append(ring(cot_steps[-1]))
    raw, query_squares, key_squares = project_other(
        normed, weights_other, query_squares, key_squares, raw
    )
    query_heads, key_heads, value_heads, context = attend(
        raw, query_squares, key_squares, query_gain_rel, key_gain_rel, cosine, sine, document
    )
    middle, mixed_piece, router_probs = middle_of(
        core_ref, context, weights, weights_other, hidden_in, mixture_gain_full, router_t
    )
    mixed_piece, x_low, y_high, cot_steps, context, middle, normed = fence(
        (mixed_piece, x_low, y_high, cot_steps, context, middle, normed)
    )
    n_prob = 2 * experts * tokens // width

    mixed_all, cot_all, mixed_last = [], [], mixed_piece
    x_high, y_low = [], []
    for r in range(nz):
        following = ring(mixed_last) if r + 1 < nz else ()
        got = ()
        if r < 3:
            sent = [(v[:, :ff], w[:, :ff], w[:, ff:])[r] for v, w in zip(own_first, own_rest)]
            got = (swap_x(sent[1]), swap_y(sent[0]))
        mixed_all += [mixed_last, swap_core(mixed_last)]
        cot_all += [cot_steps[r], swap_core(cot_steps[r])]
        following, mixed_all, cot_all, got = fence((following, mixed_all, cot_all, got))
        if r < 3:
            x_high.append(got[0])
            y_low.append(got[1])
        mixed_last = following
    number = (ex * exp_dev)[None]
    rank_row, rank_col, gate_row = plan(
        number, mixed_all, cot_all, n_prob // 2, top, exp_dev, tokens
    )

    send_pieces = ((0, 5 * ff // 4), (5 * ff // 4, 17 * ff // 16), (37 * ff // 16, 11 * ff // 16))
    last_pieces = ((0, 3 * ff // 4), (3 * ff // 4, 5 * ff // 4), (2 * ff, ff))
    corner_low, corner_high = [swap_y(v) for v in x_low], [swap_x(v) for v in y_high]
    shards = (tuple(zip(own_first, own_rest)), (x_low, x_high), (y_low, y_high))
    rows, acts, gates, products, send_x, keep_x, keep_y, send_y = experts_first(
        mixed_all, cot_all, shards, ff, rank_row, gate_row, cap, send_pieces
    )
    corner_low, corner_high, rows, acts, gates, products, send_x, send_y = fence(
        (corner_low, corner_high, rows, acts, gates, products, send_x, send_y)
    )

    got_x, got_y = [swap_x(send_x[0])], [swap_y(send_y[0])]
    parts = ()
    if nz > 4:
        parts = fence(expert_grads(acts, rows, ff))
    shards = shards + ((corner_low, corner_high),)
    acts_last, products, last_low, last_high = experts_last(
        rows, gates, products, shards[3], ff, last_pieces
    )
    acts_last, products, last_low, last_high, got_x, got_y, send_x, send_y = fence(
        (acts_last, products, last_low, last_high, got_x, got_y, send_x, send_y)
    )

    def spread(kinds, zs, gates):
        return experts_spread(
            number,
            acts,
            acts_last,
            products,
            shards,
            ff,
            width,
            rank_row,
            rank_col,
            cap,
            kinds,
            zs,
            gates,
        )

    near = tuple(range(1, nz // 2 + 1))
    far = tuple(range(nz // 2 + 1, nz)) + (0,)
    got_x.append(swap_x(send_x[1]))
    got_y.append(swap_y(send_y[1]))
    copied_near, other_near = spread((0, 1), near, True)
    copied_near, other_near, got_x, got_y, send_x, send_y = fence(
        (copied_near, other_near, got_x, got_y, send_x, send_y)
    )
    got_near = swap_core(other_near)
    got_near = fence(got_near)

    class Total:
        def __init__(self, blocks):
            self.blocks, self.value, self.at = blocks, blocks[1], 2

        def move(self):
            self.value = ring(self.value.astype(bf16))

        def add(self):
            self.value = plus(self.value, self.blocks[self.at % nz])
            self.at += 1

        def rest(self):
            while self.at <= nz:
                self.move()
                self.add()
            return self.value

    copies_sum = Total({r: plus(copied_near[i], got_near[i]) for i, r in enumerate(near)})
    copies_sum.move()
    got_x.append(swap_x(send_x[2]))
    got_y.append(swap_y(send_y[2]))
    got_last_x, got_last_y = [swap_x(last_low[0])], [swap_y(last_high[0])]
    copied_far, other_far = spread((0, 1), far, True)
    copies_sum.value, copied_far, other_far, got_x, got_y, got_last_x, got_last_y = fence(
        (copies_sum.value, copied_far, other_far, got_x, got_y, got_last_x, got_last_y)
    )
    got_far = swap_core(other_far)
    copies_sum.add()
    copies_sum.move()
    got_last_x.append(swap_x(last_low[1]))
    got_last_y.append(swap_y(last_high[1]))
    mixture, mixture_other = spread((2,), tuple(range(nz)), False)
    copies_sum.value, got_far, mixture, mixture_other, got_last_x, got_last_y = fence(
        (copies_sum.value, got_far, mixture, mixture_other, got_last_x, got_last_y)
    )
    copies_sum.blocks.update({r: plus(copied_far[i], got_far[i]) for i, r in enumerate(far)})
    copies_sum.add()
    copies_sum.move()
    got_last_x.append(swap_x(last_low[2]))
    got_last_y.append(swap_y(last_high[2]))
    got_mix = swap_core(mixture_other)
    context = in_order(core, context[:, :half], context[:, half:], 1)
    first_x = jnp.concatenate(got_last_x[:2], axis=1)
    first_y = jnp.concatenate(got_last_y[:2], axis=1)
    more_y = [plus(a, b).astype(bf16) for a, b in zip(thirds(keep_y)[:2], thirds(first_x)[:2])]
    more_x = [plus(a, b).astype(bf16) for a, b in zip(thirds(keep_x)[:2], thirds(first_y)[:2])]
    copies_sum.value, got_last_x, got_last_y, context, got_mix, more_x, more_y = fence(
        (copies_sum.value, got_last_x, got_last_y, context, got_mix, more_x, more_y)
    )
    for sums, kept, got in ((more_y, keep_y, got_last_x), (more_x, keep_x, got_last_y)):
        sums.append(plus(thirds(kept)[2], got[2]).astype(bf16))
    copies_sum.add()
    copies_sum = copies_sum.rest()

    def send_more(t):
        return swap_y(more_y[t]), swap_x(more_x[t])

    more = [send_more(0)]
    mixed = Total({r: plus(mixture[r], got_mix[r]) for r in range(nz)})
    mixed.move()
    normed_other, context_other = swap_core(normed), swap_core(context)
    (middle_grad, branch, branch_other, context_up, mixture_gain_grad, router_grad, _) = middle_back(
        core_ref,
        copies_sum,
        middle,
        cotangent,
        mixture_gain_full,
        router_probs,
        router_t,
        weights,
        weights_other,
    )
    (context_up, branch, branch_other, mixed.value, normed_other, context_other, more, more_x, more_y) = fence(
        (context_up, branch, branch_other, mixed.value, normed_other, context_other, more, more_x, more_y)
    )
    mixed.add()
    mixed.move()
    more.append(send_more(1))
    got_branch = swap_core(branch_other)
    *ups, query_gain_grad, key_gain_grad = attend_back(
        query_heads,
        key_heads,
        value_heads,
        context_up,
        raw,
        query_squares,
        key_squares,
        query_gain_rel,
        key_gain_rel,
        cosine,
        sine,
        document,
    )
    ups, mixed.value, got_branch, more = fence((ups, mixed.value, got_branch, more))
    got_ups = swap_core(ups[1])
    more.append(send_more(2))
    first, second = qkv_grad(normed, normed_other, ups[0], got_ups)
    mixed.add()
    mixed.move()
    def several(v, picks):
        return jnp.concatenate(
            [lax.dynamic_slice_in_dim(v, chip_row(plane, r), unit, 0) for plane, r in picks],
            axis=0,
        )

    def pack(v, n):
        k = n * unit // v.shape[0]
        step = v.shape[1] // k
        return jnp.concatenate([v[:, i * step : (i + 1) * step] for i in range(k)], axis=0)

    def unpack(v, rows):
        return jnp.concatenate([v[i : i + rows] for i in range(0, v.shape[0], rows)], axis=1)

    side = 3 * half // 2

    def step_one(rs):
        sent = several(first, [(1, r) for r in rs] + [(3, r) for r in rs])
        back = several(second, [(2, r) for r in rs] + [(3, r) for r in rs])
        return sent, back

    def step_two(rs, by_x, by_y):
        n = len(rs) * unit
        more_y = plus(several(first, [(2, r) for r in rs]), by_x[n:]).astype(bf16)
        more_x = plus(several(second, [(1, r) for r in rs]), by_y[n:]).astype(bf16)
        return more_y, more_x

    def step_three(rs, by_x, by_y, more_y, more_x):
        n = len(rs) * unit
        left = plus(several(first, [(0, r) for r in rs]), by_x[:n]) + more_y.astype(f32)
        right = plus(several(second, [(0, r) for r in rs]), by_y[:n]) + more_x.astype(f32)
        whole = jnp.concatenate([left, right], axis=1)
        return {r: whole[i * unit : (i + 1) * unit] for i, r in enumerate(rs)}

    near_sent = step_one(near)
    near_sent, more, ups, first, second, branch, got_branch = fence(
        (near_sent, more, ups, first, second, branch, got_branch)
    )
    output_grad = jnp.einsum(
        "tc,td->cd",
        jnp.concatenate([context, context_other], axis=0),
        jnp.concatenate([branch, got_branch], axis=0),
        preferred_element_type=f32,
    ).astype(bf16)
    near_got = (swap_x(near_sent[0]), swap_y(near_sent[1]))
    output_sum = Total(
        [several(output_grad, [(plane, r) for plane in range(n_dp)]) for r in range(nz)]
    )
    output_sum.move()
    far_sent = step_one(far)
    hidden_grad, attention_gain_grad = input_grad(
        ups, weights, weights_other, hidden_in, middle_grad, attention_gain_full
    )

    def canonical(v):
        return in_order(core, v[:half], v[half:], 0)

    gain_grads = (
        attention_gain_grad[0],
        canonical(query_gain_grad[0]),
        canonical(key_gain_grad[0]),
        mixture_gain_grad[0],
    )
    small_sum = jnp.concatenate(
        [v.reshape(n_dev, rows_dev) for v in gain_grads]
        + [
            router_grad.reshape(experts, n_dev, rows_dev)
            .swapaxes(0, 1)
            .reshape(n_dev, experts * rows_dev)
        ],
        axis=1,
    )
    folded = []

    def fold(v):
        axis, bit, mark = bits[len(folded)]
        folded.append(bit)
        v = v.reshape(v.shape[0] // 2, 2, v.shape[1])
        keep = lax.dynamic_index_in_dim(v, mark, 1, False)
        return keep + swap(lax.dynamic_index_in_dim(v, 1 - mark, 1, False), axis, bit)

    near_got, output_sum.value, small_sum, hidden_grad, far_sent, mixed.value = fence(
        (near_got, output_sum.value, small_sum, hidden_grad, far_sent, mixed.value)
    )
    mixed.add()
    mixed = mixed.rest()
    layer_out = (middle + mixed).astype(bf16)
    near_more = step_two(near, *near_got)
    near_more = fence(near_more)
    near_more = (swap_y(near_more[0]), swap_x(near_more[1]))
    far_got = (swap_x(far_sent[0]), swap_y(far_sent[1]))
    output_sum.add()
    output_sum.move()
    near_more, output_sum.value = fence((near_more, output_sum.value))
    output_sum.add()
    output_sum.move()
    weight_sum = Total(step_three(near, *near_got, *near_more))
    weight_sum.value = weight_sum.value.astype(bf16)
    small_sum = fold(small_sum)
    weight_sum.value, small_sum = fence((weight_sum.value, small_sum))
    for _ in near[:-1]:
        weight_sum.move()
        if weight_sum.at < near[-1]:
            weight_sum.add()
    if not parts:
        acts, rows, _ = fence((acts, rows, near_more))
        parts = expert_grads(acts, rows, ff)
    far_got, output_sum.value, parts, small_sum, got_x, got_y, more = fence(
        (far_got, output_sum.value, parts, small_sum, got_x, got_y, more)
    )
    output_sum.add()
    output_sum = output_sum.rest()
    out_low = output_sum[:, : half // 2].astype(bf16)
    out_high = output_sum[:, half // 2 :].astype(bf16)
    far_more = step_two(far, *far_got)
    to_y = jnp.concatenate([far_more[0], pack(out_high[2 * unit :], len(far))], axis=1)
    to_x = jnp.concatenate(
        [
            far_more[1],
            pack(jnp.concatenate([out_low[unit : 2 * unit], out_low[3 * unit :]], axis=0), len(far)),
        ],
        axis=1,
    )
    by_y, by_x = swap_y(to_y), swap_x(to_x)
    if len(near) > 1:
        weight_sum.add()
    weight_sum.move()
    small_sum = fold(small_sum)
    by_y, by_x, weight_sum.value, small_sum, parts = fence(
        (by_y, by_x, weight_sum.value, small_sum, parts)
    )
    expert_grad = finish(*parts, got_x, got_y, more)
    far_more = (by_y[:, :side], by_x[:, :side])
    got_out_x = unpack(by_x[:, side:], 2 * unit)
    got_out_y = unpack(by_y[:, side:], 2 * unit)
    out_more_y = plus(out_low[2 * unit : 3 * unit], got_out_x[unit:]).astype(bf16)
    out_more_x = plus(out_high[unit : 2 * unit], got_out_y[unit:]).astype(bf16)
    out_more_y, out_more_x = swap_y(out_more_y), swap_x(out_more_x)
    small_sum = fold(small_sum)
    weight_sum.blocks.update(step_three(far, *far_got, *far_more))
    weight_sum.add()
    weight_sum.move()
    weight_sum.value, out_more_y, out_more_x, small_sum, expert_grad = fence(
        (weight_sum.value, out_more_y, out_more_x, small_sum, expert_grad)
    )
    weight_sum.add()
    while weight_sum.at <= nz:
        weight_sum.move()
        if len(folded) < len(bits):
            small_sum = fold(small_sum)
        weight_sum.value, small_sum = fence((weight_sum.value, small_sum))
        weight_sum.add()
    total = weight_sum.value
    while len(folded) < len(bits):
        small_sum = fold(small_sum)
    small_sum = small_sum[0]
    gain_parts = small_sum[: 4 * rows_dev].reshape(4, rows_dev)
    router_part = small_sum[4 * rows_dev :].reshape(experts, rows_dev).T
    out_total = jnp.concatenate(
        [
            plus(out_low[:unit], got_out_x[:unit]) + out_more_y.astype(f32),
            plus(out_high[:unit], got_out_y[:unit]) + out_more_x.astype(f32),
        ],
        axis=1,
    )
    total = jnp.concatenate([total, out_total], axis=1)
    kept_rows = half_of(total, core, 0)
    got_rows = swap_core(half_of(total, 1 - core, 0))
    weight_grads = [
        in_order(
            core, kept_rows[:, i * half : (i + 1) * half], got_rows[:, i * half : (i + 1) * half], 1
        )
        for i in range(4)
    ]
    return (
        layer_out,
        hidden_grad,
        gain_parts[0],
        gain_parts[1],
        gain_parts[2],
        gain_parts[3],
        weight_grads[0],
        weight_grads[1],
        weight_grads[2],
        weight_grads[3],
        router_part,
        *expert_grad,
    )


def solution(mesh):
    return jax.shard_map(
        on_device,
        mesh=mesh,
        in_specs=(
            P(("dp", "expert"), None),
            P(("dp", "expert"), None),
            P(("dp", "expert")),
            P(("dp", "expert")),
            P(("dp", "expert")),
            P(("dp", "expert")),
            P(("dp", "expert"), None),
            P(("dp", "expert"), None),
            P(("dp", "expert"), None),
            P(("dp", "expert"), None),
            P(("dp", "expert"), None),
            P("expert", None, "dp"),
            P("expert", None, "dp"),
            P("expert", "dp", None),
            P(("dp", "expert"), None),
            P(("dp", "expert"), None),
        ),
        out_specs=(
            P(("dp", "expert"), None),
            P(("dp", "expert"), None),
            P(("dp", "expert")),
            P(("dp", "expert")),
            P(("dp", "expert")),
            P(("dp", "expert")),
            P(("dp", "expert"), None),
            P(("dp", "expert"), None),
            P(("dp", "expert"), None),
            P(("dp", "expert"), None),
            P(("dp", "expert"), None),
            P("expert", None, "dp"),
            P("expert", None, "dp"),
            P("expert", "dp", None),
        ),
        check_vma=False,
    )
```
